32 devices in a mesh: dp: 4 (over y, core), chan: 8 (over z, x).
Axes of the slice: x: 2, y: 2, z: 4, core: 2. Of those that a mesh axis runs over, the one named last changes fastest.
Arguments:
- inputs: bfloat16 [2, 6272, 2048], P(None, 'dp', 'chan'), may hold values from -6 to 6
- cotangent: bfloat16 [2, 6272, 2048], P(None, 'dp', 'chan'), may hold values from -6 to 6
- w_first: float32 [2048, 512], P('chan', 'dp'), may hold values from -0.125 to 0.125
- first_m: float32 [2048, 512], P('chan', 'dp'), may hold values from -256 to 256
- first_v: float32 [2048, 512], P('chan', 'dp'), may hold values from 940.8 to 7526.4
- w_middle: float32 [3, 3, 512, 512], P(None, None, 'chan', 'dp'), may hold values from -0.09375 to 0.09375
- middle_m: float32 [3, 3, 512, 512], P(None, None, 'chan', 'dp'), may hold values from -256 to 256
- middle_v: float32 [3, 3, 512, 512], P(None, None, 'chan', 'dp'), may hold values from 940.8 to 7526.4
- w_last: float32 [512, 2048], P('chan', 'dp'), may hold values from -0.25 to 0.25
- last_m: float32 [512, 2048], P('chan', 'dp'), may hold values from -256 to 256
- last_v: float32 [512, 2048], P('chan', 'dp'), may hold values from 940.8 to 7526.4
- mid_params: float32 [4, 512], P(None, 'chan'), may hold values from 0.5 to 1.5
- mid_m: float32 [4, 512], P(None, 'chan'), may hold values from -256 to 256
- mid_v: float32 [4, 512], P(None, 'chan'), may hold values from 940.8 to 7526.4
- out_params: float32 [2, 2048], P(None, 'chan'), may hold values from 0.5 to 1.5
- out_m: float32 [2, 2048], P(None, 'chan'), may hold values from -256 to 256
- out_v: float32 [2, 2048], P(None, 'chan'), may hold values from 940.8 to 7526.4
- image_counts: int32 [2, 4], replicated, may hold values from 1 to 32, 96 in all within a row
Outputs:
- block_out: float32 [2, 6272, 2048], P(None, 'dp', 'chan')
- input_grad: float32 [2, 6272, 2048], P(None, 'dp', 'chan')
- first_new: float32 [2048, 512], P('chan', 'dp')
- first_m_new: float32 [2048, 512], P('chan', 'dp')
- first_v_new: float32 [2048, 512], P('chan', 'dp')
- middle_new: float32 [3, 3, 512, 512], P(None, None, 'chan', 'dp')
- middle_m_new: float32 [3, 3, 512, 512], P(None, None, 'chan', 'dp')
- middle_v_new: float32 [3, 3, 512, 512], P(None, None, 'chan', 'dp')
- last_new: float32 [512, 2048], P('chan', 'dp')
- last_m_new: float32 [512, 2048], P('chan', 'dp')
- last_v_new: float32 [512, 2048], P('chan', 'dp')
- mid_new: float32 [4, 512], P(None, 'chan')
- mid_m_new: float32 [4, 512], P(None, 'chan')
- mid_v_new: float32 [4, 512], P(None, 'chan')
- out_new: float32 [2, 2048], P(None, 'chan')
- out_m_new: float32 [2, 2048], P(None, 'chan')
- out_v_new: float32 [2, 2048], P(None, 'chan')
The draws below stay inside these ranges and needn't reach their ends.
Inputs may be any that keep to these rules, and one draw needn't show every extreme that they name: image_counts[m, g] live images stand first among the 32 slots of index g of dp; each micro-batch has exactly (384) // 4 live images, and some index holds 32.
All inputs are finite; a program needn't handle non-finite values.
Results may differ from the reference program's by a relative error of at most 0.03.
Values may be sent and summed in bfloat16 or wider, within the bound.
No kernel may reach another device: no remote copies, remote signals or barrier semaphores. Data moves between devices by JAX's collectives and lax.ppermute only.
A program may use at most 128 MiB of HBM per device.

```python
import math
import jax
import jax.numpy as jnp
import numpy as np
from jax import lax

C_IN = 2048
C_MID = 512
IMG_DEV = 32
MB = 2
STEPS = 5
GROUPS = 4
IMAGES = 128
ROWS = 6272
VALID = 9408


def levels(rng, extent, cuts, smallest, high):
    loudness = 1.0
    for axis_at, blocks in cuts:
        draws = jax.random.uniform(jax.random.fold_in(jax.random.fold_in(rng, 6), axis_at), (blocks,), jnp.float32, smallest / len(cuts), high / len(cuts))
        loudness = loudness * jnp.repeat(jnp.exp(draws), extent[axis_at] // blocks).reshape((-1,) + (1,) * (len(extent) - 1 - axis_at))
    return loudness


def profile(amount, total, limit, lean):
    loads = [(1 << 20) // math.isqrt(standing ** lean) + 1 for standing in range(2, amount + 1)]
    surplus, given = total - limit - (amount - 1), [1] * (amount - 1)
    while surplus > 0:
        candidates = [i for i in range(amount - 1) if given[i] < limit]
        mass, remaining = sum([loads[i] for i in candidates]), surplus
        for i in candidates:
            more = min(limit - given[i], max(1, remaining * loads[i] // mass), surplus)
            given[i] = given[i] + more
            surplus = surplus - more
    return np.array([limit] + given)


def ragged(stream_key, amount, total, most, slope):
    if amount == 2:
        one = jax.random.randint(stream_key, (), max(1, total - most), min(most, total - 1) + 1)
        return jnp.stack([one, total - one])
    lengths = jnp.asarray(profile(amount, total, most, slope), jnp.int32)
    twos = (amount - 1) // 2
    source_of, taker = lengths[1:1 + 2 * twos:2], lengths[2:2 + 2 * twos:2]
    margin = jnp.minimum(source_of - 1, most - taker)
    shifted = jax.random.randint(jax.random.fold_in(stream_key, 1), (twos,), 0, 1 << 20) % (margin + 1)
    lengths = lengths.at[1:1 + 2 * twos:2].set(source_of - shifted).at[2:2 + 2 * twos:2].set(taker + shifted)
    return lengths[jax.random.permutation(jax.random.fold_in(stream_key, 2), amount)]


def centred(rng, dims, scale, most, split=(), dtype=jnp.bfloat16):
    entries = jax.random.normal(rng, dims, jnp.float32) * scale
    if len(split) > 0:
        entries = levels(rng, dims, split, -0.22, 0.18) * entries
    return jnp.clip(entries, min=-most, max=most).astype(dtype)


def setup_inputs(seed: int = 0) -> dict:
    streams_of = jax.random.split(jax.random.key(seed), 19)
    return {
        "inputs": centred(streams_of[0], (MB, ROWS, C_IN), 1.0, 6.0, ((1, 4), (2, 8))),
        "cotangent": centred(streams_of[1], (MB, ROWS, C_IN), 1.0, 6.0, ((1, 4), (2, 8))),
        "w_first": centred(streams_of[2], (C_IN, C_MID), C_IN ** -0.5, 0.125, ((0, 8), (1, 4)), jnp.float32),
        "first_m": centred(streams_of[3], (C_IN, C_MID), (0.45 * VALID ** 0.5), 256.0, ((0, 8), (1, 4)), jnp.float32),
        "first_v": jnp.clip(jnp.exp(math.log(7526.4) - 2.0794415 * jax.random.uniform(streams_of[4], (C_IN, C_MID), jnp.float32) ** levels(streams_of[4], (C_IN, C_MID), ((0, 8), (1, 4)), -0.2, 0.2)), 940.8, 7526.4),
        "w_middle": centred(streams_of[5], (3, 3, C_MID, C_MID), (9 * C_MID) ** -0.5, 0.09375, ((2, 8), (3, 4)), jnp.float32),
        "middle_m": centred(streams_of[6], (3, 3, C_MID, C_MID), (0.45 * VALID ** 0.5), 256.0, ((2, 8), (3, 4)), jnp.float32),
        "middle_v": jnp.clip(jnp.exp(math.log(7526.4) - 2.0794415 * jax.random.uniform(streams_of[7], (3, 3, C_MID, C_MID), jnp.float32) ** levels(streams_of[7], (3, 3, C_MID, C_MID), ((2, 8), (3, 4)), -0.2, 0.2)), 940.8, 7526.4),
        "w_last": centred(streams_of[8], (C_MID, C_IN), C_MID ** -0.5, 0.25, ((0, 8), (1, 4)), jnp.float32),
        "last_m": centred(streams_of[9], (C_MID, C_IN), (0.45 * VALID ** 0.5), 256.0, ((0, 8), (1, 4)), jnp.float32),
        "last_v": jnp.clip(jnp.exp(math.log(7526.4) - 2.0794415 * jax.random.uniform(streams_of[10], (C_MID, C_IN), jnp.float32) ** levels(streams_of[10], (C_MID, C_IN), ((0, 8), (1, 4)), -0.2, 0.2)), 940.8, 7526.4),
        "mid_params": jnp.clip(0.5 + 1.0 * jax.random.uniform(streams_of[11], (4, C_MID), jnp.float32) ** levels(streams_of[11], (4, C_MID), ((1, 8),), -0.2, 0.2), 0.5, 1.5),
        "mid_m": centred(streams_of[12], (4, C_MID), (0.45 * VALID ** 0.5), 256.0, ((1, 8),), jnp.float32),
        "mid_v": jnp.clip(jnp.exp(math.log(7526.4) - 2.0794415 * jax.random.uniform(streams_of[13], (4, C_MID), jnp.float32) ** levels(streams_of[13], (4, C_MID), ((1, 8),), -0.2, 0.2)), 940.8, 7526.4),
        "out_params": jnp.clip(0.5 + 1.0 * jax.random.uniform(streams_of[14], (2, C_IN), jnp.float32) ** levels(streams_of[14], (2, C_IN), ((1, 8),), -0.2, 0.2), 0.5, 1.5),
        "out_m": centred(streams_of[15], (2, C_IN), (0.45 * VALID ** 0.5), 256.0, ((1, 8),), jnp.float32),
        "out_v": jnp.clip(jnp.exp(math.log(7526.4) - 2.0794415 * jax.random.uniform(streams_of[16], (2, C_IN), jnp.float32) ** levels(streams_of[16], (2, C_IN), ((1, 8),), -0.2, 0.2)), 940.8, 7526.4),
        "image_counts": jax.vmap(lambda own: ragged(own, GROUPS, (3 * IMAGES) // 4, IMG_DEV, 2))(jax.random.split(streams_of[17], MB)).reshape((MB, GROUPS)).astype(jnp.int32),
    }


@jax.custom_vjp
def low(v):
    return lax.optimization_barrier(v.astype(jnp.bfloat16)).astype(jnp.float32)

@jax.custom_vjp
def low_back(v):
    return v

def low_keep(v):
    return (low(v), None)

def low_pass(kept, grad):
    return (grad,)

def back_keep(v):
    return (v, None)

def back_low(kept, grad):
    return (low(grad),)
low.defvjp(low_keep, low_pass)
low_back.defvjp(back_keep, back_low)
norm_eps = 1e-05
adam_eps = 1e-08
adam_beta = 0.5
decay_rate = 0.05
rate_first = 0.02
rate_middle = 0.015
rate_last = 0.04
rate_norm = 0.25

def silu(value):
    return value * jax.nn.sigmoid(value)

def matmul(left, right):
    return jnp.dot(left, right, precision=lax.Precision.HIGHEST, preferred_element_type=jnp.float32)

def conv_three(acts, weights):
    grid = acts.reshape(-1, 7, 7, acts.shape[1])
    padded = jnp.pad(grid, ((0, 0), (1, 1), (1, 1), (0, 0)))
    total = jnp.zeros((grid.shape[0], 7, 7, weights.shape[3]), jnp.float32)
    for row_off in range(3):
        for col_off in range(3):
            window = padded[:, row_off:row_off + 7, col_off:col_off + 7, :]
            total = total + jnp.einsum('nijc,cd->nijd', window, weights[row_off, col_off], precision=lax.Precision.HIGHEST)
    return total.reshape(-1, weights.shape[3])

def normalize(pre, gain_row, shift_row, live_rows, live_count):
    average = lax.optimization_barrier(jnp.sum(live_rows * pre, axis=0)) / live_count
    variance = lax.optimization_barrier(jnp.sum(live_rows * pre * pre, axis=0)) / live_count - average * average
    normed = (pre - average) * lax.rsqrt(variance + norm_eps)
    return gain_row * normed + shift_row

def block(block_in, low_first, low_middle, low_last, mid_params, out_params, live_rows, live_count):
    pre_first = low_back(matmul(block_in, low_first))
    act_first = low(silu(normalize(pre_first, mid_params[0], mid_params[1], live_rows, live_count)))
    pre_middle = low_back(conv_three(act_first, low_middle))
    act_middle = low(silu(normalize(pre_middle, mid_params[2], mid_params[3], live_rows, live_count)))
    pre_last = low_back(matmul(act_middle, low_last))
    summed = normalize(pre_last, out_params[0], out_params[1], live_rows, live_count) + block_in
    return live_rows * silu(summed)

def adamw(weight, gradient, moment_one, moment_two, step_rate):
    one_new = adam_beta * moment_one + (1.0 - adam_beta) * gradient
    two_new = adam_beta * moment_two + (1.0 - adam_beta) * gradient * gradient
    correct = 1.0 - adam_beta ** STEPS
    weight_new = weight - step_rate * (one_new / correct / (jnp.sqrt(two_new / correct) + adam_eps) + decay_rate * weight)
    return (weight_new, one_new, two_new)

def reference(inputs, cotangent, w_first, first_m, first_v, w_middle, middle_m, middle_v, w_last, last_m, last_v, mid_params, mid_m, mid_v, out_params, out_m, out_v, image_counts):
    places = jnp.arange(ROWS) // 49
    owners = places // IMG_DEV
    slots = places % IMG_DEV
    lives = []
    counts = []
    for batch_index in range(MB):
        row_counts = image_counts[batch_index]
        lives.append((slots < jnp.take(row_counts, owners)).astype(jnp.float32)[:, None])
        counts.append(49.0 * jnp.sum(row_counts).astype(jnp.float32))

    def forward(inputs_f, weight_a, weight_b, weight_c, params_mid, params_out):
        low_a, low_b, low_c = (low(weight_a), low(weight_b), low(weight_c))
        results = [block(inputs_f[k], low_a, low_b, low_c, params_mid, params_out, lives[k], counts[k]) for k in range(MB)]
        return jnp.stack(results)
    block_out, pullback = jax.vjp(forward, inputs.astype(jnp.float32), w_first, w_middle, w_last, mid_params, out_params)
    input_grad, grad_first, grad_middle, grad_last, grad_mid, grad_out = pullback(cotangent.astype(jnp.float32))
    first_new, first_m_new, first_v_new = adamw(w_first, grad_first, first_m, first_v, rate_first)
    middle_new, middle_m_new, middle_v_new = adamw(w_middle, grad_middle, middle_m, middle_v, rate_middle)
    last_new, last_m_new, last_v_new = adamw(w_last, grad_last, last_m, last_v, rate_last)
    mid_new, mid_m_new, mid_v_new = adamw(mid_params, grad_mid, mid_m, mid_v, rate_norm)
    out_new, out_m_new, out_v_new = adamw(out_params, grad_out, out_m, out_v, rate_norm)
    return (block_out, input_grad, first_new, first_m_new, first_v_new, middle_new, middle_m_new, middle_v_new, last_new, last_m_new, last_v_new, mid_new, mid_m_new, mid_v_new, out_new, out_m_new, out_v_new)
```

```python
import functools

import jax
import jax.numpy as jnp
import numpy as np
from jax import lax
from jax.experimental import pallas as pl
from jax.experimental.pallas import tpu as pltpu
from jax.sharding import PartitionSpec as P

STEPS = 5
SIDE = 7
PIXELS = SIDE * SIDE
TAPS = 9
F32 = jnp.float32
BF16 = jnp.bfloat16

norm_eps = 1e-05
adam_eps = 1e-08
adam_beta = 0.5
decay_rate = 0.05
rate_first = 0.02
rate_middle = 0.015
rate_last = 0.04
rate_norm = 0.25


def sigmoid(value):
    return 0.5 * jnp.tanh(0.5 * value) + 0.5


def silu_slope(value):
    sigma = sigmoid(value)
    return sigma * (1.0 + value * (1.0 - sigma))


def moments(stat, count):
    average = stat[0:1] / count
    variance = stat[1:2] / count - average * average
    return average, lax.rsqrt(variance + norm_eps)


def adamw(weight, gradient, moment_one, moment_two, step_rate):
    one_new = adam_beta * moment_one + (1.0 - adam_beta) * gradient
    two_new = adam_beta * moment_two + (1.0 - adam_beta) * gradient * gradient
    correct = 1.0 - adam_beta**STEPS
    weight_new = weight - step_rate * (
        one_new / correct / (jnp.sqrt(two_new / correct) + adam_eps) + decay_rate * weight
    )
    return (weight_new, one_new, two_new)


def ring_of(size):
    across = max(size // 4, 1)
    along = size // across
    order = [(z, 0) for z in range(along)]
    outward = True
    for z in reversed(range(along)):
        steps = list(range(1, across))
        order += [(z, x) for x in (steps if outward else steps[::-1])]
        outward = not outward
    return [z * across + x for z, x in order]


class Ring:
    def __init__(self, size):
        self.size = size
        self.order = ring_of(size)
        ahead = [(self.order[i], self.order[(i + 1) % size]) for i in range(size)]
        self.ahead = ahead
        self.back = [(b, a) for a, b in ahead]
        place = np.argsort(np.array(self.order))
        self.table = np.array(
            [[self.order[(place[c] + k) % size] for k in range(size)] for c in range(size)],
            np.int32,
        )

    def fw(self, x):
        return lax.ppermute(x, "chan", self.ahead)

    def bw(self, x):
        return lax.ppermute(x, "chan", self.back)

    def gather(self, x, axis):
        size, half = self.size, x.shape[axis] // 2
        pieces = [None] * size
        pieces[0] = x
        a = b = x
        for step in range(1, size // 2):
            a, b = self.fw(a), self.bw(b)
            pieces[size - step], pieces[step] = a, b
        low = self.fw(lax.slice_in_dim(a, 0, half, axis=axis))
        high = self.bw(lax.slice_in_dim(b, half, x.shape[axis], axis=axis))
        pieces[size // 2] = (low, high)
        return pieces

    def scatter(self, parts, axis):
        size = self.size
        width = parts[0].shape[axis]
        half = width // 2
        middle = parts[size // 2]
        f = self.fw(lax.slice_in_dim(middle, 0, half, axis=axis))
        b = self.bw(lax.slice_in_dim(middle, half, width, axis=axis))
        for step in range(size // 2 - 1, 0, -1):
            left, right = parts[step], parts[size - step]
            if step == size // 2 - 1:
                f = jnp.concatenate(
                    [
                        add16(lax.slice_in_dim(left, 0, half, axis=axis), f),
                        lax.slice_in_dim(left, half, width, axis=axis),
                    ],
                    axis,
                )
                b = jnp.concatenate(
                    [
                        lax.slice_in_dim(right, 0, half, axis=axis),
                        add16(lax.slice_in_dim(right, half, width, axis=axis), b),
                    ],
                    axis,
                )
            else:
                f, b = add16(left, f), add16(right, b)
            f, b = self.fw(f), self.bw(b)
        return f, b


def add16(one, two):
    return (one.astype(F32) + two.astype(F32)).astype(BF16)


def swap(x, axis, bit, size):
    return lax.ppermute(x, axis, [(i, i ^ bit) for i in range(size)])


def bits_below(size):
    return [1 << k for k in range(size.bit_length() - 1)]


def sum_over(x, axis, bits, size):
    for bit in bits:
        x = x + swap(x, axis, bit, size)
    return x


def run(body, meta, grid, ins, outs, scratch=(), vmem=48, cost=None):
    return pl.pallas_call(
        body,
        grid_spec=pltpu.PrefetchScalarGridSpec(
            num_scalar_prefetch=1,
            grid=grid,
            in_specs=[pl.BlockSpec(b, m) for _, b, m in ins],
            out_specs=[pl.BlockSpec(b, m) for _, _, b, m in outs],
            scratch_shapes=list(scratch),
        ),
        out_shape=[jax.ShapeDtypeStruct(s, d) for s, d, _, _ in outs],
        compiler_params=pltpu.CompilerParams(vmem_limit_bytes=vmem << 20),
        cost_estimate=pl.CostEstimate(
            flops=cost[0], bytes_accessed=cost[1], transcendentals=0
        )
        if cost
        else None,
    )(meta, *[a for a, _, _ in ins])


def whole(x):
    zeros = (0,) * x.ndim
    return (x, x.shape, lambda *_: zeros)


def whole_out(shape, dtype):
    zeros = (0,) * len(shape)
    return (shape, dtype, shape, lambda *_: zeros)


class Sizes:
    def __init__(self, chunks, micro, images):
        self.chunks = chunks
        self.micro = micro
        self.images = images
        self.rows = PIXELS * images
        self.padded = SIDE * 8 * images
        self.live = chunks
        self.batch = 2 * chunks
        self.count = 3 * chunks
        self.planes = 3 * chunks + micro

    def own_count(self, meta):
        batch = meta[self.batch]
        count = meta[self.count]
        for m in range(1, self.micro):
            count = jnp.where(batch == m, meta[self.count + m], count)
        return count.astype(F32)


def split_lanes(value, native):
    for q in range(native.shape[0]):
        native[q] = value[:, q * 128 : (q + 1) * 128]


def to_padded(sz, native, padded):
    n = sz.images
    for q in range(native.shape[0]):
        for i in range(SIDE):
            for j in range(SIDE):
                at = (i * 8 + j) * n
                padded[at : at + n, q * 128 : (q + 1) * 128] = native[
                    q, pl.ds(i * SIDE + j, n, stride=PIXELS), :
                ]
    for i in range(SIDE):
        at = (i * 8 + 7) * n
        padded[at : at + n, :] = jnp.zeros((n, padded.shape[1]), F32)


def to_native(sz, padded, native, out):
    n = sz.images
    for q in range(native.shape[0]):
        for i in range(SIDE):
            for j in range(SIDE):
                at = (i * 8 + j) * n
                native[q, pl.ds(i * SIDE + j, n, stride=PIXELS), :] = padded[
                    at : at + n, q * 128 : (q + 1) * 128
                ]
        out[:, q * 128 : (q + 1) * 128] = native[q].astype(out.dtype)


def row_mask(sz, width, live):
    rows = lax.broadcasted_iota(jnp.int32, (sz.padded, width), 0)
    n = sz.images
    inside = lax.rem(lax.div(rows, n), 8) < SIDE
    if live is None:
        return inside
    return jnp.logical_and(inside, lax.rem(rows, n) < live)


def put_sums(stat, one, two):
    stat[0:1, :] = jnp.sum(one, axis=0, keepdims=True)
    stat[1:2, :] = jnp.sum(two, axis=0, keepdims=True)


def lay_taps(sz, value, strip, taps):
    n = sz.images
    width = strip.shape[1]
    strip[0 : 9 * n, :] = jnp.zeros((9 * n, width), F32)
    strip[65 * n : 74 * n, :] = jnp.zeros((9 * n, width), F32)
    strip[9 * n : 65 * n, :] = value
    for b in range(3):
        taps[b] = strip[b * n : b * n + 72 * n, :].astype(BF16)


def first_body(sz, meta, f, b, own, pre, stat, native):
    split_lanes(f[...].astype(F32) + b[...].astype(F32) + own[0].astype(F32), native)
    to_padded(sz, native, pre)
    value = pre[...]
    kept = jnp.where(row_mask(sz, value.shape[1], meta[sz.live]), value, 0.0)
    put_sums(stat, kept, kept * kept)


def conv_body(sz, meta, pre, stat, params, weight, out, raw, stat_out, taps, strip, total, native):
    step = pl.program_id(0)
    n = sz.images
    width = pre.shape[1]

    @pl.when(step == 0)
    def _():
        average, inv = moments(stat[...], sz.own_count(meta))
        z = params[0:1] * ((pre[...] - average) * inv) + params[1:2]
        act = jnp.where(row_mask(sz, width, None), z * sigmoid(z), 0.0)
        lay_taps(sz, act, strip, taps)
        total[...] = jnp.zeros_like(total)

    at = pl.multiple_of(step * 8 * n, 8 * n)
    for b in range(3):
        total[...] += jnp.dot(
            taps[b, pl.ds(at, sz.padded), :], weight[0, b], preferred_element_type=F32
        )

    @pl.when(step == 2)
    def _():
        value = jnp.where(row_mask(sz, width, None), total[...], 0.0)
        out[...] = value
        to_native(sz, total, native, raw)
        kept = jnp.where(row_mask(sz, width, meta[sz.live]), value, 0.0)
        put_sums(stat_out, kept, kept * kept)


def pick(sz, stat, batch):
    found = stat[0:2]
    for m in range(1, sz.micro):
        found = jnp.where(batch == m, stat[2 * m : 2 * m + 2], found)
    return found


def pick_count(sz, meta, batch):
    count = meta[sz.count]
    for m in range(1, sz.micro):
        count = jnp.where(batch == m, meta[sz.count + m], count)
    return count.astype(F32)


def add_sums(sz, stat, batch, one, two):
    sums = jnp.concatenate(
        [jnp.sum(one, axis=0, keepdims=True), jnp.sum(two, axis=0, keepdims=True)], axis=0
    )
    for m in range(sz.micro):
        stat[2 * m : 2 * m + 2, :] += jnp.where(batch == m, sums, 0.0)


def stage_piece(pieces, place, step):
    for k, piece in enumerate(pieces):

        @pl.when(step == k)
        def _(piece=piece):
            if len(piece) == 1:
                place[...] = piece[0][...]
            else:
                half = piece[0].shape[1]
                place[:, :half] = piece[0][...]
                place[:, half:] = piece[1][...]


def split_refs(layout, refs):
    pieces, at = [], 0
    for many in layout:
        pieces.append(refs[at : at + many])
        at += many
    return pieces, refs[at:]


def expand_body(sz, layout, meta, *refs):
    pieces, rest = split_refs(layout, refs)
    stat, params, weight, act, pre, stat_out, place = rest
    step = pl.program_id(0)
    stage_piece(pieces, place, step)
    batch = meta[sz.batch + step]
    average, inv = moments(pick(sz, stat[...], batch), pick_count(sz, meta, batch))
    z = params[2:3] * ((place[...].astype(F32) - average) * inv) + params[3:4]
    acted = (z * sigmoid(z)).astype(BF16)
    act[0] = acted
    value = jnp.dot(acted, weight[...], preferred_element_type=F32)
    pre[0] = value

    @pl.when(step == 0)
    def _():
        stat_out[...] = jnp.zeros_like(stat_out)

    rows = lax.broadcasted_iota(jnp.int32, value.shape, 0)
    kept = jnp.where(rows < PIXELS * meta[sz.live + step], value, 0.0)
    add_sums(sz, stat_out, batch, kept, kept * kept)


def out_body(sz, meta, pre, stat, params, x, cot, out, grad, stat_out):
    step = pl.program_id(0)
    batch = meta[sz.batch + step]
    average, inv = moments(pick(sz, stat[...], batch), pick_count(sz, meta, batch))
    normed = (pre[0] - average) * inv
    summed = params[0:1] * normed + params[1:2] + x[0].astype(F32)
    sigma = sigmoid(summed)
    rows = lax.broadcasted_iota(jnp.int32, summed.shape, 0)
    live = rows < PIXELS * meta[sz.live + step]
    out[0] = jnp.where(live, summed * sigma, 0.0)
    upstream = jnp.where(
        live, cot[0].astype(F32) * (sigma * (1.0 + summed * (1.0 - sigma))), 0.0
    )
    grad[0] = upstream

    @pl.when(step == 0)
    def _():
        stat_out[...] = jnp.zeros_like(stat_out)

    add_sums(sz, stat_out, batch, upstream, upstream * normed)


def shrink_body(sz, meta, pre, stat, params, grad, sums, weight, back, part):
    step = pl.program_id(0)
    batch = meta[sz.batch + step]
    count = pick_count(sz, meta, batch)
    average, inv = moments(pick(sz, stat[...], batch), count)
    both = pick(sz, sums[...], batch)
    normed = (pre[0] - average) * inv
    rows = lax.broadcasted_iota(jnp.int32, normed.shape, 0)
    live = rows < PIXELS * meta[sz.live + step]
    value = params[0:1] * inv * (grad[0] - (both[0:1] + normed * both[1:2]) / count)
    value = jnp.where(live, value, 0.0).astype(BF16)
    back[0] = value
    part[0] = lax.dot_general(
        value, weight[...], (((1,), (1,)), ((), ())), preferred_element_type=F32
    ).astype(BF16)


def middle_up_body(sz, meta, f, b, own, pre, stat, params, up, stat_out, native, padded):
    split_lanes(f[...].astype(F32) + b[...].astype(F32) + own[0].astype(F32), native)
    to_padded(sz, native, padded)
    average, inv = moments(stat[...], sz.own_count(meta))
    normed = (pre[...] - average) * inv
    z = params[2:3] * normed + params[3:4]
    value = jnp.where(
        row_mask(sz, pre.shape[1], meta[sz.live]), padded[...] * silu_slope(z), 0.0
    )
    up[...] = value
    put_sums(stat_out, value, value * normed)


def conv_back_body(
    sz,
    meta,
    up,
    sums,
    pre_two,
    stat_two,
    pre_one,
    stat_one,
    params,
    weight,
    back,
    up_one,
    stat_out,
    strip,
    taps,
    total,
):
    step = pl.program_id(0)
    n = sz.images
    width = up.shape[1]

    @pl.when(step == 0)
    def _():
        count = sz.own_count(meta)
        average, inv = moments(stat_two[...], count)
        normed = (pre_two[...] - average) * inv
        value = params[2:3] * inv * (up[...] - (sums[0:1] + normed * sums[1:2]) / count)
        value = jnp.where(row_mask(sz, width, meta[sz.live]), value, 0.0)
        back[...] = value.astype(BF16)
        lay_taps(sz, value, strip, taps)
        total[...] = jnp.zeros_like(total)

    at = pl.multiple_of((2 - step) * 8 * n, 8 * n)
    for b in range(3):
        total[...] += lax.dot_general(
            taps[2 - b, pl.ds(at, sz.padded), :],
            weight[0, b],
            (((1,), (1,)), ((), ())),
            preferred_element_type=F32,
        )

    @pl.when(step == 2)
    def _():
        average, inv = moments(stat_one[...], sz.own_count(meta))
        normed = (pre_one[...] - average) * inv
        z = params[0:1] * normed + params[1:2]
        value = jnp.where(
            row_mask(sz, width, meta[sz.live]), total[...] * silu_slope(z), 0.0
        )
        up_one[...] = value
        put_sums(stat_out, value, value * normed)


def first_back_body(sz, meta, up, sums, pre, stat, params, back, padded, native):
    count = sz.own_count(meta)
    average, inv = moments(stat[...], count)
    normed = (pre[...] - average) * inv
    value = params[0:1] * inv * (up[...] - (sums[0:1] + normed * sums[1:2]) / count)
    padded[...] = jnp.where(row_mask(sz, pre.shape[1], meta[sz.live]), value, 0.0)
    to_native(sz, padded, native, back)


def input_body(sz, layout, meta, *refs):
    pieces, rest = split_refs(layout, refs)
    grad, x, weight, out, grad_weight, place, total = rest
    step = pl.program_id(0)
    stage_piece(pieces, place, step)
    value = place[...]
    out[0] = grad[0] + lax.dot_general(
        value, weight[...], (((1,), (1,)), ((), ())), preferred_element_type=F32
    )

    @pl.when(step == 0)
    def _():
        total[...] = jnp.zeros_like(total)

    total[...] += lax.dot_general(
        x[0], value, (((0,), (0,)), ((), ())), preferred_element_type=F32
    )

    @pl.when(step == sz.chunks - 1)
    def _():
        grad_weight[...] = total[...].astype(BF16)


def middle_grad_body(sz, dp, meta, taps, back, out, whole_grad):
    step = pl.program_id(0)
    n = sz.images
    at = pl.multiple_of(lax.div(step, 3) * 8 * n, 8 * n)
    window = taps[lax.rem(step, 3), pl.ds(at, sz.padded), :]
    value = lax.dot_general(
        window, back[...], (((0,), (0,)), ((), ())), preferred_element_type=F32
    )
    lanes = value.shape[1] // dp
    for d in range(dp):
        whole_grad[d] = value[:, d * lanes : (d + 1) * lanes]
    depth = value.shape[0] // sz.chunks
    for p in range(dp):
        for k in range(sz.chunks):
            at = pl.multiple_of(meta[k] * depth, depth)
            out[p, k, 0] = whole_grad[meta[sz.planes + p], pl.ds(at, depth), :].astype(BF16)


def assemble_body(sz, half, meta, near, far, out):
    @pl.when(pl.program_id(0) < half)
    def _():
        out[...] = near[0, 0]

    @pl.when(pl.program_id(0) >= half)
    def _():
        out[...] = far[0, 0]


def last_assemble_body(meta, blocks, out):
    lanes = blocks.shape[3]
    for b in range(blocks.shape[1]):
        out[:, b * lanes : (b + 1) * lanes] = blocks[0, b]


def copy_body(meta, source, out):
    out[...] = source[...]


def reorder(sz, meta, x, inward):
    rest = x.shape[2:]

    def ordered(p, k, meta):
        return (p, k) + (0,) * len(rest)

    def placed(p, k, meta):
        return (meta[sz.planes + p], meta[k]) + (0,) * len(rest)

    (moved,) = run(
        copy_body,
        meta,
        x.shape[:2],
        [(x, (1, 1) + rest, placed if inward else ordered)],
        [(x.shape, x.dtype, (1, 1) + rest, ordered if inward else placed)],
        vmem=16,
    )
    return moved


def last_grad_body(sz, meta, act, back, out, total):
    step = pl.program_id(0)

    @pl.when(step == 0)
    def _():
        total[...] = jnp.zeros_like(total)

    total[...] += lax.dot_general(
        act[0], back[0], (((0,), (0,)), ((), ())), preferred_element_type=F32
    )

    @pl.when(step == sz.chunks - 1)
    def _():
        depth = out.shape[1]
        for k in range(sz.chunks):
            at = pl.multiple_of(meta[k] * depth, depth)
            out[k] = total[pl.ds(at, depth), :].astype(BF16)


def pieces_in(sz, pieces):
    ins, layout = [], []
    for piece in pieces:
        parts = piece if isinstance(piece, tuple) else (piece,)
        layout.append(len(parts))
        ins += [whole(p) for p in parts]
    return ins, layout


def local(
    dp,
    chan,
    inputs,
    cotangent,
    w_first,
    first_m,
    first_v,
    w_middle,
    middle_m,
    middle_v,
    w_last,
    last_m,
    last_v,
    mid_params,
    mid_m,
    mid_v,
    out_params,
    out_m,
    out_v,
    image_counts,
):
    ring = Ring(chan)
    d = lax.axis_index("dp")
    c = lax.axis_index("chan")
    micro, pixels, deep = inputs.shape
    images = micro * pixels // PIXELS // chan
    sz = Sizes(chan, micro, images)
    rows, padded = sz.rows, sz.padded
    per_batch = chan // micro
    depth, lanes = w_middle.shape[2], w_middle.shape[3]
    mid = depth * chan
    half = dp // 2
    last_blocks = w_last.shape[1] // lanes
    own_blocks = deep // lanes
    ratio = last_blocks // own_blocks

    at = lax.dynamic_index_in_dim(jnp.asarray(ring.table), c, keepdims=False)
    batch = at // per_batch
    own_counts = lax.dynamic_index_in_dim(image_counts, d, axis=1, keepdims=False)
    counts_at = own_counts[0]
    for m in range(1, micro):
        counts_at = jnp.where(batch == m, own_counts[m], counts_at)
    live = jnp.clip(counts_at - images * (at % per_batch), 0, images)
    planes = d ^ jnp.asarray([(p % half) * 2 + p // half for p in range(dp)], jnp.int32)
    meta = jnp.concatenate(
        [at, live, batch, PIXELS * jnp.sum(image_counts, axis=1), planes]
    ).astype(jnp.int32)

    first = w_first.astype(BF16)
    for bit in bits_below(dp):
        other = swap(first, "dp", bit, dp)
        first = jnp.where(
            (d & bit) == 0,
            jnp.concatenate([first, other], axis=1),
            jnp.concatenate([other, first], axis=1),
        )
    one = mid_params.astype(BF16)
    left = mid_params - one.astype(F32)
    two = left.astype(BF16)
    three = (left - two.astype(F32)).astype(BF16)
    param_rows = jnp.concatenate([one, two, three], axis=0)
    param_rows = jnp.pad(param_rows, ((0, 4), (0, lanes - depth)))
    low_last = w_last.astype(BF16)
    payload = jnp.concatenate(
        [w_middle.astype(BF16).reshape(TAPS * depth, lanes)]
        + [low_last[:, b * lanes : (b + 1) * lanes] for b in range(last_blocks)]
        + [param_rows],
        axis=0,
    )
    got = ring.gather(payload, 0)
    got[chan // 2] = jnp.concatenate(got[chan // 2], axis=0)
    got = jnp.stack(got)
    mids = got[:, : TAPS * depth]
    lasts = got[:, TAPS * depth : (TAPS + last_blocks) * depth].reshape(
        chan, ratio, own_blocks, depth, lanes
    )
    tail = got[:, (TAPS + last_blocks) * depth :, :depth].astype(F32)
    tail = (tail[:, 8:12] + tail[:, 4:8]) + tail[:, 0:4]
    here = (at[None, :] == jnp.arange(chan)[:, None])[:, :, None, None]
    params = jnp.sum(jnp.where(here, tail[None], 0.0), axis=1)
    params = params.transpose(1, 0, 2).reshape(4, mid)

    near = mids[None]
    for bit in bits_below(dp)[1:]:
        near = jnp.concatenate([near, swap(near, "dp", bit, dp)], axis=0)
    far = swap(near, "dp", 1, dp)
    if lanes % 128 == 0:
        near = near.reshape(half, chan, TAPS, depth, lanes)
        far = far.reshape(half, chan, TAPS, depth, lanes)
        (middle,) = run(
            functools.partial(assemble_body, sz, half),
            meta,
            (dp, chan),
            [
                (
                    near,
                    (1, 1, TAPS, depth, lanes),
                    lambda p, k, meta: (
                        jnp.minimum(p, half - 1),
                        jnp.where(p < half, k, chan - 1),
                        0,
                        0,
                        0,
                    ),
                ),
                (
                    far,
                    (1, 1, TAPS, depth, lanes),
                    lambda p, k, meta: (
                        jnp.maximum(p - half, 0),
                        jnp.where(p < half, 0, k),
                        0,
                        0,
                        0,
                    ),
                ),
            ],
            [
                (
                    (TAPS, mid, mid),
                    BF16,
                    (TAPS, depth, lanes),
                    lambda p, k, meta: (0, meta[k], meta[sz.planes + p]),
                )
            ],
            vmem=16,
            cost=(0, 4 * TAPS * mid * mid),
        )
    else:
        both = jnp.concatenate([near, far], axis=0)
        middle = (
            reorder(sz, meta, both, False)
            .reshape(dp, chan, TAPS, depth, lanes)
            .transpose(2, 1, 3, 0, 4)
            .reshape(TAPS, mid, mid)
        )
    middle = middle.reshape(3, 3, mid, mid)

    own_last = lax.dynamic_index_in_dim(lasts, c % ratio, axis=1, keepdims=False)
    found = jnp.where(d == c // ratio, own_last, jnp.zeros_like(own_last))
    for shift in range(1, dp):
        moves = [
            ((k // ratio) * chan + k, ((k // ratio) ^ shift) * chan + k) for k in range(chan)
        ]
        found = found + lax.ppermute(own_last, ("dp", "chan"), moves)
    (last,) = run(
        last_assemble_body,
        meta,
        (chan,),
        [(found, (1, own_blocks, depth, lanes), lambda k, meta: (k, 0, 0, 0))],
        [((mid, deep), BF16, (depth, deep), lambda k, meta: (meta[k], 0))],
        vmem=16,
        cost=(0, 4 * mid * deep),
    )

    x = inputs.reshape(chan, rows, deep)
    cot = cotangent.reshape(chan, rows, deep)

    def at_place(k, meta):
        return (meta[k], 0, 0)

    def in_order(k, meta):
        return (k, 0, 0)

    def first_part_body(meta, x_ref, weight, out):
        out[0] = jnp.dot(x_ref[0], weight[...], preferred_element_type=F32).astype(BF16)

    (parts,) = run(
        first_part_body,
        meta,
        (chan,),
        [(x, (1, rows, deep), at_place), whole(first)],
        [((chan, rows, mid), BF16, (1, rows, mid), in_order)],
        vmem=16,
        cost=(2 * chan * rows * deep * mid, 2 * chan * rows * (deep + mid)),
    )
    f, b = ring.scatter(parts, 1)

    def head(stack):
        return (stack, (1,) + stack.shape[1:], lambda *_: (0, 0, 0))

    stat_bits = [k for k in bits_below(chan) if k < per_batch]

    def total_rows(stat):
        stat = sum_over(stat, "dp", bits_below(dp), dp)
        return sum_over(stat, "chan", stat_bits, chan)

    def all_batches(stat):
        for bit in bits_below(chan):
            if bit >= per_batch:
                other = swap(stat, "chan", bit, chan)
                stat = jnp.where(
                    (c & bit) == 0,
                    jnp.concatenate([stat, other], axis=0),
                    jnp.concatenate([other, stat], axis=0),
                )
        return stat

    pre_one, stat_one = run(
        functools.partial(first_body, sz),
        meta,
        (1,),
        [whole(f), whole(b), head(parts)],
        [whole_out((padded, mid), F32), whole_out((2, mid), F32)],
        [pltpu.VMEM((mid // 128, rows, 128), F32)],
        vmem=16,
        cost=(10 * padded * mid, 10 * padded * mid),
    )
    stat_one = total_rows(stat_one)

    tap_block = (1, 3, mid, mid)
    conv_flops = 2 * TAPS * padded * mid * mid
    conv_bytes = 2 * TAPS * mid * mid + 16 * padded * mid
    pre_two, raw, stat_two, taps = run(
        functools.partial(conv_body, sz),
        meta,
        (3,),
        [
            whole(pre_one),
            whole(stat_one),
            whole(params),
            (middle, tap_block, lambda s, meta: (s, 0, 0, 0)),
        ],
        [
            whole_out((padded, mid), F32),
            whole_out((rows, mid), BF16),
            whole_out((2, mid), F32),
            whole_out((3, 72 * images, mid), BF16),
        ],
        [
            pltpu.VMEM((74 * images, mid), F32),
            pltpu.VMEM((padded, mid), F32),
            pltpu.VMEM((mid // 128, rows, 128), F32),
        ],
        vmem=32,
        cost=(conv_flops, conv_bytes),
    )
    pieces = ring.gather(raw, 1)
    stat_two = total_rows(stat_two)
    stats_two = all_batches(stat_two)

    ins, layout = pieces_in(sz, pieces)
    act, pre_three, stat_three = run(
        functools.partial(expand_body, sz, layout),
        meta,
        (chan,),
        ins + [whole(stats_two), whole(params), whole(last)],
        [
            ((chan, rows, mid), BF16, (1, rows, mid), in_order),
            ((chan, rows, deep), F32, (1, rows, deep), in_order),
            whole_out((2 * micro, deep), F32),
        ],
        [pltpu.VMEM((rows, mid), BF16)],
        vmem=32,
        cost=(2 * chan * rows * deep * mid, chan * rows * (4 * mid + 4 * deep)),
    )
    stat_three = sum_over(stat_three, "dp", bits_below(dp), dp)
    block_out, grad_summed, sums_three = run(
        functools.partial(out_body, sz),
        meta,
        (chan,),
        [
            (pre_three, (1, rows, deep), in_order),
            whole(stat_three),
            whole(out_params),
            (x, (1, rows, deep), at_place),
            (cot, (1, rows, deep), at_place),
        ],
        [
            ((chan, rows, deep), F32, (1, rows, deep), at_place),
            ((chan, rows, deep), F32, (1, rows, deep), in_order),
            whole_out((2 * micro, deep), F32),
        ],
        vmem=24,
        cost=(20 * chan * rows * deep, 16 * chan * rows * deep),
    )
    sums_three = sum_over(sums_three, "dp", bits_below(dp), dp)
    back_last, back_parts = run(
        functools.partial(shrink_body, sz),
        meta,
        (chan,),
        [
            (pre_three, (1, rows, deep), in_order),
            whole(stat_three),
            whole(out_params),
            (grad_summed, (1, rows, deep), in_order),
            whole(sums_three),
            whole(last),
        ],
        [
            ((chan, rows, deep), BF16, (1, rows, deep), in_order),
            ((chan, rows, mid), BF16, (1, rows, mid), in_order),
        ],
        vmem=24,
        cost=(2 * chan * rows * deep * mid, chan * rows * (2 * mid + 10 * deep)),
    )
    f, b = ring.scatter(back_parts, 1)

    (grad_last,) = run(
        functools.partial(last_grad_body, sz),
        meta,
        (chan,),
        [(act, (1, rows, mid), in_order), (back_last, (1, rows, deep), in_order)],
        [whole_out((chan, depth, deep), BF16)],
        [pltpu.VMEM((mid, deep), F32)],
        vmem=16,
        cost=(2 * chan * rows * deep * mid, 2 * chan * rows * (mid + deep)),
    )
    for bit in bits_below(dp):
        grad_last = add16(grad_last, swap(grad_last, "dp", bit, dp))
    held = [
        jnp.where(c % ratio == r, grad_last, jnp.zeros_like(grad_last)) for r in range(ratio)
    ]
    held = jnp.concatenate(held, axis=2)
    held = jnp.where(d == c // ratio, held, jnp.zeros_like(held))
    last_f, last_b = ring.scatter(held, 1)
    owned_last = held[0].astype(F32) + last_f.astype(F32) + last_b.astype(F32)

    up_two, sums_two = run(
        functools.partial(middle_up_body, sz),
        meta,
        (1,),
        [
            whole(f),
            whole(b),
            head(back_parts),
            whole(pre_two),
            whole(stat_two),
            whole(params),
        ],
        [whole_out((padded, mid), F32), whole_out((2, mid), F32)],
        [pltpu.VMEM((mid // 128, rows, 128), F32), pltpu.VMEM((padded, mid), F32)],
        vmem=16,
        cost=(20 * padded * mid, 14 * padded * mid),
    )
    sums_two = total_rows(sums_two)
    back_two, up_one, sums_one = run(
        functools.partial(conv_back_body, sz),
        meta,
        (3,),
        [
            whole(up_two),
            whole(sums_two),
            whole(pre_two),
            whole(stat_two),
            whole(pre_one),
            whole(stat_one),
            whole(params),
            (middle, tap_block, lambda s, meta: (s, 0, 0, 0)),
        ],
        [
            whole_out((padded, mid), BF16),
            whole_out((padded, mid), F32),
            whole_out((2, mid), F32),
        ],
        [
            pltpu.VMEM((74 * images, mid), F32),
            pltpu.VMEM((3, 72 * images, mid), BF16),
            pltpu.VMEM((padded, mid), F32),
        ],
        vmem=32,
        cost=(conv_flops, conv_bytes),
    )
    sums_one = total_rows(sums_one)
    (back_one,) = run(
        functools.partial(first_back_body, sz),
        meta,
        (1,),
        [whole(up_one), whole(sums_one), whole(pre_one), whole(stat_one), whole(params)],
        [whole_out((rows, mid), BF16)],
        [pltpu.VMEM((padded, mid), F32), pltpu.VMEM((mid // 128, rows, 128), F32)],
        vmem=16,
        cost=(10 * padded * mid, 10 * padded * mid),
    )
    pieces = ring.gather(back_one, 1)

    if lanes % 128 == 0:
        (grad_middle,) = run(
            functools.partial(middle_grad_body, sz, dp),
            meta,
            (TAPS,),
            [whole(taps), whole(back_two)],
            [
                (
                    (dp, chan, TAPS, depth, lanes),
                    BF16,
                    (dp, chan, 1, depth, lanes),
                    lambda s, meta: (0, 0, s, 0, 0),
                )
            ],
            [pltpu.VMEM((dp, mid, lanes), F32)],
            vmem=32,
            cost=(conv_flops, conv_bytes),
        )
    else:

        def plain_grad_body(meta, taps, back, out):
            step = pl.program_id(0)
            start = pl.multiple_of(lax.div(step, 3) * 8 * images, 8 * images)
            window = taps[lax.rem(step, 3), pl.ds(start, padded), :]
            out[0] = lax.dot_general(
                window, back[...], (((0,), (0,)), ((), ())), preferred_element_type=F32
            ).astype(BF16)

        (grad_middle,) = run(
            plain_grad_body,
            meta,
            (TAPS,),
            [whole(taps), whole(back_two)],
            [((TAPS, mid, mid), BF16, (1, mid, mid), lambda s, meta: (s, 0, 0))],
            vmem=32,
            cost=(conv_flops, conv_bytes),
        )
        grad_middle = grad_middle.reshape(TAPS, chan, depth, dp, lanes).transpose(3, 1, 0, 2, 4)
        grad_middle = reorder(sz, meta, grad_middle, True)
    kept = grad_middle.reshape(dp, chan, TAPS * depth, lanes)
    for bit in [1] + bits_below(dp)[:0:-1]:
        cut = kept.shape[0] // 2
        kept = add16(kept[:cut], swap(kept[cut:], "dp", bit, dp))
    kept = kept[0]
    middle_f, middle_b = ring.scatter(kept, 0)
    owned_middle = kept[0].astype(F32) + middle_f.astype(F32) + middle_b.astype(F32)
    owned_middle = owned_middle.reshape(3, 3, depth, lanes)

    ins, layout = pieces_in(sz, pieces)
    input_grad, grad_first = run(
        functools.partial(input_body, sz, layout),
        meta,
        (chan,),
        ins
        + [
            (grad_summed, (1, rows, deep), in_order),
            (x, (1, rows, deep), at_place),
            whole(first),
        ],
        [
            ((chan, rows, deep), F32, (1, rows, deep), at_place),
            whole_out((deep, mid), BF16),
        ],
        [pltpu.VMEM((rows, mid), BF16), pltpu.VMEM((deep, mid), F32)],
        vmem=32,
        cost=(4 * chan * rows * deep * mid, chan * rows * (2 * mid + 10 * deep)),
    )
    owned_first = scatter_columns(grad_first, d, dp)

    sums_first, sums_middle = all_batches(sums_one), all_batches(sums_two)

    def over_batches(stat, row):
        total = stat[row]
        for m in range(1, micro):
            total = total + stat[2 * m + row]
        return total

    grad_mid = jnp.stack(
        [
            over_batches(sums_first, 1),
            over_batches(sums_first, 0),
            over_batches(sums_middle, 1),
            over_batches(sums_middle, 0),
        ]
    )
    grad_mid = lax.dynamic_slice_in_dim(grad_mid, c * depth, depth, axis=1)
    grad_out = jnp.stack([over_batches(sums_three, 1), over_batches(sums_three, 0)])

    return (
        block_out.reshape(inputs.shape),
        input_grad.reshape(inputs.shape),
        *adamw(w_first, owned_first, first_m, first_v, rate_first),
        *adamw(w_middle, owned_middle, middle_m, middle_v, rate_middle),
        *adamw(w_last, owned_last, last_m, last_v, rate_last),
        *adamw(mid_params, grad_mid, mid_m, mid_v, rate_norm),
        *adamw(out_params, grad_out, out_m, out_v, rate_norm),
    )


def scatter_columns(grad, d, dp):
    blocks = grad.reshape(grad.shape[0], dp, grad.shape[1] // dp)
    kept = [blocks[:, p] for p in range(dp)]
    for bit in bits_below(dp):
        kept = [
            jnp.where((d & bit) == 0, kept[q], kept[q ^ bit]) for q in range(len(kept))
        ]
    todo = {q: kept[q] for q in range(dp)}
    for bit in [1] + bits_below(dp)[:0:-1]:
        send = sorted(q for q in todo if q & bit)
        stay = sorted(q for q in todo if not q & bit)
        got = swap(jnp.stack([todo[q] for q in send]), "dp", bit, dp)
        todo = {
            q: todo[q].astype(F32) + got[send.index(q | bit)].astype(F32) for q in stay
        }
        if len(todo) > 1:
            todo = {q: v.astype(BF16) for q, v in todo.items()}
    return todo[0]


def solution(mesh):
    rows = P(None, "dp", "chan")
    flat = P("chan", "dp")
    square = P(None, None, "chan", "dp")
    vector = P(None, "chan")
    state = (flat,) * 3 + (square,) * 3 + (flat,) * 3 + (vector,) * 6
    return jax.shard_map(
        functools.partial(local, mesh.shape["dp"], mesh.shape["chan"]),
        mesh=mesh,
        in_specs=(rows, rows) + state + (P(),),
        out_specs=(rows, rows) + state,
        check_vma=False,
    )
```

```python
import functools

import jax
import jax.numpy as jnp
import numpy as np
from jax import lax
from jax.experimental import pallas as pl
from jax.experimental.pallas import tpu as pltpu
from jax.sharding import PartitionSpec as P

STEPS = 5
SIDE = 7
PIXELS = SIDE * SIDE
TAPS = 9
VMEM = 24
F32 = jnp.float32
BF16 = jnp.bfloat16

norm_eps = 1e-05
adam_eps = 1e-08
adam_beta = 0.5
decay_rate = 0.05
rate_first = 0.02
rate_middle = 0.015
rate_last = 0.04
rate_norm = 0.25


def sigmoid(value):
    return 0.5 * jnp.tanh(0.5 * value) + 0.5


def silu_slope(value):
    sigma = sigmoid(value)
    return sigma * (1.0 + value * (1.0 - sigma))


def moments(stat, count):
    average = stat[0:1] / count
    variance = stat[1:2] / count - average * average
    return average, lax.rsqrt(variance + norm_eps)


def adamw(weight, gradient, moment_one, moment_two, step_rate):
    one_new = adam_beta * moment_one + (1.0 - adam_beta) * gradient
    two_new = adam_beta * moment_two + (1.0 - adam_beta) * gradient * gradient
    correct = 1.0 - adam_beta**STEPS
    weight_new = weight - step_rate * (
        one_new / correct / (jnp.sqrt(two_new / correct) + adam_eps) + decay_rate * weight
    )
    return (weight_new, one_new, two_new)


def ring_of(size):
    across = max(size // 4, 1)
    along = size // across
    order = [(z, 0) for z in range(along)]
    outward = True
    for z in reversed(range(along)):
        steps = list(range(1, across))
        order += [(z, x) for x in (steps if outward else steps[::-1])]
        outward = not outward
    return [z * across + x for z, x in order]


class Ring:
    def __init__(self, size):
        self.size = size
        self.order = ring_of(size)
        ahead = [(self.order[i], self.order[(i + 1) % size]) for i in range(size)]
        self.ahead = ahead
        self.back = [(b, a) for a, b in ahead]
        place = np.argsort(np.array(self.order))
        self.table = np.array(
            [[self.order[(place[c] + k) % size] for k in range(size)] for c in range(size)],
            np.int32,
        )

    def fw(self, x):
        return lax.ppermute(x, "chan", self.ahead)

    def bw(self, x):
        return lax.ppermute(x, "chan", self.back)


def tie(x, other):
    first = lax.slice(other, (0,) * other.ndim, (1,) * other.ndim).reshape(())
    return jnp.where(first > -3e38, x, jnp.zeros_like(x))


class Gather:
    def __init__(self, ring, x, axis):
        self.ring, self.axis, self.half = ring, axis, x.shape[axis] // 2
        self.pieces = [x] + [None] * (ring.size - 1)
        self.count = 0

    def step(self, other=None):
        ring, size = self.ring, self.ring.size
        a, b = self.pieces[(size - self.count) % size], self.pieces[self.count]
        if other is not None:
            a, b = tie(a, other), tie(b, other)
        self.count += 1
        if self.count < size // 2:
            got = [ring.fw(a), ring.bw(b)]
            self.pieces[size - self.count], self.pieces[self.count] = got
        else:
            got = [
                ring.fw(lax.slice_in_dim(a, 0, self.half, axis=self.axis)),
                ring.bw(lax.slice_in_dim(b, self.half, b.shape[self.axis], axis=self.axis)),
            ]
            self.pieces[size // 2] = tuple(got)
        return got


class Scatter:
    def __init__(self, ring, low, high, part, axis):
        self.ring, self.part, self.axis = ring, part, axis
        self.f, self.b = ring.fw(low), ring.bw(high)
        self.count = 1

    def step(self):
        size, axis = self.ring.size, self.axis
        k = size // 2 - self.count
        left, right = self.part(k), self.part(size - k)
        if self.count == 1:
            width = left.shape[axis]
            half = width // 2
            f = jnp.concatenate(
                [
                    add16(lax.slice_in_dim(left, 0, half, axis=axis), self.f),
                    lax.slice_in_dim(left, half, width, axis=axis),
                ],
                axis,
            )
            b = jnp.concatenate(
                [
                    lax.slice_in_dim(right, 0, half, axis=axis),
                    add16(lax.slice_in_dim(right, half, width, axis=axis), self.b),
                ],
                axis,
            )
        else:
            f, b = add16(left, self.f), add16(right, self.b)
        self.count += 1
        self.f, self.b = self.ring.fw(f), self.ring.bw(b)


def add16(one, two):
    return (one.astype(F32) + two.astype(F32)).astype(BF16)


def swap(x, axis, bit, size):
    return lax.ppermute(x, axis, [(i, i ^ bit) for i in range(size)])


def bits_below(size):
    return [1 << k for k in range(size.bit_length() - 1)]


def sum_over(x, axis, bits, size):
    for bit in bits:
        x = x + swap(x, axis, bit, size)
    return x


def run(body, meta, grid, ins, outs, scratch=(), vmem=VMEM, cost=None, after=(), into=()):
    extra = list(into) + list(after)
    first, last = len(ins), len(ins) + len(extra)

    def kernel(meta, *refs):
        body(meta, *refs[:first], *refs[last:])

    return pl.pallas_call(
        kernel if extra else body,
        grid_spec=pltpu.PrefetchScalarGridSpec(
            num_scalar_prefetch=1,
            grid=grid,
            in_specs=[pl.BlockSpec(b, m) for _, b, m in ins]
            + [pl.BlockSpec(memory_space=pl.ANY)] * len(extra),
            out_specs=[pl.BlockSpec(b, m) for _, _, b, m in outs],
            scratch_shapes=list(scratch),
        ),
        out_shape=[jax.ShapeDtypeStruct(s, d) for s, d, _, _ in outs],
        compiler_params=pltpu.CompilerParams(vmem_limit_bytes=vmem << 20),
        cost_estimate=pl.CostEstimate(
            flops=cost[0], bytes_accessed=cost[1], transcendentals=0
        )
        if cost
        else None,
        input_output_aliases={1 + first + q: q for q in range(len(into))},
    )(meta, *[a for a, _, _ in ins], *extra)


def whole(x):
    zeros = (0,) * x.ndim
    return (x, x.shape, lambda *_: zeros)


def whole_out(shape, dtype):
    zeros = (0,) * len(shape)
    return (shape, dtype, shape, lambda *_: zeros)


class Sizes:
    def __init__(self, chunks, micro, images):
        self.chunks = chunks
        self.half = chunks // 2
        self.micro = micro
        self.images = images
        self.rows = PIXELS * images
        self.padded = SIDE * 8 * images
        self.live = chunks
        self.batch = 2 * chunks
        self.count = 3 * chunks
        self.arrive = 3 * chunks + micro
        self.planes = 4 * chunks + micro
        self.arrival = [0]
        for step in range(1, chunks // 2):
            self.arrival += [chunks - step, step]
        self.arrival.append(chunks // 2)

    def own_count(self, meta):
        batch = meta[self.batch]
        count = meta[self.count]
        for m in range(1, self.micro):
            count = jnp.where(batch == m, meta[self.count + m], count)
        return count.astype(F32)


def split_lanes(value, native):
    for q in range(native.shape[0]):
        native[q] = value[:, q * 128 : (q + 1) * 128]


def meta_body(sz, dp, ratio, counts, table, out):
    d, c = lax.axis_index("dp"), lax.axis_index("chan")
    per_batch = sz.chunks // sz.micro
    for k in range(sz.chunks):
        chunk = table[c, k]
        batch = lax.div(chunk, per_batch)
        have = counts[batch, d] - sz.images * lax.rem(chunk, per_batch)
        out[k] = chunk
        out[sz.live + k] = jnp.minimum(jnp.maximum(have, 0), sz.images)
        out[sz.batch + k] = batch
        out[sz.arrive + k] = jnp.int32(sz.arrival[k])
    for m in range(sz.micro):
        total = counts[m, 0]
        for g in range(1, dp):
            total += counts[m, g]
        out[sz.count + m] = PIXELS * total
    for p in range(dp):
        out[sz.planes + p] = d ^ ((p % (dp // 2)) * 2 + p // (dp // 2))
    out[sz.planes + dp] = lax.div(c, ratio)
    out[sz.planes + dp + 1] = lax.rem(c, ratio)


def make_meta(sz, ring, dp, ratio, counts):
    smem = pl.BlockSpec(memory_space=pltpu.SMEM)
    return pl.pallas_call(
        functools.partial(meta_body, sz, dp, ratio),
        in_specs=[smem, smem],
        out_specs=smem,
        out_shape=jax.ShapeDtypeStruct((sz.planes + dp + 2,), jnp.int32),
    )(counts, jnp.asarray(ring.table))


def to_padded(sz, native, padded):
    n = sz.images
    for q in range(native.shape[0]):
        for i in range(SIDE):
            for j in range(SIDE):
                at = (i * 8 + j) * n
                padded[at : at + n, q * 128 : (q + 1) * 128] = native[
                    q, pl.ds(i * SIDE + j, n, stride=PIXELS), :
                ]
    for i in range(SIDE):
        at = (i * 8 + 7) * n
        padded[at : at + n, :] = jnp.zeros((n, padded.shape[1]), F32)


def to_native(sz, padded, native, out):
    n = sz.images
    for q in range(native.shape[0]):
        for i in range(SIDE):
            for j in range(SIDE):
                at = (i * 8 + j) * n
                native[q, pl.ds(i * SIDE + j, n, stride=PIXELS), :] = padded[
                    at : at + n, q * 128 : (q + 1) * 128
                ]
        out[:, q * 128 : (q + 1) * 128] = native[q].astype(out.dtype)


def row_mask(sz, width, live):
    rows = lax.broadcasted_iota(jnp.int32, (sz.padded, width), 0)
    n = sz.images
    inside = lax.rem(lax.div(rows, n), 8) < SIDE
    if live is None:
        return inside
    return jnp.logical_and(inside, lax.rem(rows, n) < live)


def put_sums(stat, one, two):
    stat[0:1, :] = jnp.sum(one, axis=0, keepdims=True)
    stat[1:2, :] = jnp.sum(two, axis=0, keepdims=True)


def lay_taps(sz, value, strip, taps):
    n = sz.images
    width = strip.shape[1]
    strip[0 : 9 * n, :] = jnp.zeros((9 * n, width), F32)
    strip[65 * n : 74 * n, :] = jnp.zeros((9 * n, width), F32)
    strip[9 * n : 65 * n, :] = value
    for b in range(3):
        taps[b] = strip[b * n : b * n + 72 * n, :].astype(BF16)


def first_lead_body(meta, x, weight, low, high):
    value = jnp.dot(x[0], weight[...], preferred_element_type=F32).astype(BF16)
    half = low.shape[1]
    low[...] = value[:, :half]
    high[...] = value[:, half:]


def first_part_body(meta, x, weight, out):
    out[0] = jnp.dot(x[0], weight[...], preferred_element_type=F32).astype(BF16)


def first_body(sz, meta, f, b, own, pre, stat, native):
    split_lanes(f[...].astype(F32) + b[...].astype(F32) + own[0].astype(F32), native)
    to_padded(sz, native, pre)
    value = pre[...]
    kept = jnp.where(row_mask(sz, value.shape[1], meta[sz.live]), value, 0.0)
    put_sums(stat, kept, kept * kept)


def conv_body(
    sz, meta, pre, stat, params, weight, out, raw, stat_out, acted, strip, taps, total, native
):
    step = pl.program_id(0)
    n = sz.images
    width = pre.shape[1]

    @pl.when(step == 0)
    def _():
        average, inv = moments(stat[...], sz.own_count(meta))
        z = params[0:1] * ((pre[...] - average) * inv) + params[1:2]
        act = jnp.where(row_mask(sz, width, None), z * sigmoid(z), 0.0)
        acted[...] = act.astype(BF16)
        lay_taps(sz, act, strip, taps)
        total[...] = jnp.zeros_like(total)

    at = pl.multiple_of(step * 8 * n, 8 * n)
    for b in range(3):
        total[...] += jnp.dot(
            taps[b, pl.ds(at, sz.padded), :], weight[0, b], preferred_element_type=F32
        )

    @pl.when(step == 2)
    def _():
        value = jnp.where(row_mask(sz, width, None), total[...], 0.0)
        out[...] = value
        to_native(sz, total, native, raw)
        kept = jnp.where(row_mask(sz, width, meta[sz.live]), value, 0.0)
        put_sums(stat_out, kept, kept * kept)


def pick(sz, stat, batch):
    found = stat[0:2]
    for m in range(1, sz.micro):
        found = jnp.where(batch == m, stat[2 * m : 2 * m + 2], found)
    return found


def pick_count(sz, meta, batch):
    count = meta[sz.count]
    for m in range(1, sz.micro):
        count = jnp.where(batch == m, meta[sz.count + m], count)
    return count.astype(F32)


def add_sums(sz, stat, batch, one, two):
    sums = jnp.concatenate(
        [jnp.sum(one, axis=0, keepdims=True), jnp.sum(two, axis=0, keepdims=True)], axis=0
    )
    for m in range(sz.micro):
        stat[2 * m : 2 * m + 2, :] += jnp.where(batch == m, sums, 0.0)


def stage_piece(pieces, place, step):
    for k, piece in enumerate(pieces):

        @pl.when(step == k)
        def _(piece=piece):
            if len(piece) == 1:
                place[...] = piece[0][...]
            else:
                half = piece[0].shape[1]
                place[:, :half] = piece[0][...]
                place[:, half:] = piece[1][...]


def split_refs(layout, refs):
    pieces, at = [], 0
    for many in layout:
        pieces.append(refs[at : at + many])
        at += many
    return pieces, refs[at:]


def expand_body(sz, layout, offset, meta, *refs):
    pieces, rest = split_refs(layout, refs)
    stat, params, weight, act, pre, stat_out, place = rest
    step = pl.program_id(0)
    stage_piece(pieces, place, step)
    k = meta[sz.arrive + offset + step]
    batch = meta[sz.batch + k]
    average, inv = moments(pick(sz, stat[...], batch), pick_count(sz, meta, batch))
    z = params[2:3] * ((place[...].astype(F32) - average) * inv) + params[3:4]
    acted = (z * sigmoid(z)).astype(BF16)
    act[0] = acted
    value = jnp.dot(acted, weight[...], preferred_element_type=F32)
    pre[0] = value

    @pl.when(step == 0)
    def _():
        stat_out[...] = jnp.zeros_like(stat_out)

    rows = lax.broadcasted_iota(jnp.int32, value.shape, 0)
    kept = jnp.where(rows < PIXELS * meta[sz.live + k], value, 0.0)
    add_sums(sz, stat_out, batch, kept, kept * kept)


def out_body(sz, meta, pre, stat, params, x, cot, out, grad, stat_out):
    step = pl.program_id(0)
    batch = meta[sz.batch + step]
    average, inv = moments(pick(sz, stat[...], batch), pick_count(sz, meta, batch))
    normed = (pre[0] - average) * inv
    summed = params[0:1] * normed + params[1:2] + x[0].astype(F32)
    sigma = sigmoid(summed)
    rows = lax.broadcasted_iota(jnp.int32, summed.shape, 0)
    live = rows < PIXELS * meta[sz.live + step]
    out[0] = jnp.where(live, summed * sigma, 0.0)
    upstream = jnp.where(
        live, cot[0].astype(F32) * (sigma * (1.0 + summed * (1.0 - sigma))), 0.0
    )
    grad[0] = upstream

    @pl.when(step == 0)
    def _():
        stat_out[...] = jnp.zeros_like(stat_out)

    add_sums(sz, stat_out, batch, upstream, upstream * normed)


def shrink_body(sz, lead, meta, pre, stat, params, grad, sums, weight, back, *parts):
    if lead:
        k = sz.half
    else:
        step = pl.program_id(0)
        k = jnp.where(step < sz.half, step, step + 1)
    batch = meta[sz.batch + k]
    count = pick_count(sz, meta, batch)
    average, inv = moments(pick(sz, stat[...], batch), count)
    both = pick(sz, sums[...], batch)
    normed = (pre[0] - average) * inv
    rows = lax.broadcasted_iota(jnp.int32, normed.shape, 0)
    live = rows < PIXELS * meta[sz.live + k]
    value = params[0:1] * inv * (grad[0] - (both[0:1] + normed * both[1:2]) / count)
    value = jnp.where(live, value, 0.0).astype(BF16)
    back[0] = value
    part = lax.dot_general(
        value, weight[...], (((1,), (1,)), ((), ())), preferred_element_type=F32
    ).astype(BF16)
    if lead:
        half = part.shape[1] // 2
        parts[0][...] = part[:, :half]
        parts[1][...] = part[:, half:]
    else:
        parts[0][0] = part


def middle_up_body(sz, meta, f, b, own, pre, stat, params, up, stat_out, native, padded):
    split_lanes(f[...].astype(F32) + b[...].astype(F32) + own[0].astype(F32), native)
    to_padded(sz, native, padded)
    average, inv = moments(stat[...], sz.own_count(meta))
    normed = (pre[...] - average) * inv
    z = params[2:3] * normed + params[3:4]
    value = jnp.where(
        row_mask(sz, pre.shape[1], meta[sz.live]), padded[...] * silu_slope(z), 0.0
    )
    up[...] = value
    put_sums(stat_out, value, value * normed)


def conv_back_body(
    sz,
    meta,
    up,
    sums,
    pre_two,
    stat_two,
    pre_one,
    stat_one,
    params,
    weight,
    stay,
    send,
    up_one,
    stat_out,
    strip,
    taps,
    total,
):
    step = pl.program_id(0)
    n = sz.images
    width = up.shape[1]

    @pl.when(step == 0)
    def _():
        count = sz.own_count(meta)
        average, inv = moments(stat_two[...], count)
        normed = (pre_two[...] - average) * inv
        value = params[2:3] * inv * (up[...] - (sums[0:1] + normed * sums[1:2]) / count)
        value = jnp.where(row_mask(sz, width, meta[sz.live]), value, 0.0)
        half, _, lanes = stay.shape
        for p in range(2 * half):
            for plane in range(2 * half):

                @pl.when(meta[sz.planes + p] == plane)
                def _(p=p, plane=plane):
                    out = stay if p < half else send
                    out[p % half] = value[:, plane * lanes : (plane + 1) * lanes].astype(BF16)

        lay_taps(sz, value, strip, taps)
        total[...] = jnp.zeros_like(total)

    at = pl.multiple_of((2 - step) * 8 * n, 8 * n)
    for b in range(3):
        total[...] += lax.dot_general(
            taps[2 - b, pl.ds(at, sz.padded), :],
            weight[0, b],
            (((1,), (1,)), ((), ())),
            preferred_element_type=F32,
        )

    @pl.when(step == 2)
    def _():
        average, inv = moments(stat_one[...], sz.own_count(meta))
        normed = (pre_one[...] - average) * inv
        z = params[0:1] * normed + params[1:2]
        value = jnp.where(
            row_mask(sz, width, meta[sz.live]), total[...] * silu_slope(z), 0.0
        )
        up_one[...] = value
        put_sums(stat_out, value, value * normed)


def first_back_body(sz, meta, up, sums, pre, stat, params, back, padded, native):
    count = sz.own_count(meta)
    average, inv = moments(stat[...], count)
    normed = (pre[...] - average) * inv
    value = params[0:1] * inv * (up[...] - (sums[0:1] + normed * sums[1:2]) / count)
    padded[...] = jnp.where(row_mask(sz, pre.shape[1], meta[sz.live]), value, 0.0)
    to_native(sz, padded, native, back)


def input_body(sz, layout, more, meta, *refs):
    pieces, rest = split_refs(layout, refs)
    if more:
        grad, x, weight, had, out, grad_weight, place, total = rest
    else:
        grad, x, weight, out, grad_weight, place, total = rest
    step = pl.program_id(0)
    stage_piece(pieces, place, step)
    value = place[...]
    out[0] = grad[0] + lax.dot_general(
        value, weight[...], (((1,), (1,)), ((), ())), preferred_element_type=F32
    )

    @pl.when(step == 0)
    def _():
        total[...] = had[...] if more else jnp.zeros_like(total)

    total[...] += lax.dot_general(
        x[0], value, (((0,), (0,)), ((), ())), preferred_element_type=F32
    )

    @pl.when(step == len(layout) - 1)
    def _():
        grad_weight[...] = total[...].astype(grad_weight.dtype)


def middle_grad_body(sz, dp, meta, acts, backs, out, strip, taps, total):
    source = pl.program_id(0)
    n = sz.images
    lay_taps(sz, backs[0, 0].astype(F32), strip, taps)
    shifted = [
        taps[2 - b, (2 - a) * 8 * n : (2 - a) * 8 * n + sz.padded, :]
        for a in range(3)
        for b in range(3)
    ]

    @pl.when(source == 0)
    def _():
        total[...] = jnp.zeros_like(total)

    total[...] += lax.dot_general(
        acts[0],
        jnp.concatenate(shifted, axis=1),
        (((0,), (0,)), ((), ())),
        preferred_element_type=F32,
    )

    @pl.when(source == dp - 1)
    def _():
        depth, lanes = out.shape[1] // TAPS, out.shape[2]
        for k in range(sz.chunks):
            at = pl.multiple_of(meta[k] * depth, depth)
            for tap in range(TAPS):
                out[k, tap * depth : (tap + 1) * depth, :] = total[
                    pl.ds(at, depth), tap * lanes : (tap + 1) * lanes
                ].astype(BF16)


def assemble_body(sz, half, depth, meta, *refs):
    stacks, out = refs[:-1], refs[-1]
    early = sz.chunks - 3

    def fill(plane):
        for q, k in enumerate(sz.arrival):
            pieces = stacks[plane if q < early else half + plane]
            at = pl.multiple_of(meta[k] * depth, depth)
            for tap in range(TAPS):
                value = pieces[0, q if q < early else q - early, tap * depth : (tap + 1) * depth, :]
                if len(out.shape) == 3:
                    out[tap, pl.ds(at, depth), :] = value
                else:
                    out[0, tap, pl.ds(at, depth), :] = value

    for p in range(2 * half):

        @pl.when(pl.program_id(0) == p)
        def _(p=p):
            fill(p if p < half else half + p)


def prepare_body(weights, last, params, out):
    many, lanes = weights.shape
    out[:many, :] = weights[...].astype(BF16)
    depth = last.shape[0]
    for b in range(last.shape[1] // lanes):
        out[many + b * depth : many + (b + 1) * depth, :] = last[
            :, b * lanes : (b + 1) * lanes
        ].astype(BF16)
    value = params[...]
    count, width = value.shape
    one = value.astype(BF16)
    left = value - one.astype(F32)
    two = left.astype(BF16)
    three = (left - two.astype(F32)).astype(BF16)
    rest = jnp.zeros((16 - 3 * count, width), F32)
    rows = jnp.concatenate([part.astype(F32) for part in (one, two, three)] + [rest], axis=0)
    if width < lanes:
        rows = jnp.concatenate([rows, jnp.zeros((16, lanes - width), F32)], axis=1)
    out[out.shape[0] - 16 :, :] = rows.astype(BF16)


def last_assemble_body(meta, blocks, out):
    lanes = blocks.shape[3]
    for b in range(blocks.shape[1]):
        out[:, b * lanes : (b + 1) * lanes] = blocks[0, b]


def last_grad_body(sz, meta, act, back, out, total):
    step = pl.program_id(0)

    @pl.when(step == 0)
    def _():
        total[...] = jnp.zeros_like(total)

    total[...] += lax.dot_general(
        act[0], back[0], (((0,), (0,)), ((), ())), preferred_element_type=F32
    )

    @pl.when(step == sz.chunks - 1)
    def _():
        depth = out.shape[1]
        for k in range(sz.chunks):
            at = pl.multiple_of(meta[k] * depth, depth)
            out[k] = total[pl.ds(at, depth), :].astype(BF16)


def pieces_in(sz, pieces):
    ins, layout = [], []
    for piece in pieces:
        parts = piece if isinstance(piece, tuple) else (piece,)
        layout.append(len(parts))
        ins += [whole(p) for p in parts]
    return ins, layout


def local(
    dp,
    chan,
    inputs,
    cotangent,
    w_first,
    first_m,
    first_v,
    w_middle,
    middle_m,
    middle_v,
    w_last,
    last_m,
    last_v,
    mid_params,
    mid_m,
    mid_v,
    out_params,
    out_m,
    out_v,
    image_counts,
):
    ring = Ring(chan)
    d = lax.axis_index("dp")
    c = lax.axis_index("chan")
    micro, pixels, deep = inputs.shape
    images = micro * pixels // PIXELS // chan
    sz = Sizes(chan, micro, images)
    rows, padded = sz.rows, sz.padded
    per_batch = chan // micro
    depth, lanes = w_middle.shape[2], w_middle.shape[3]
    mid = depth * chan
    half = dp // 2
    last_blocks = w_last.shape[1] // lanes
    own_blocks = deep // lanes
    ratio = last_blocks // own_blocks

    meta = make_meta(sz, ring, dp, ratio, image_counts)
    at = meta[:chan]

    dp_bits = bits_below(dp)
    wide_bits = dp_bits[1:]
    first = w_first.astype(BF16)
    for bit in dp_bits:
        other = swap(first, "dp", bit, dp)
        first = jnp.where(
            (d & bit) == 0,
            jnp.concatenate([first, other], axis=1),
            jnp.concatenate([other, first], axis=1),
        )
    many = TAPS * depth
    tail_at = many + last_blocks * depth
    (payload,) = pl.pallas_call(
        prepare_body,
        in_specs=[pl.BlockSpec(memory_space=pltpu.VMEM)] * 3,
        out_specs=[pl.BlockSpec(memory_space=pltpu.VMEM)],
        out_shape=[jax.ShapeDtypeStruct((tail_at + 16, lanes), BF16)],
    )(w_middle.reshape(many, lanes), w_last, mid_params)
    mids = Gather(ring, payload, 0)
    while mids.count < chan // 2:
        mids.step()

    x = inputs.reshape(chan, rows, deep)
    cot = cotangent.reshape(chan, rows, deep)

    def at_place(k, meta):
        return (meta[k], 0, 0)

    def in_order(k, meta):
        return (k, 0, 0)

    opposite = chan // 2

    def skipping(k, meta):
        return (jnp.where(k < opposite, k, k + 1), 0, 0)

    def skipping_at(k, meta):
        return (meta[jnp.where(k < opposite, k, k + 1)], 0, 0)

    low, high = run(
        first_lead_body,
        meta,
        (1,),
        [(x, (1, rows, deep), lambda k, meta: (meta[opposite], 0, 0)), whole(first)],
        [whole_out((rows, mid // 2), BF16), whole_out((rows, mid // 2), BF16)],
    )
    (parts,) = run(
        first_part_body,
        meta,
        (chan - 1,),
        [(x, (1, rows, deep), skipping_at), whole(first)],
        [((chan, rows, mid), BF16, (1, rows, mid), skipping)],
        cost=(2 * chan * rows * deep * mid, 2 * chan * rows * (deep + mid)),
    )
    sums = Scatter(ring, low, high, lambda k: parts[k], 1)
    while sums.count < opposite:
        sums.step()
    f, b = sums.f, sums.b

    came = [jnp.concatenate(p, axis=0) if isinstance(p, tuple) else p for p in mids.pieces]
    tails = jnp.stack([p[many:] for p in came])
    near, far = [], []
    for group in (sz.arrival[: chan - 3], sz.arrival[chan - 3 :]):
        stack = jnp.stack([came[k][:many] for k in group])[None]
        planes = [stack]
        for bit in wide_bits:
            planes += [swap(p, "dp", bit, dp) for p in planes]
        near.append(planes)
        far.append([swap(p, "dp", 1, dp) for p in planes])
    near = [near[g][q] for g in range(2) for q in range(half)]
    far = [far[g][q] for g in range(2) for q in range(half)]
    if lanes % 128 == 0:
        placed = ((TAPS, mid, mid), BF16, (TAPS, mid, lanes), lambda p, meta: (0, 0, meta[sz.planes + p]))
    else:
        placed = (
            (dp, TAPS, mid, lanes),
            BF16,
            (1, TAPS, mid, lanes),
            lambda p, meta: (meta[sz.planes + p], 0, 0, 0),
        )
    (middle,) = run(
        functools.partial(assemble_body, sz, half, depth),
        meta,
        (dp,),
        [whole(p) for p in near + far],
        [placed],
    )
    here = (at[None, :] == jnp.arange(chan)[:, None])[:, :, None, None]
    tail = tails[:, last_blocks * depth :, :depth].astype(F32)
    tail = (tail[:, 8:12] + tail[:, 4:8]) + tail[:, 0:4]
    params = jnp.sum(jnp.where(here, tail[None], 0.0), axis=1)
    params = params.transpose(1, 0, 2).reshape(4, mid)
    if lanes % 128 != 0:
        middle = middle.transpose(1, 2, 0, 3)
    middle = middle.reshape(3, 3, mid, mid)
    lasts = tails[:, : last_blocks * depth].reshape(chan, ratio, own_blocks, depth, lanes)
    own_last = lax.dynamic_index_in_dim(lasts, c % ratio, axis=1, keepdims=False)
    found = jnp.where(d == c // ratio, own_last, jnp.zeros_like(own_last))
    for shift in range(1, dp):
        moves = [
            ((k // ratio) * chan + k, ((k // ratio) ^ shift) * chan + k) for k in range(chan)
        ]
        found = found + lax.ppermute(own_last, ("dp", "chan"), moves)
    (last,) = run(
        last_assemble_body,
        meta,
        (chan,),
        [(found, (1, own_blocks, depth, lanes), lambda k, meta: (k, 0, 0, 0))],
        [((mid, deep), BF16, (depth, deep), lambda k, meta: (meta[k], 0))],
    )

    def head(stack):
        return (stack, (1,) + stack.shape[1:], lambda *_: (0, 0, 0))

    stat_bits = [k for k in bits_below(chan) if k < per_batch]

    def total_rows(stat):
        return sum_over(sum_over(stat, "dp", dp_bits, dp), "chan", stat_bits, chan)

    def all_batches(stat):
        for bit in bits_below(chan):
            if bit >= per_batch:
                other = swap(stat, "chan", bit, chan)
                stat = jnp.where(
                    (c & bit) == 0,
                    jnp.concatenate([stat, other], axis=0),
                    jnp.concatenate([other, stat], axis=0),
                )
        return stat

    pre_one, stat_one = run(
        functools.partial(first_body, sz),
        meta,
        (1,),
        [whole(f), whole(b), head(parts)],
        [whole_out((padded, mid), F32), whole_out((2, mid), F32)],
        [pltpu.VMEM((mid // 128, rows, 128), F32)],
        vmem=VMEM,
        cost=(10 * padded * mid, 10 * padded * mid),
    )
    stat_one = total_rows(stat_one)

    tap_block = (1, 3, mid, mid)
    conv_flops = 2 * TAPS * padded * mid * mid
    conv_bytes = 2 * TAPS * mid * mid + 16 * padded * mid
    pre_two, raw, stat_two, acted = run(
        functools.partial(conv_body, sz),
        meta,
        (3,),
        [
            whole(pre_one),
            whole(stat_one),
            whole(params),
            (middle, tap_block, lambda s, meta: (s, 0, 0, 0)),
        ],
        [
            whole_out((padded, mid), F32),
            whole_out((rows, mid), BF16),
            whole_out((2, mid), F32),
            whole_out((padded, mid), BF16),
        ],
        [
            pltpu.VMEM((74 * images, mid), F32),
            pltpu.VMEM((3, 72 * images, mid), BF16),
            pltpu.VMEM((padded, mid), F32),
            pltpu.VMEM((mid // 128, rows, 128), F32),
        ],
        vmem=VMEM,
        cost=(conv_flops, conv_bytes),
    )
    gather = Gather(ring, raw, 1)
    gather.step()
    stat_two = sum_over(stat_two, "dp", dp_bits, dp)
    gather.step(stat_two)
    stat_two = sum_over(stat_two, "chan", stat_bits, chan)
    if gather.count < opposite - 1:
        gather.step(stat_two)
    stats_two = all_batches(stat_two)
    while gather.count < opposite - 1:
        gather.step()
    gather.step(stats_two)
    pieces = gather.pieces
    order = [1] + wide_bits[::-1]
    acts = acted[None]
    for bit in order:
        acts = jnp.concatenate([acts, swap(acts, "dp", bit, dp)], axis=0)

    def expand(start, steps, into):
        ins, layout = pieces_in(sz, [pieces[k] for k in sz.arrival[start : start + steps]])

        def arrived(k, meta):
            return (meta[sz.arrive + start + k], 0, 0)

        return run(
            functools.partial(expand_body, sz, layout, start),
            meta,
            (steps,),
            ins + [whole(stats_two), whole(params), whole(last)],
            [
                ((chan, rows, mid), BF16, (1, rows, mid), arrived),
                ((chan, rows, deep), F32, (1, rows, deep), arrived),
                whole_out((2 * micro, deep), F32),
            ],
            [pltpu.VMEM((rows, mid), BF16)],
            vmem=VMEM,
            cost=(2 * steps * rows * deep * mid, steps * rows * (4 * mid + 4 * deep)),
            into=into,
        )

    early = chan - 3
    act, pre_three, stat_early = expand(0, early, [])
    act, pre_three, stat_late = expand(early, 3, [act, pre_three])
    stat_three = stat_early + stat_late
    stat_three = sum_over(stat_three, "dp", bits_below(dp), dp)
    block_out, grad_summed, sums_three = run(
        functools.partial(out_body, sz),
        meta,
        (chan,),
        [
            (pre_three, (1, rows, deep), in_order),
            whole(stat_three),
            whole(out_params),
            (x, (1, rows, deep), at_place),
            (cot, (1, rows, deep), at_place),
        ],
        [
            ((chan, rows, deep), F32, (1, rows, deep), at_place),
            ((chan, rows, deep), F32, (1, rows, deep), in_order),
            whole_out((2 * micro, deep), F32),
        ],
        vmem=VMEM,
        cost=(20 * chan * rows * deep, 16 * chan * rows * deep),
    )
    sums_three = sum_over(sums_three, "dp", bits_below(dp), dp)

    def shrink(steps, place, into, lead):
        if lead:
            made = [whole_out((rows, mid // 2), BF16), whole_out((rows, mid // 2), BF16)]
        else:
            made = [((chan, rows, mid), BF16, (1, rows, mid), place)]
        return run(
            functools.partial(shrink_body, sz, lead),
            meta,
            (steps,),
            [
                (pre_three, (1, rows, deep), place),
                whole(stat_three),
                whole(out_params),
                (grad_summed, (1, rows, deep), place),
                whole(sums_three),
                whole(last),
            ],
            [((chan, rows, deep), BF16, (1, rows, deep), place)] + made,
            vmem=VMEM,
            cost=(2 * steps * rows * deep * mid, steps * rows * (2 * mid + 10 * deep)),
            into=into,
        )

    back_last, low, high = shrink(1, lambda k, meta: (opposite, 0, 0), [], True)
    back_last, back_parts = shrink(chan - 1, skipping, [back_last], False)
    sums = Scatter(ring, low, high, lambda k: back_parts[k], 1)
    while sums.count < opposite:
        sums.step()
    f, b = sums.f, sums.b
    (grad_last,) = run(
        functools.partial(last_grad_body, sz),
        meta,
        (chan,),
        [(act, (1, rows, mid), in_order), (back_last, (1, rows, deep), in_order)],
        [whole_out((chan, depth, deep), BF16)],
        [pltpu.VMEM((mid, deep), F32)],
        cost=(2 * chan * rows * deep * mid, 2 * chan * rows * (mid + deep)),
    )
    for bit in dp_bits:
        grad_last = add16(grad_last, swap(grad_last, "dp", bit, dp))
    held = [
        jnp.where(c % ratio == r, grad_last, jnp.zeros_like(grad_last)) for r in range(ratio)
    ]
    held = jnp.concatenate(held, axis=2)
    held = jnp.where(d == c // ratio, held, jnp.zeros_like(held))
    cut = held.shape[2] // 2
    last_sums = Scatter(
        ring, held[opposite, :, :cut], held[opposite, :, cut:], lambda k: held[k], 1
    )
    while last_sums.count < opposite:
        last_sums.step()
    owned_last = held[0].astype(F32) + last_sums.f.astype(F32) + last_sums.b.astype(F32)

    up_two, sums_two = run(
        functools.partial(middle_up_body, sz),
        meta,
        (1,),
        [
            whole(f),
            whole(b),
            head(back_parts),
            whole(pre_two),
            whole(stat_two),
            whole(params),
        ],
        [whole_out((padded, mid), F32), whole_out((2, mid), F32)],
        [pltpu.VMEM((mid // 128, rows, 128), F32), pltpu.VMEM((padded, mid), F32)],
        vmem=VMEM,
        cost=(20 * padded * mid, 14 * padded * mid),
    )
    sums_two = total_rows(sums_two)
    stay, send, up_one, sums_one = run(
        functools.partial(conv_back_body, sz),
        meta,
        (3,),
        [
            whole(up_two),
            whole(sums_two),
            whole(pre_two),
            whole(stat_two),
            whole(pre_one),
            whole(stat_one),
            whole(params),
            (middle, tap_block, lambda s, meta: (s, 0, 0, 0)),
        ],
        [
            whole_out((half, padded, lanes), BF16),
            whole_out((half, padded, lanes), BF16),
            whole_out((padded, mid), F32),
            whole_out((2, mid), F32),
        ],
        [
            pltpu.VMEM((74 * images, mid), F32),
            pltpu.VMEM((3, 72 * images, mid), BF16),
            pltpu.VMEM((padded, mid), F32),
        ],
        vmem=VMEM,
        cost=(conv_flops, conv_bytes),
    )

    sums_one = total_rows(sums_one)
    (back_one,) = run(
        functools.partial(first_back_body, sz),
        meta,
        (1,),
        [whole(up_one), whole(sums_one), whole(pre_one), whole(stat_one), whole(params)],
        [whole_out((rows, mid), BF16)],
        [pltpu.VMEM((padded, mid), F32), pltpu.VMEM((mid // 128, rows, 128), F32)],
        cost=(10 * padded * mid, 10 * padded * mid),
    )
    gather = Gather(ring, back_one, 1)
    while gather.count < opposite:
        gather.step()
    pieces = gather.pieces

    backs = jnp.stack([stay, swap(send, "dp", 1, dp)])
    for bit in wide_bits[::-1]:
        cut = backs.shape[1] // 2
        backs = jnp.concatenate(
            [backs[:, :cut], swap(backs[:, cut:], "dp", bit, dp)], axis=0
        )
    (grad_middle,) = run(
        functools.partial(middle_grad_body, sz, dp),
        meta,
        (dp,),
        [
            (acts, (1, padded, mid), lambda r, meta: (r, 0, 0)),
            (backs, (1, 1, padded, lanes), lambda r, meta: (r, 0, 0, 0)),
        ],
        [whole_out((chan, TAPS * depth, lanes), BF16)],
        [
            pltpu.VMEM((74 * images, lanes), F32),
            pltpu.VMEM((3, 72 * images, lanes), BF16),
            pltpu.VMEM((mid, TAPS * lanes), F32),
        ],
        cost=(conv_flops, conv_bytes),
        after=[back_one],
    )
    cut = TAPS * depth // 2
    middle_sums = Scatter(
        ring,
        grad_middle[opposite, :cut],
        grad_middle[opposite, cut:],
        lambda k: grad_middle[k],
        0,
    )
    middle_steps = [middle_sums.f]
    while middle_sums.count < opposite:
        middle_sums.step()
        middle_steps.append(middle_sums.f)
    owned_middle = (
        grad_middle[0].astype(F32) + middle_sums.f.astype(F32) + middle_sums.b.astype(F32)
    ).reshape(3, 3, depth, lanes)

    def input_back(start, steps, had, into, after):
        ins, layout = pieces_in(sz, [pieces[k] for k in sz.arrival[start : start + steps]])
        done = start + steps == chan

        def arrived(k, meta):
            return (meta[sz.arrive + start + k], 0, 0)

        def arrived_at(k, meta):
            return (meta[meta[sz.arrive + start + k]], 0, 0)

        return run(
            functools.partial(input_body, sz, layout, bool(had)),
            meta,
            (steps,),
            ins
            + [
                (grad_summed, (1, rows, deep), arrived),
                (x, (1, rows, deep), arrived_at),
                whole(first),
            ]
            + [whole(h) for h in had],
            [
                ((chan, rows, deep), F32, (1, rows, deep), arrived_at),
                whole_out((deep, mid), BF16 if done else F32),
            ],
            [pltpu.VMEM((rows, mid), BF16), pltpu.VMEM((deep, mid), F32)],
            vmem=VMEM,
            cost=(4 * steps * rows * deep * mid, steps * rows * (2 * mid + 10 * deep)),
            into=into,
            after=after,
        )

    input_grad, grad_early = input_back(0, early, [], [], middle_steps[1:2])
    input_grad, grad_first = input_back(early, 3, [grad_early], [input_grad], middle_steps[2:3])
    owned_first = scatter_columns(grad_first, d, dp)

    sums_first, sums_middle = all_batches(sums_one), all_batches(sums_two)

    def over_batches(stat, row):
        total = stat[row]
        for m in range(1, micro):
            total = total + stat[2 * m + row]
        return total

    grad_mid = jnp.stack(
        [
            over_batches(sums_first, 1),
            over_batches(sums_first, 0),
            over_batches(sums_middle, 1),
            over_batches(sums_middle, 0),
        ]
    )
    grad_mid = lax.dynamic_slice_in_dim(grad_mid, c * depth, depth, axis=1)
    grad_out = jnp.stack([over_batches(sums_three, 1), over_batches(sums_three, 0)])

    return (
        block_out.reshape(inputs.shape),
        input_grad.reshape(inputs.shape),
        *adamw(w_first, owned_first, first_m, first_v, rate_first),
        *adamw(w_middle, owned_middle, middle_m, middle_v, rate_middle),
        *adamw(w_last, owned_last, last_m, last_v, rate_last),
        *adamw(mid_params, grad_mid, mid_m, mid_v, rate_norm),
        *adamw(out_params, grad_out, out_m, out_v, rate_norm),
    )


def scatter_columns(grad, d, dp):
    blocks = grad.reshape(grad.shape[0], dp, grad.shape[1] // dp)
    kept = [blocks[:, p] for p in range(dp)]
    for bit in bits_below(dp):
        kept = [
            jnp.where((d & bit) == 0, kept[q], kept[q ^ bit]) for q in range(len(kept))
        ]
    todo = {q: kept[q] for q in range(dp)}
    for bit in [1] + bits_below(dp)[:0:-1]:
        send = sorted(q for q in todo if q & bit)
        stay = sorted(q for q in todo if not q & bit)
        got = swap(jnp.stack([todo[q] for q in send]), "dp", bit, dp)
        todo = {
            q: todo[q].astype(F32) + got[send.index(q | bit)].astype(F32) for q in stay
        }
        if len(todo) > 1:
            todo = {q: v.astype(BF16) for q, v in todo.items()}
    return todo[0]


def solution(mesh):
    rows = P(None, "dp", "chan")
    flat = P("chan", "dp")
    square = P(None, None, "chan", "dp")
    vector = P(None, "chan")
    state = (flat,) * 3 + (square,) * 3 + (flat,) * 3 + (vector,) * 6
    return jax.shard_map(
        functools.partial(local, mesh.shape["dp"], mesh.shape["chan"]),
        mesh=mesh,
        in_specs=(rows, rows) + state + (P(),),
        out_specs=(rows, rows) + state,
        check_vma=False,
    )
```

```python
import functools

import jax
import jax.numpy as jnp
import numpy as np
from jax import lax
from jax.experimental import pallas as pl
from jax.experimental.pallas import tpu as pltpu
from jax.sharding import PartitionSpec as P

STEPS = 5
SIDE = 7
PIXELS = SIDE * SIDE
TAPS = 9
VMEM = 24
F32 = jnp.float32
BF16 = jnp.bfloat16

norm_eps = 1e-05
adam_eps = 1e-08
adam_beta = 0.5
decay_rate = 0.05
rate_first = 0.02
rate_middle = 0.015
rate_last = 0.04
rate_norm = 0.25


def sigmoid(value):
    return 0.5 * jnp.tanh(0.5 * value) + 0.5


def silu_slope(value):
    sigma = sigmoid(value)
    return sigma * (1.0 + value * (1.0 - sigma))


def moments(stat, count):
    average = stat[0:1] / count
    variance = stat[1:2] / count - average * average
    return average, lax.rsqrt(variance + norm_eps)


def adamw(weight, gradient, moment_one, moment_two, step_rate):
    one_new = adam_beta * moment_one + (1.0 - adam_beta) * gradient
    two_new = adam_beta * moment_two + (1.0 - adam_beta) * gradient * gradient
    correct = 1.0 - adam_beta**STEPS
    weight_new = weight - step_rate * (
        one_new / correct / (jnp.sqrt(two_new / correct) + adam_eps) + decay_rate * weight
    )
    return (weight_new, one_new, two_new)


def ring_of(size):
    across = max(size // 4, 1)
    along = size // across
    order = [(z, 0) for z in range(along)]
    outward = True
    for z in reversed(range(along)):
        steps = list(range(1, across))
        order += [(z, x) for x in (steps if outward else steps[::-1])]
        outward = not outward
    return [z * across + x for z, x in order]


class Ring:
    def __init__(self, size):
        self.size = size
        self.order = ring_of(size)
        ahead = [(self.order[i], self.order[(i + 1) % size]) for i in range(size)]
        self.ahead = ahead
        self.back = [(b, a) for a, b in ahead]
        place = np.argsort(np.array(self.order))
        self.table = np.array(
            [[self.order[(place[c] + k) % size] for k in range(size)] for c in range(size)],
            np.int32,
        )

    def fw(self, x):
        return lax.ppermute(x, "chan", self.ahead)

    def bw(self, x):
        return lax.ppermute(x, "chan", self.back)


def tie(x, other):
    first = lax.slice(other, (0,) * other.ndim, (1,) * other.ndim).reshape(())
    return jnp.where(first > -3e38, x, jnp.zeros_like(x))


def beside(x, other):
    return jnp.where(other > -3e38, x, jnp.zeros_like(x))


class Gather:
    def __init__(self, ring, x, axis):
        self.ring, self.axis, self.half = ring, axis, x.shape[axis] // 2
        self.pieces = [x] + [None] * (ring.size - 1)
        self.count = 0

    def step(self, other=None):
        ring, size = self.ring, self.ring.size
        a, b = self.pieces[(size - self.count) % size], self.pieces[self.count]
        if other is not None:
            a, b = tie(a, other), tie(b, other)
        self.count += 1
        if self.count < size // 2:
            got = [ring.fw(a), ring.bw(b)]
            self.pieces[size - self.count], self.pieces[self.count] = got
        else:
            got = [
                ring.fw(lax.slice_in_dim(a, 0, self.half, axis=self.axis)),
                ring.bw(lax.slice_in_dim(b, self.half, b.shape[self.axis], axis=self.axis)),
            ]
            self.pieces[size // 2] = tuple(got)
        return got


class Scatter:
    def __init__(self, ring, low, high, part, axis):
        self.ring, self.part, self.axis = ring, part, axis
        self.f, self.b = ring.fw(low), ring.bw(high)
        self.count = 1

    def step(self):
        size, axis = self.ring.size, self.axis
        k = size // 2 - self.count
        left, right = self.part(k), self.part(size - k)
        if self.count == 1:
            width = left.shape[axis]
            half = width // 2
            f = jnp.concatenate(
                [
                    beside(add16(lax.slice_in_dim(left, 0, half, axis=axis), self.f), self.b),
                    lax.slice_in_dim(left, half, width, axis=axis),
                ],
                axis,
            )
            b = jnp.concatenate(
                [
                    lax.slice_in_dim(right, 0, half, axis=axis),
                    beside(add16(lax.slice_in_dim(right, half, width, axis=axis), self.b), self.f),
                ],
                axis,
            )
        else:
            f = beside(add16(left, self.f), self.b)
            b = beside(add16(right, self.b), self.f)
        self.count += 1
        self.f, self.b = self.ring.fw(f), self.ring.bw(b)


def add16(one, two):
    return (one.astype(F32) + two.astype(F32)).astype(BF16)


def swap(x, axis, bit, size):
    return lax.ppermute(x, axis, [(i, i ^ bit) for i in range(size)])


def bits_below(size):
    return [1 << k for k in range(size.bit_length() - 1)]


def sum_over(x, axis, bits, size):
    for bit in bits:
        x = x + swap(x, axis, bit, size)
    return x


def run(body, meta, grid, ins, outs, scratch=(), vmem=VMEM, cost=None, after=(), into=()):
    extra = list(into) + list(after)
    first, last = len(ins), len(ins) + len(extra)

    def kernel(meta, *refs):
        body(meta, *refs[:first], *refs[last:])

    return pl.pallas_call(
        kernel if extra else body,
        grid_spec=pltpu.PrefetchScalarGridSpec(
            num_scalar_prefetch=1,
            grid=grid,
            in_specs=[pl.BlockSpec(b, m) for _, b, m in ins]
            + [pl.BlockSpec(memory_space=pl.ANY)] * len(extra),
            out_specs=[pl.BlockSpec(b, m) for _, _, b, m in outs],
            scratch_shapes=list(scratch),
        ),
        out_shape=[jax.ShapeDtypeStruct(s, d) for s, d, _, _ in outs],
        compiler_params=pltpu.CompilerParams(vmem_limit_bytes=vmem << 20),
        cost_estimate=pl.CostEstimate(
            flops=cost[0], bytes_accessed=cost[1], transcendentals=0
        )
        if cost
        else None,
        input_output_aliases={1 + first + q: q for q in range(len(into))},
    )(meta, *[a for a, _, _ in ins], *extra)


def whole(x):
    zeros = (0,) * x.ndim
    return (x, x.shape, lambda *_: zeros)


def whole_out(shape, dtype):
    zeros = (0,) * len(shape)
    return (shape, dtype, shape, lambda *_: zeros)


class Sizes:
    def __init__(self, chunks, micro, images):
        self.chunks = chunks
        self.half = chunks // 2
        self.micro = micro
        self.images = images
        self.rows = PIXELS * images
        self.padded = SIDE * 8 * images
        self.live = chunks
        self.batch = 2 * chunks
        self.count = 3 * chunks
        self.arrive = 3 * chunks + micro
        self.planes = 4 * chunks + micro
        self.arrival = [0]
        for step in range(1, chunks // 2):
            self.arrival += [chunks - step, step]
        self.arrival.append(chunks // 2)

    def own_count(self, meta):
        batch = meta[self.batch]
        count = meta[self.count]
        for m in range(1, self.micro):
            count = jnp.where(batch == m, meta[self.count + m], count)
        return count.astype(F32)


def split_lanes(value, native):
    for q in range(native.shape[0]):
        native[q] = value[:, q * 128 : (q + 1) * 128]


def meta_body(sz, dp, ratio, counts, table, out):
    d, c = lax.axis_index("dp"), lax.axis_index("chan")
    per_batch = sz.chunks // sz.micro
    for k in range(sz.chunks):
        chunk = table[c, k]
        batch = lax.div(chunk, per_batch)
        have = counts[batch, d] - sz.images * lax.rem(chunk, per_batch)
        out[k] = chunk
        out[sz.live + k] = jnp.minimum(jnp.maximum(have, 0), sz.images)
        out[sz.batch + k] = batch
        out[sz.arrive + k] = jnp.int32(sz.arrival[k])
    for m in range(sz.micro):
        total = counts[m, 0]
        for g in range(1, dp):
            total += counts[m, g]
        out[sz.count + m] = PIXELS * total
    for p in range(dp):
        out[sz.planes + p] = d ^ ((p % (dp // 2)) * 2 + p // (dp // 2))
    out[sz.planes + dp] = lax.div(c, ratio)
    out[sz.planes + dp + 1] = lax.rem(c, ratio)


def make_meta(sz, ring, dp, ratio, counts):
    smem = pl.BlockSpec(memory_space=pltpu.SMEM)
    return pl.pallas_call(
        functools.partial(meta_body, sz, dp, ratio),
        in_specs=[smem, smem],
        out_specs=smem,
        out_shape=jax.ShapeDtypeStruct((sz.planes + dp + 2,), jnp.int32),
    )(counts, jnp.asarray(ring.table))


def to_padded(sz, native, padded):
    n = sz.images
    for q in range(native.shape[0]):
        for i in range(SIDE):
            for j in range(SIDE):
                at = (i * 8 + j) * n
                padded[at : at + n, q * 128 : (q + 1) * 128] = native[
                    q, pl.ds(i * SIDE + j, n, stride=PIXELS), :
                ]
    for i in range(SIDE):
        at = (i * 8 + 7) * n
        padded[at : at + n, :] = jnp.zeros((n, padded.shape[1]), F32)


def to_native(sz, padded, native, out):
    n = sz.images
    for q in range(native.shape[0]):
        for i in range(SIDE):
            for j in range(SIDE):
                at = (i * 8 + j) * n
                native[q, pl.ds(i * SIDE + j, n, stride=PIXELS), :] = padded[
                    at : at + n, q * 128 : (q + 1) * 128
                ]
        out[:, q * 128 : (q + 1) * 128] = native[q].astype(out.dtype)


def row_mask(sz, width, live):
    rows = lax.broadcasted_iota(jnp.int32, (sz.padded, width), 0)
    n = sz.images
    inside = lax.rem(lax.div(rows, n), 8) < SIDE
    if live is None:
        return inside
    return jnp.logical_and(inside, lax.rem(rows, n) < live)


def put_sums(stat, one, two):
    stat[0:1, :] = jnp.sum(one, axis=0, keepdims=True)
    stat[1:2, :] = jnp.sum(two, axis=0, keepdims=True)


def lay_taps(sz, value, strip, taps):
    n = sz.images
    width = strip.shape[1]
    strip[0 : 9 * n, :] = jnp.zeros((9 * n, width), F32)
    strip[65 * n : 74 * n, :] = jnp.zeros((9 * n, width), F32)
    strip[9 * n : 65 * n, :] = value
    for b in range(3):
        taps[b] = strip[b * n : b * n + 72 * n, :].astype(BF16)


def first_lead_body(meta, x, weight, low, high):
    value = jnp.dot(x[0], weight[...], preferred_element_type=F32).astype(BF16)
    half = low.shape[1]
    low[...] = value[:, :half]
    high[...] = value[:, half:]


def first_part_body(meta, x, weight, out):
    out[0] = jnp.dot(x[0], weight[...], preferred_element_type=F32).astype(BF16)


def first_body(sz, meta, f, b, own, pre, stat, native):
    split_lanes(f[...].astype(F32) + b[...].astype(F32) + own[0].astype(F32), native)
    to_padded(sz, native, pre)
    value = pre[...]
    kept = jnp.where(row_mask(sz, value.shape[1], meta[sz.live]), value, 0.0)
    put_sums(stat, kept, kept * kept)


def conv_body(
    sz, meta, pre, stat, params, weight, out, raw, stat_out, acted, strip, taps, total, native
):
    step = pl.program_id(0)
    n = sz.images
    width = pre.shape[1]

    @pl.when(step == 0)
    def _():
        average, inv = moments(stat[...], sz.own_count(meta))
        z = params[0:1] * ((pre[...] - average) * inv) + params[1:2]
        act = jnp.where(row_mask(sz, width, None), z * sigmoid(z), 0.0)
        acted[...] = act.astype(BF16)
        lay_taps(sz, act, strip, taps)
        total[...] = jnp.zeros_like(total)

    at = pl.multiple_of(step * 8 * n, 8 * n)
    for b in range(3):
        total[...] += jnp.dot(
            taps[b, pl.ds(at, sz.padded), :], weight[0, b], preferred_element_type=F32
        )

    @pl.when(step == 2)
    def _():
        value = jnp.where(row_mask(sz, width, None), total[...], 0.0)
        out[...] = value
        to_native(sz, total, native, raw)
        kept = jnp.where(row_mask(sz, width, meta[sz.live]), value, 0.0)
        put_sums(stat_out, kept, kept * kept)


def pick(sz, stat, batch):
    found = stat[0:2]
    for m in range(1, sz.micro):
        found = jnp.where(batch == m, stat[2 * m : 2 * m + 2], found)
    return found


def pick_count(sz, meta, batch):
    count = meta[sz.count]
    for m in range(1, sz.micro):
        count = jnp.where(batch == m, meta[sz.count + m], count)
    return count.astype(F32)


def add_sums(sz, stat, batch, one, two):
    sums = jnp.concatenate(
        [jnp.sum(one, axis=0, keepdims=True), jnp.sum(two, axis=0, keepdims=True)], axis=0
    )
    for m in range(sz.micro):
        stat[2 * m : 2 * m + 2, :] += jnp.where(batch == m, sums, 0.0)


def stage_piece(pieces, place, step):
    for k, piece in enumerate(pieces):

        @pl.when(step == k)
        def _(piece=piece):
            if len(piece) == 1:
                place[...] = piece[0][...]
            else:
                half = piece[0].shape[1]
                place[:, :half] = piece[0][...]
                place[:, half:] = piece[1][...]


def split_refs(layout, refs):
    pieces, at = [], 0
    for many in layout:
        pieces.append(refs[at : at + many])
        at += many
    return pieces, refs[at:]


def expand_body(sz, layout, offset, meta, *refs):
    pieces, rest = split_refs(layout, refs)
    stat, params, weight, act, pre, stat_out, place = rest
    step = pl.program_id(0)
    stage_piece(pieces, place, step)
    k = meta[sz.arrive + offset + step]
    batch = meta[sz.batch + k]
    average, inv = moments(pick(sz, stat[...], batch), pick_count(sz, meta, batch))
    z = params[2:3] * ((place[...].astype(F32) - average) * inv) + params[3:4]
    acted = (z * sigmoid(z)).astype(BF16)
    act[0] = acted
    value = jnp.dot(acted, weight[...], preferred_element_type=F32)
    pre[0] = value

    @pl.when(step == 0)
    def _():
        stat_out[...] = jnp.zeros_like(stat_out)

    rows = lax.broadcasted_iota(jnp.int32, value.shape, 0)
    kept = jnp.where(rows < PIXELS * meta[sz.live + k], value, 0.0)
    add_sums(sz, stat_out, batch, kept, kept * kept)


def out_body(sz, meta, pre, stat, params, x, cot, out, grad, stat_out):
    step = pl.program_id(0)
    batch = meta[sz.batch + step]
    average, inv = moments(pick(sz, stat[...], batch), pick_count(sz, meta, batch))
    normed = (pre[0] - average) * inv
    summed = params[0:1] * normed + params[1:2] + x[0].astype(F32)
    sigma = sigmoid(summed)
    rows = lax.broadcasted_iota(jnp.int32, summed.shape, 0)
    live = rows < PIXELS * meta[sz.live + step]
    out[0] = jnp.where(live, summed * sigma, 0.0)
    upstream = jnp.where(
        live, cot[0].astype(F32) * (sigma * (1.0 + summed * (1.0 - sigma))), 0.0
    )
    grad[0] = upstream

    @pl.when(step == 0)
    def _():
        stat_out[...] = jnp.zeros_like(stat_out)

    add_sums(sz, stat_out, batch, upstream, upstream * normed)


def shrink_body(sz, lead, meta, pre, stat, params, grad, sums, weight, back, *parts):
    if lead:
        k = sz.half
    else:
        step = pl.program_id(0)
        k = jnp.where(step < sz.half, step, step + 1)
    batch = meta[sz.batch + k]
    count = pick_count(sz, meta, batch)
    average, inv = moments(pick(sz, stat[...], batch), count)
    both = pick(sz, sums[...], batch)
    normed = (pre[0] - average) * inv
    rows = lax.broadcasted_iota(jnp.int32, normed.shape, 0)
    live = rows < PIXELS * meta[sz.live + k]
    value = params[0:1] * inv * (grad[0] - (both[0:1] + normed * both[1:2]) / count)
    value = jnp.where(live, value, 0.0).astype(BF16)
    back[0] = value
    part = lax.dot_general(
        value, weight[...], (((1,), (1,)), ((), ())), preferred_element_type=F32
    ).astype(BF16)
    if lead:
        half = part.shape[1] // 2
        parts[0][...] = part[:, :half]
        parts[1][...] = part[:, half:]
    else:
        parts[0][0] = part


def middle_up_body(sz, meta, f, b, own, pre, stat, params, up, stat_out, native, padded):
    split_lanes(f[...].astype(F32) + b[...].astype(F32) + own[0].astype(F32), native)
    to_padded(sz, native, padded)
    average, inv = moments(stat[...], sz.own_count(meta))
    normed = (pre[...] - average) * inv
    z = params[2:3] * normed + params[3:4]
    value = jnp.where(
        row_mask(sz, pre.shape[1], meta[sz.live]), padded[...] * silu_slope(z), 0.0
    )
    up[...] = value
    put_sums(stat_out, value, value * normed)


def conv_back_body(
    sz,
    meta,
    up,
    sums,
    pre_two,
    stat_two,
    pre_one,
    stat_one,
    params,
    weight,
    stay,
    send,
    up_one,
    stat_out,
    strip,
    taps,
    total,
):
    step = pl.program_id(0)
    n = sz.images
    width = up.shape[1]

    @pl.when(step == 0)
    def _():
        count = sz.own_count(meta)
        average, inv = moments(stat_two[...], count)
        normed = (pre_two[...] - average) * inv
        value = params[2:3] * inv * (up[...] - (sums[0:1] + normed * sums[1:2]) / count)
        value = jnp.where(row_mask(sz, width, meta[sz.live]), value, 0.0)
        half, _, lanes = stay.shape
        for p in range(2 * half):
            for plane in range(2 * half):

                @pl.when(meta[sz.planes + p] == plane)
                def _(p=p, plane=plane):
                    out = stay if p < half else send
                    out[p % half] = value[:, plane * lanes : (plane + 1) * lanes].astype(BF16)

        lay_taps(sz, value, strip, taps)
        total[...] = jnp.zeros_like(total)

    at = pl.multiple_of((2 - step) * 8 * n, 8 * n)
    for b in range(3):
        total[...] += lax.dot_general(
            taps[2 - b, pl.ds(at, sz.padded), :],
            weight[0, b],
            (((1,), (1,)), ((), ())),
            preferred_element_type=F32,
        )

    @pl.when(step == 2)
    def _():
        average, inv = moments(stat_one[...], sz.own_count(meta))
        normed = (pre_one[...] - average) * inv
        z = params[0:1] * normed + params[1:2]
        value = jnp.where(
            row_mask(sz, width, meta[sz.live]), total[...] * silu_slope(z), 0.0
        )
        up_one[...] = value
        put_sums(stat_out, value, value * normed)


def first_back_body(sz, meta, up, sums, pre, stat, params, back, padded, native):
    count = sz.own_count(meta)
    average, inv = moments(stat[...], count)
    normed = (pre[...] - average) * inv
    value = params[0:1] * inv * (up[...] - (sums[0:1] + normed * sums[1:2]) / count)
    padded[...] = jnp.where(row_mask(sz, pre.shape[1], meta[sz.live]), value, 0.0)
    to_native(sz, padded, native, back)


def input_body(sz, layout, more, meta, *refs):
    pieces, rest = split_refs(layout, refs)
    if more:
        grad, x, weight, had, out, grad_weight, place, total = rest
    else:
        grad, x, weight, out, grad_weight, place, total = rest
    step = pl.program_id(0)
    stage_piece(pieces, place, step)
    value = place[...]
    out[0] = grad[0] + lax.dot_general(
        value, weight[...], (((1,), (1,)), ((), ())), preferred_element_type=F32
    )

    @pl.when(step == 0)
    def _():
        total[...] = had[...] if more else jnp.zeros_like(total)

    total[...] += lax.dot_general(
        x[0], value, (((0,), (0,)), ((), ())), preferred_element_type=F32
    )

    @pl.when(step == len(layout) - 1)
    def _():
        grad_weight[...] = total[...].astype(grad_weight.dtype)


def middle_grad_body(sz, dp, meta, acts, backs, out, strip, taps, total):
    source = pl.program_id(0)
    n = sz.images
    lay_taps(sz, backs[0, 0].astype(F32), strip, taps)
    shifted = [
        taps[2 - b, (2 - a) * 8 * n : (2 - a) * 8 * n + sz.padded, :]
        for a in range(3)
        for b in range(3)
    ]

    @pl.when(source == 0)
    def _():
        total[...] = jnp.zeros_like(total)

    total[...] += lax.dot_general(
        acts[0],
        jnp.concatenate(shifted, axis=1),
        (((0,), (0,)), ((), ())),
        preferred_element_type=F32,
    )

    @pl.when(source == dp - 1)
    def _():
        depth, lanes = out.shape[1] // TAPS, out.shape[2]
        for k in range(sz.chunks):
            at = pl.multiple_of(meta[k] * depth, depth)
            for tap in range(TAPS):
                out[k, tap * depth : (tap + 1) * depth, :] = total[
                    pl.ds(at, depth), tap * lanes : (tap + 1) * lanes
                ].astype(BF16)


def assemble_body(sz, half, depth, meta, *refs):
    stacks, out = refs[:-1], refs[-1]
    early = sz.chunks - 3

    def fill(plane):
        for q, k in enumerate(sz.arrival):
            pieces = stacks[plane if q < early else half + plane]
            at = pl.multiple_of(meta[k] * depth, depth)
            for tap in range(TAPS):
                value = pieces[0, q if q < early else q - early, tap * depth : (tap + 1) * depth, :]
                if len(out.shape) == 3:
                    out[tap, pl.ds(at, depth), :] = value
                else:
                    out[0, tap, pl.ds(at, depth), :] = value

    for p in range(2 * half):

        @pl.when(pl.program_id(0) == p)
        def _(p=p):
            fill(p if p < half else half + p)


def prepare_body(weights, last, params, out):
    many, lanes = weights.shape
    out[:many, :] = weights[...].astype(BF16)
    depth = last.shape[0]
    for b in range(last.shape[1] // lanes):
        out[many + b * depth : many + (b + 1) * depth, :] = last[
            :, b * lanes : (b + 1) * lanes
        ].astype(BF16)
    value = params[...]
    count, width = value.shape
    one = value.astype(BF16)
    left = value - one.astype(F32)
    two = left.astype(BF16)
    three = (left - two.astype(F32)).astype(BF16)
    rest = jnp.zeros((16 - 3 * count, width), F32)
    rows = jnp.concatenate([part.astype(F32) for part in (one, two, three)] + [rest], axis=0)
    if width < lanes:
        rows = jnp.concatenate([rows, jnp.zeros((16, lanes - width), F32)], axis=1)
    out[out.shape[0] - 16 :, :] = rows.astype(BF16)


def last_assemble_body(meta, blocks, out):
    lanes = blocks.shape[3]
    for b in range(blocks.shape[1]):
        out[:, b * lanes : (b + 1) * lanes] = blocks[0, b]


def last_grad_body(sz, meta, act, back, out, total):
    step = pl.program_id(0)

    @pl.when(step == 0)
    def _():
        total[...] = jnp.zeros_like(total)

    total[...] += lax.dot_general(
        act[0], back[0], (((0,), (0,)), ((), ())), preferred_element_type=F32
    )

    @pl.when(step == sz.chunks - 1)
    def _():
        depth = out.shape[1]
        for k in range(sz.chunks):
            at = pl.multiple_of(meta[k] * depth, depth)
            out[k] = total[pl.ds(at, depth), :].astype(BF16)


def pieces_in(sz, pieces):
    ins, layout = [], []
    for piece in pieces:
        parts = piece if isinstance(piece, tuple) else (piece,)
        layout.append(len(parts))
        ins += [whole(p) for p in parts]
    return ins, layout


def local(
    dp,
    chan,
    inputs,
    cotangent,
    w_first,
    first_m,
    first_v,
    w_middle,
    middle_m,
    middle_v,
    w_last,
    last_m,
    last_v,
    mid_params,
    mid_m,
    mid_v,
    out_params,
    out_m,
    out_v,
    image_counts,
):
    ring = Ring(chan)
    d = lax.axis_index("dp")
    c = lax.axis_index("chan")
    micro, pixels, deep = inputs.shape
    images = micro * pixels // PIXELS // chan
    sz = Sizes(chan, micro, images)
    rows, padded = sz.rows, sz.padded
    per_batch = chan // micro
    depth, lanes = w_middle.shape[2], w_middle.shape[3]
    mid = depth * chan
    half = dp // 2
    last_blocks = w_last.shape[1] // lanes
    own_blocks = deep // lanes
    ratio = last_blocks // own_blocks

    meta = make_meta(sz, ring, dp, ratio, image_counts)
    at = meta[:chan]

    dp_bits = bits_below(dp)
    wide_bits = dp_bits[1:]
    first = w_first.astype(BF16)
    for bit in dp_bits:
        other = swap(first, "dp", bit, dp)
        first = jnp.where(
            (d & bit) == 0,
            jnp.concatenate([first, other], axis=1),
            jnp.concatenate([other, first], axis=1),
        )
    many = TAPS * depth
    tail_at = many + last_blocks * depth
    (payload,) = pl.pallas_call(
        prepare_body,
        in_specs=[pl.BlockSpec(memory_space=pltpu.VMEM)] * 3,
        out_specs=[pl.BlockSpec(memory_space=pltpu.VMEM)],
        out_shape=[jax.ShapeDtypeStruct((tail_at + 16, lanes), BF16)],
    )(w_middle.reshape(many, lanes), w_last, mid_params)
    mids = Gather(ring, payload, 0)
    while mids.count < chan // 2:
        mids.step()

    x = inputs.reshape(chan, rows, deep)
    cot = cotangent.reshape(chan, rows, deep)

    def at_place(k, meta):
        return (meta[k], 0, 0)

    def in_order(k, meta):
        return (k, 0, 0)

    opposite = chan // 2

    def skipping(k, meta):
        return (jnp.where(k < opposite, k, k + 1), 0, 0)

    def skipping_at(k, meta):
        return (meta[jnp.where(k < opposite, k, k + 1)], 0, 0)

    low, high = run(
        first_lead_body,
        meta,
        (1,),
        [(x, (1, rows, deep), lambda k, meta: (meta[opposite], 0, 0)), whole(first)],
        [whole_out((rows, mid // 2), BF16), whole_out((rows, mid // 2), BF16)],
    )
    (parts,) = run(
        first_part_body,
        meta,
        (chan - 1,),
        [(x, (1, rows, deep), skipping_at), whole(first)],
        [((chan, rows, mid), BF16, (1, rows, mid), skipping)],
        cost=(2 * chan * rows * deep * mid, 2 * chan * rows * (deep + mid)),
    )
    sums = Scatter(ring, low, high, lambda k: parts[k], 1)
    while sums.count < opposite:
        sums.step()
    f, b = sums.f, sums.b

    came = [jnp.concatenate(p, axis=0) if isinstance(p, tuple) else p for p in mids.pieces]
    tails = jnp.stack([p[many:] for p in came])
    near, far = [], []
    for group in (sz.arrival[: chan - 3], sz.arrival[chan - 3 :]):
        stack = jnp.stack([came[k][:many] for k in group])[None]
        planes = [stack]
        for bit in wide_bits:
            planes += [swap(p, "dp", bit, dp) for p in planes]
        near.append(planes)
        far.append([swap(p, "dp", 1, dp) for p in planes])
    near = [near[g][q] for g in range(2) for q in range(half)]
    far = [far[g][q] for g in range(2) for q in range(half)]
    if lanes % 128 == 0:
        placed = ((TAPS, mid, mid), BF16, (TAPS, mid, lanes), lambda p, meta: (0, 0, meta[sz.planes + p]))
    else:
        placed = (
            (dp, TAPS, mid, lanes),
            BF16,
            (1, TAPS, mid, lanes),
            lambda p, meta: (meta[sz.planes + p], 0, 0, 0),
        )
    (middle,) = run(
        functools.partial(assemble_body, sz, half, depth),
        meta,
        (dp,),
        [whole(p) for p in near + far],
        [placed],
    )
    here = (at[None, :] == jnp.arange(chan)[:, None])[:, :, None, None]
    tail = tails[:, last_blocks * depth :, :depth].astype(F32)
    tail = (tail[:, 8:12] + tail[:, 4:8]) + tail[:, 0:4]
    params = jnp.sum(jnp.where(here, tail[None], 0.0), axis=1)
    params = params.transpose(1, 0, 2).reshape(4, mid)
    if lanes % 128 != 0:
        middle = middle.transpose(1, 2, 0, 3)
    middle = middle.reshape(3, 3, mid, mid)
    lasts = tails[:, : last_blocks * depth].reshape(chan, ratio, own_blocks, depth, lanes)
    own_last = lax.dynamic_index_in_dim(lasts, c % ratio, axis=1, keepdims=False)
    found = jnp.where(d == c // ratio, own_last, jnp.zeros_like(own_last))
    for shift in range(1, dp):
        moves = [
            ((k // ratio) * chan + k, ((k // ratio) ^ shift) * chan + k) for k in range(chan)
        ]
        found = found + lax.ppermute(own_last, ("dp", "chan"), moves)
    (last,) = run(
        last_assemble_body,
        meta,
        (chan,),
        [(found, (1, own_blocks, depth, lanes), lambda k, meta: (k, 0, 0, 0))],
        [((mid, deep), BF16, (depth, deep), lambda k, meta: (meta[k], 0))],
    )

    def head(stack):
        return (stack, (1,) + stack.shape[1:], lambda *_: (0, 0, 0))

    stat_bits = [k for k in bits_below(chan) if k < per_batch]

    def total_rows(stat):
        return sum_over(sum_over(stat, "dp", dp_bits, dp), "chan", stat_bits, chan)

    def all_batches(stat):
        for bit in bits_below(chan):
            if bit >= per_batch:
                other = swap(stat, "chan", bit, chan)
                stat = jnp.where(
                    (c & bit) == 0,
                    jnp.concatenate([stat, other], axis=0),
                    jnp.concatenate([other, stat], axis=0),
                )
        return stat

    pre_one, stat_one = run(
        functools.partial(first_body, sz),
        meta,
        (1,),
        [whole(f), whole(b), head(parts)],
        [whole_out((padded, mid), F32), whole_out((2, mid), F32)],
        [pltpu.VMEM((mid // 128, rows, 128), F32)],
        vmem=VMEM,
        cost=(10 * padded * mid, 10 * padded * mid),
    )
    stat_one = total_rows(stat_one)

    tap_block = (1, 3, mid, mid)
    conv_flops = 2 * TAPS * padded * mid * mid
    conv_bytes = 2 * TAPS * mid * mid + 16 * padded * mid
    pre_two, raw, stat_two, acted = run(
        functools.partial(conv_body, sz),
        meta,
        (3,),
        [
            whole(pre_one),
            whole(stat_one),
            whole(params),
            (middle, tap_block, lambda s, meta: (s, 0, 0, 0)),
        ],
        [
            whole_out((padded, mid), F32),
            whole_out((rows, mid), BF16),
            whole_out((2, mid), F32),
            whole_out((padded, mid), BF16),
        ],
        [
            pltpu.VMEM((74 * images, mid), F32),
            pltpu.VMEM((3, 72 * images, mid), BF16),
            pltpu.VMEM((padded, mid), F32),
            pltpu.VMEM((mid // 128, rows, 128), F32),
        ],
        vmem=VMEM,
        cost=(conv_flops, conv_bytes),
    )
    gather = Gather(ring, raw, 1)
    gather.step()
    stat_two = sum_over(stat_two, "dp", dp_bits, dp)
    gather.step(stat_two)
    stat_two = sum_over(stat_two, "chan", stat_bits, chan)
    if gather.count < opposite - 1:
        gather.step(stat_two)
    stats_two = all_batches(stat_two)
    while gather.count < opposite - 1:
        gather.step()
    gather.step(stats_two)
    pieces = gather.pieces
    order = [1] + wide_bits[::-1]
    acts = acted[None]
    for bit in order:
        acts = jnp.concatenate([acts, swap(acts, "dp", bit, dp)], axis=0)

    def expand(start, steps, into):
        ins, layout = pieces_in(sz, [pieces[k] for k in sz.arrival[start : start + steps]])

        def arrived(k, meta):
            return (meta[sz.arrive + start + k], 0, 0)

        return run(
            functools.partial(expand_body, sz, layout, start),
            meta,
            (steps,),
            ins + [whole(stats_two), whole(params), whole(last)],
            [
                ((chan, rows, mid), BF16, (1, rows, mid), arrived),
                ((chan, rows, deep), F32, (1, rows, deep), arrived),
                whole_out((2 * micro, deep), F32),
            ],
            [pltpu.VMEM((rows, mid), BF16)],
            vmem=VMEM,
            cost=(2 * steps * rows * deep * mid, steps * rows * (4 * mid + 4 * deep)),
            into=into,
        )

    early = chan - 3
    act, pre_three, stat_early = expand(0, early, [])
    act, pre_three, stat_late = expand(early, 3, [act, pre_three])
    stat_three = stat_early + stat_late
    stat_three = sum_over(stat_three, "dp", bits_below(dp), dp)
    block_out, grad_summed, sums_three = run(
        functools.partial(out_body, sz),
        meta,
        (chan,),
        [
            (pre_three, (1, rows, deep), in_order),
            whole(stat_three),
            whole(out_params),
            (x, (1, rows, deep), at_place),
            (cot, (1, rows, deep), at_place),
        ],
        [
            ((chan, rows, deep), F32, (1, rows, deep), at_place),
            ((chan, rows, deep), F32, (1, rows, deep), in_order),
            whole_out((2 * micro, deep), F32),
        ],
        vmem=VMEM,
        cost=(20 * chan * rows * deep, 16 * chan * rows * deep),
    )
    sums_three = sum_over(sums_three, "dp", bits_below(dp), dp)

    def shrink(steps, place, into, lead):
        if lead:
            made = [whole_out((rows, mid // 2), BF16), whole_out((rows, mid // 2), BF16)]
        else:
            made = [((chan, rows, mid), BF16, (1, rows, mid), place)]
        return run(
            functools.partial(shrink_body, sz, lead),
            meta,
            (steps,),
            [
                (pre_three, (1, rows, deep), place),
                whole(stat_three),
                whole(out_params),
                (grad_summed, (1, rows, deep), place),
                whole(sums_three),
                whole(last),
            ],
            [((chan, rows, deep), BF16, (1, rows, deep), place)] + made,
            vmem=VMEM,
            cost=(2 * steps * rows * deep * mid, steps * rows * (2 * mid + 10 * deep)),
            into=into,
        )

    back_last, low, high = shrink(1, lambda k, meta: (opposite, 0, 0), [], True)
    back_last, back_parts = shrink(chan - 1, skipping, [back_last], False)
    sums = Scatter(ring, low, high, lambda k: back_parts[k], 1)
    while sums.count < opposite:
        sums.step()
    f, b = sums.f, sums.b
    (grad_last,) = run(
        functools.partial(last_grad_body, sz),
        meta,
        (chan,),
        [(act, (1, rows, mid), in_order), (back_last, (1, rows, deep), in_order)],
        [whole_out((chan, depth, deep), BF16)],
        [pltpu.VMEM((mid, deep), F32)],
        cost=(2 * chan * rows * deep * mid, 2 * chan * rows * (mid + deep)),
    )
    for bit in dp_bits:
        grad_last = add16(grad_last, swap(grad_last, "dp", bit, dp))
    held = [
        jnp.where(c % ratio == r, grad_last, jnp.zeros_like(grad_last)) for r in range(ratio)
    ]
    held = jnp.concatenate(held, axis=2)
    held = jnp.where(d == c // ratio, held, jnp.zeros_like(held))
    cut = held.shape[2] // 2
    last_sums = Scatter(
        ring, held[opposite, :, :cut], held[opposite, :, cut:], lambda k: held[k], 1
    )
    while last_sums.count < opposite:
        last_sums.step()
    owned_last = held[0].astype(F32) + last_sums.f.astype(F32) + last_sums.b.astype(F32)

    up_two, sums_two = run(
        functools.partial(middle_up_body, sz),
        meta,
        (1,),
        [
            whole(f),
            whole(b),
            head(back_parts),
            whole(pre_two),
            whole(stat_two),
            whole(params),
        ],
        [whole_out((padded, mid), F32), whole_out((2, mid), F32)],
        [pltpu.VMEM((mid // 128, rows, 128), F32), pltpu.VMEM((padded, mid), F32)],
        vmem=VMEM,
        cost=(20 * padded * mid, 14 * padded * mid),
    )
    sums_two = total_rows(sums_two)
    stay, send, up_one, sums_one = run(
        functools.partial(conv_back_body, sz),
        meta,
        (3,),
        [
            whole(up_two),
            whole(sums_two),
            whole(pre_two),
            whole(stat_two),
            whole(pre_one),
            whole(stat_one),
            whole(params),
            (middle, tap_block, lambda s, meta: (s, 0, 0, 0)),
        ],
        [
            whole_out((half, padded, lanes), BF16),
            whole_out((half, padded, lanes), BF16),
            whole_out((padded, mid), F32),
            whole_out((2, mid), F32),
        ],
        [
            pltpu.VMEM((74 * images, mid), F32),
            pltpu.VMEM((3, 72 * images, mid), BF16),
            pltpu.VMEM((padded, mid), F32),
        ],
        vmem=VMEM,
        cost=(conv_flops, conv_bytes),
    )

    sums_one = total_rows(sums_one)
    (back_one,) = run(
        functools.partial(first_back_body, sz),
        meta,
        (1,),
        [whole(up_one), whole(sums_one), whole(pre_one), whole(stat_one), whole(params)],
        [whole_out((rows, mid), BF16)],
        [pltpu.VMEM((padded, mid), F32), pltpu.VMEM((mid // 128, rows, 128), F32)],
        cost=(10 * padded * mid, 10 * padded * mid),
    )
    gather = Gather(ring, back_one, 1)
    while gather.count < opposite:
        gather.step()
    pieces = gather.pieces

    backs = jnp.stack([stay, swap(send, "dp", 1, dp)])
    for bit in wide_bits[::-1]:
        cut = backs.shape[1] // 2
        backs = jnp.concatenate(
            [backs[:, :cut], swap(backs[:, cut:], "dp", bit, dp)], axis=0
        )
    (grad_middle,) = run(
        functools.partial(middle_grad_body, sz, dp),
        meta,
        (dp,),
        [
            (acts, (1, padded, mid), lambda r, meta: (r, 0, 0)),
            (backs, (1, 1, padded, lanes), lambda r, meta: (r, 0, 0, 0)),
        ],
        [whole_out((chan, TAPS * depth, lanes), BF16)],
        [
            pltpu.VMEM((74 * images, lanes), F32),
            pltpu.VMEM((3, 72 * images, lanes), BF16),
            pltpu.VMEM((mid, TAPS * lanes), F32),
        ],
        cost=(conv_flops, conv_bytes),
        after=[back_one],
    )
    cut = TAPS * depth // 2
    middle_sums = Scatter(
        ring,
        grad_middle[opposite, :cut],
        grad_middle[opposite, cut:],
        lambda k: grad_middle[k],
        0,
    )
    middle_steps = [middle_sums.f]
    while middle_sums.count < opposite:
        middle_sums.step()
        middle_steps.append(middle_sums.f)
    owned_middle = (
        grad_middle[0].astype(F32) + middle_sums.f.astype(F32) + middle_sums.b.astype(F32)
    ).reshape(3, 3, depth, lanes)

    def input_back(start, steps, had, into, after):
        ins, layout = pieces_in(sz, [pieces[k] for k in sz.arrival[start : start + steps]])
        done = start + steps == chan

        def arrived(k, meta):
            return (meta[sz.arrive + start + k], 0, 0)

        def arrived_at(k, meta):
            return (meta[meta[sz.arrive + start + k]], 0, 0)

        return run(
            functools.partial(input_body, sz, layout, bool(had)),
            meta,
            (steps,),
            ins
            + [
                (grad_summed, (1, rows, deep), arrived),
                (x, (1, rows, deep), arrived_at),
                whole(first),
            ]
            + [whole(h) for h in had],
            [
                ((chan, rows, deep), F32, (1, rows, deep), arrived_at),
                whole_out((deep, mid), BF16 if done else F32),
            ],
            [pltpu.VMEM((rows, mid), BF16), pltpu.VMEM((deep, mid), F32)],
            vmem=VMEM,
            cost=(4 * steps * rows * deep * mid, steps * rows * (2 * mid + 10 * deep)),
            into=into,
            after=after,
        )

    input_grad, grad_early = input_back(0, early, [], [], middle_steps[1:2])
    input_grad, grad_first = input_back(early, 3, [grad_early], [input_grad], middle_steps[2:3])
    owned_first = scatter_columns(grad_first, d, dp)

    sums_first, sums_middle = all_batches(sums_one), all_batches(sums_two)

    def over_batches(stat, row):
        total = stat[row]
        for m in range(1, micro):
            total = total + stat[2 * m + row]
        return total

    grad_mid = jnp.stack(
        [
            over_batches(sums_first, 1),
            over_batches(sums_first, 0),
            over_batches(sums_middle, 1),
            over_batches(sums_middle, 0),
        ]
    )
    grad_mid = lax.dynamic_slice_in_dim(grad_mid, c * depth, depth, axis=1)
    grad_out = jnp.stack([over_batches(sums_three, 1), over_batches(sums_three, 0)])

    return (
        block_out.reshape(inputs.shape),
        input_grad.reshape(inputs.shape),
        *adamw(w_first, owned_first, first_m, first_v, rate_first),
        *adamw(w_middle, owned_middle, middle_m, middle_v, rate_middle),
        *adamw(w_last, owned_last, last_m, last_v, rate_last),
        *adamw(mid_params, grad_mid, mid_m, mid_v, rate_norm),
        *adamw(out_params, grad_out, out_m, out_v, rate_norm),
    )


def scatter_columns(grad, d, dp):
    blocks = grad.reshape(grad.shape[0], dp, grad.shape[1] // dp)
    kept = [blocks[:, p] for p in range(dp)]
    for bit in bits_below(dp):
        kept = [
            jnp.where((d & bit) == 0, kept[q], kept[q ^ bit]) for q in range(len(kept))
        ]
    todo = {q: kept[q] for q in range(dp)}
    for bit in [1] + bits_below(dp)[:0:-1]:
        send = sorted(q for q in todo if q & bit)
        stay = sorted(q for q in todo if not q & bit)
        got = swap(jnp.stack([todo[q] for q in send]), "dp", bit, dp)
        todo = {
            q: todo[q].astype(F32) + got[send.index(q | bit)].astype(F32) for q in stay
        }
        if len(todo) > 1:
            todo = {q: v.astype(BF16) for q, v in todo.items()}
    return todo[0]


def solution(mesh):
    rows = P(None, "dp", "chan")
    flat = P("chan", "dp")
    square = P(None, None, "chan", "dp")
    vector = P(None, "chan")
    state = (flat,) * 3 + (square,) * 3 + (flat,) * 3 + (vector,) * 6
    return jax.shard_map(
        functools.partial(local, mesh.shape["dp"], mesh.shape["chan"]),
        mesh=mesh,
        in_specs=(rows, rows) + state + (P(),),
        out_specs=(rows, rows) + state,
        check_vma=False,
    )
```

```python
import functools

import jax
import jax.numpy as jnp
import numpy as np
from jax import lax
from jax.experimental import pallas as pl
from jax.experimental.pallas import tpu as pltpu
from jax.sharding import PartitionSpec as P

STEPS = 5
SIDE = 7
PIXELS = SIDE * SIDE
TAPS = 9
VMEM = 24
F32 = jnp.float32
BF16 = jnp.bfloat16

norm_eps = 1e-05
adam_eps = 1e-08
adam_beta = 0.5
decay_rate = 0.05
rate_first = 0.02
rate_middle = 0.015
rate_last = 0.04
rate_norm = 0.25


def sigmoid(value):
    return 0.5 * jnp.tanh(0.5 * value) + 0.5


def silu_slope(value):
    sigma = sigmoid(value)
    return sigma * (1.0 + value * (1.0 - sigma))


def moments(stat, count):
    average = stat[0:1] / count
    variance = stat[1:2] / count - average * average
    return average, lax.rsqrt(variance + norm_eps)


def adamw(weight, gradient, moment_one, moment_two, step_rate):
    one_new = adam_beta * moment_one + (1.0 - adam_beta) * gradient
    two_new = adam_beta * moment_two + (1.0 - adam_beta) * gradient * gradient
    correct = 1.0 - adam_beta**STEPS
    weight_new = weight - step_rate * (
        one_new / correct / (jnp.sqrt(two_new / correct) + adam_eps) + decay_rate * weight
    )
    return (weight_new, one_new, two_new)


def ring_of(size):
    across = max(size // 4, 1)
    along = size // across
    order = [(z, 0) for z in range(along)]
    outward = True
    for z in reversed(range(along)):
        steps = list(range(1, across))
        order += [(z, x) for x in (steps if outward else steps[::-1])]
        outward = not outward
    return [z * across + x for z, x in order]


class Ring:
    def __init__(self, size):
        self.size = size
        self.order = ring_of(size)
        ahead = [(self.order[i], self.order[(i + 1) % size]) for i in range(size)]
        self.ahead = ahead
        self.back = [(b, a) for a, b in ahead]
        place = np.argsort(np.array(self.order))
        self.table = np.array(
            [[self.order[(place[c] + k) % size] for k in range(size)] for c in range(size)],
            np.int32,
        )

    def fw(self, x):
        return lax.ppermute(x, "chan", self.ahead)

    def bw(self, x):
        return lax.ppermute(x, "chan", self.back)


def tie(x, other):
    first = lax.slice(other, (0,) * other.ndim, (1,) * other.ndim).reshape(())
    return jnp.where(first > -3e38, x, jnp.zeros_like(x))


def beside(x, other):
    return jnp.where(other > -3e38, x, jnp.zeros_like(x))


class Gather:
    def __init__(self, ring, x, axis):
        self.ring, self.axis, self.half = ring, axis, x.shape[axis] // 2
        self.pieces = [x] + [None] * (ring.size - 1)
        self.count = 0

    def step(self, other=None):
        ring, size = self.ring, self.ring.size
        a, b = self.pieces[(size - self.count) % size], self.pieces[self.count]
        if other is not None:
            a, b = tie(a, other), tie(b, other)
        self.count += 1
        if self.count < size // 2:
            got = [ring.fw(a), ring.bw(b)]
            self.pieces[size - self.count], self.pieces[self.count] = got
        else:
            got = [
                ring.fw(lax.slice_in_dim(a, 0, self.half, axis=self.axis)),
                ring.bw(lax.slice_in_dim(b, self.half, b.shape[self.axis], axis=self.axis)),
            ]
            self.pieces[size // 2] = tuple(got)
        return got


class Scatter:
    def __init__(self, ring, low, high, part, axis):
        self.ring, self.part, self.axis = ring, part, axis
        self.f, self.b = ring.fw(low), ring.bw(high)
        self.count = 1

    def step(self):
        size, axis = self.ring.size, self.axis
        k = size // 2 - self.count
        left, right = self.part(k), self.part(size - k)
        if self.count == 1:
            width = left.shape[axis]
            half = width // 2
            f = jnp.concatenate(
                [
                    beside(add16(lax.slice_in_dim(left, 0, half, axis=axis), self.f), self.b),
                    lax.slice_in_dim(left, half, width, axis=axis),
                ],
                axis,
            )
            b = jnp.concatenate(
                [
                    lax.slice_in_dim(right, 0, half, axis=axis),
                    beside(add16(lax.slice_in_dim(right, half, width, axis=axis), self.b), self.f),
                ],
                axis,
            )
        else:
            f = beside(add16(left, self.f), self.b)
            b = beside(add16(right, self.b), self.f)
        self.count += 1
        self.f, self.b = self.ring.fw(f), self.ring.bw(b)


def add16(one, two):
    return (one.astype(F32) + two.astype(F32)).astype(BF16)


def swap(x, axis, bit, size):
    return lax.ppermute(x, axis, [(i, i ^ bit) for i in range(size)])


def bits_below(size):
    return [1 << k for k in range(size.bit_length() - 1)]


def sum_over(x, axis, bits, size):
    for bit in bits:
        x = x + swap(x, axis, bit, size)
    return x


def run(body, meta, grid, ins, outs, scratch=(), vmem=VMEM, cost=None, after=(), into=()):
    extra = list(into) + list(after)
    first, last = len(ins), len(ins) + len(extra)

    def kernel(meta, *refs):
        body(meta, *refs[:first], *refs[last:])

    return pl.pallas_call(
        kernel if extra else body,
        grid_spec=pltpu.PrefetchScalarGridSpec(
            num_scalar_prefetch=1,
            grid=grid,
            in_specs=[pl.BlockSpec(b, m) for _, b, m in ins]
            + [pl.BlockSpec(memory_space=pl.ANY)] * len(extra),
            out_specs=[pl.BlockSpec(b, m) for _, _, b, m in outs],
            scratch_shapes=list(scratch),
        ),
        out_shape=[jax.ShapeDtypeStruct(s, d) for s, d, _, _ in outs],
        compiler_params=pltpu.CompilerParams(vmem_limit_bytes=vmem << 20),
        cost_estimate=pl.CostEstimate(
            flops=cost[0], bytes_accessed=cost[1], transcendentals=0
        )
        if cost
        else None,
        input_output_aliases={1 + first + q: q for q in range(len(into))},
    )(meta, *[a for a, _, _ in ins], *extra)


def whole(x):
    zeros = (0,) * x.ndim
    return (x, x.shape, lambda *_: zeros)


def whole_out(shape, dtype):
    zeros = (0,) * len(shape)
    return (shape, dtype, shape, lambda *_: zeros)


class Sizes:
    def __init__(self, chunks, micro, images):
        self.chunks = chunks
        self.half = chunks // 2
        self.micro = micro
        self.images = images
        self.rows = PIXELS * images
        self.padded = SIDE * 8 * images
        self.live = chunks
        self.batch = 2 * chunks
        self.count = 3 * chunks
        self.arrive = 3 * chunks + micro
        self.planes = 4 * chunks + micro
        self.arrival = [0]
        for step in range(1, chunks // 2):
            self.arrival += [chunks - step, step]
        self.arrival.append(chunks // 2)

    def own_count(self, meta):
        batch = meta[self.batch]
        count = meta[self.count]
        for m in range(1, self.micro):
            count = jnp.where(batch == m, meta[self.count + m], count)
        return count.astype(F32)


def split_lanes(value, native):
    for q in range(native.shape[0]):
        native[q] = value[:, q * 128 : (q + 1) * 128]


def meta_body(sz, dp, ratio, counts, table, _, out):
    d, c = lax.axis_index("dp"), lax.axis_index("chan")
    per_batch = sz.chunks // sz.micro
    for k in range(sz.chunks):
        chunk = table[c, k]
        batch = lax.div(chunk, per_batch)
        have = counts[batch, d] - sz.images * lax.rem(chunk, per_batch)
        out[k] = chunk
        out[sz.live + k] = jnp.minimum(jnp.maximum(have, 0), sz.images)
        out[sz.batch + k] = batch
        out[sz.arrive + k] = jnp.int32(sz.arrival[k])
    for m in range(sz.micro):
        total = counts[m, 0]
        for g in range(1, dp):
            total += counts[m, g]
        out[sz.count + m] = PIXELS * total
    for p in range(dp):
        out[sz.planes + p] = d ^ ((p % (dp // 2)) * 2 + p // (dp // 2))
    out[sz.planes + dp] = lax.div(c, ratio)
    out[sz.planes + dp + 1] = lax.rem(c, ratio)


def make_meta(sz, ring, dp, ratio, counts, other):
    smem = pl.BlockSpec(memory_space=pltpu.SMEM)
    return pl.pallas_call(
        functools.partial(meta_body, sz, dp, ratio),
        in_specs=[smem, smem, pl.BlockSpec(memory_space=pl.ANY)],
        out_specs=smem,
        out_shape=jax.ShapeDtypeStruct((sz.planes + dp + 2,), jnp.int32),
    )(counts, jnp.asarray(ring.table), other)


def to_padded(sz, native, padded):
    n = sz.images
    for q in range(native.shape[0]):
        for i in range(SIDE):
            for j in range(SIDE):
                at = (i * 8 + j) * n
                padded[at : at + n, q * 128 : (q + 1) * 128] = native[
                    q, pl.ds(i * SIDE + j, n, stride=PIXELS), :
                ]
    for i in range(SIDE):
        at = (i * 8 + 7) * n
        padded[at : at + n, :] = jnp.zeros((n, padded.shape[1]), F32)


def to_native(sz, padded, native, out):
    n = sz.images
    for q in range(native.shape[0]):
        for i in range(SIDE):
            for j in range(SIDE):
                at = (i * 8 + j) * n
                native[q, pl.ds(i * SIDE + j, n, stride=PIXELS), :] = padded[
                    at : at + n, q * 128 : (q + 1) * 128
                ]
        out[:, q * 128 : (q + 1) * 128] = native[q].astype(out.dtype)


def row_mask(sz, width, live):
    rows = lax.broadcasted_iota(jnp.int32, (sz.padded, width), 0)
    n = sz.images
    inside = lax.rem(lax.div(rows, n), 8) < SIDE
    if live is None:
        return inside
    return jnp.logical_and(inside, lax.rem(rows, n) < live)


def put_sums(stat, one, two):
    stat[0:1, :] = jnp.sum(one, axis=0, keepdims=True)
    stat[1:2, :] = jnp.sum(two, axis=0, keepdims=True)


def lay_taps(sz, value, strip, taps):
    n = sz.images
    width = strip.shape[1]
    strip[0 : 9 * n, :] = jnp.zeros((9 * n, width), F32)
    strip[65 * n : 74 * n, :] = jnp.zeros((9 * n, width), F32)
    strip[9 * n : 65 * n, :] = value
    for b in range(3):
        taps[b] = strip[b * n : b * n + 72 * n, :].astype(BF16)


def first_lead_body(meta, x, weight, low, high):
    value = jnp.dot(x[0], weight[...], preferred_element_type=F32).astype(BF16)
    half = low.shape[1]
    low[...] = value[:, :half]
    high[...] = value[:, half:]


def first_part_body(meta, x, weight, out):
    out[0] = jnp.dot(x[0], weight[...], preferred_element_type=F32).astype(BF16)


def first_body(sz, meta, f, b, own, pre, stat, native):
    split_lanes(f[...].astype(F32) + b[...].astype(F32) + own[0].astype(F32), native)
    to_padded(sz, native, pre)
    value = pre[...]
    kept = jnp.where(row_mask(sz, value.shape[1], meta[sz.live]), value, 0.0)
    put_sums(stat, kept, kept * kept)


def conv_body(
    sz, meta, pre, stat, params, weight, out, raw, stat_out, acted, strip, taps, total, native
):
    step = pl.program_id(0)
    n = sz.images
    width = pre.shape[1]

    @pl.when(step == 0)
    def _():
        average, inv = moments(stat[...], sz.own_count(meta))
        z = params[0:1] * ((pre[...] - average) * inv) + params[1:2]
        act = jnp.where(row_mask(sz, width, None), z * sigmoid(z), 0.0)
        acted[...] = act.astype(BF16)
        lay_taps(sz, act, strip, taps)
        total[...] = jnp.zeros_like(total)

    at = pl.multiple_of(step * 8 * n, 8 * n)
    for b in range(3):
        total[...] += jnp.dot(
            taps[b, pl.ds(at, sz.padded), :], weight[0, b], preferred_element_type=F32
        )

    @pl.when(step == 2)
    def _():
        value = jnp.where(row_mask(sz, width, None), total[...], 0.0)
        out[...] = value
        to_native(sz, total, native, raw)
        kept = jnp.where(row_mask(sz, width, meta[sz.live]), value, 0.0)
        put_sums(stat_out, kept, kept * kept)


def pick(sz, stat, batch):
    found = stat[0:2]
    for m in range(1, sz.micro):
        found = jnp.where(batch == m, stat[2 * m : 2 * m + 2], found)
    return found


def pick_count(sz, meta, batch):
    count = meta[sz.count]
    for m in range(1, sz.micro):
        count = jnp.where(batch == m, meta[sz.count + m], count)
    return count.astype(F32)


def add_sums(sz, stat, batch, one, two):
    sums = jnp.concatenate(
        [jnp.sum(one, axis=0, keepdims=True), jnp.sum(two, axis=0, keepdims=True)], axis=0
    )
    for m in range(sz.micro):
        stat[2 * m : 2 * m + 2, :] += jnp.where(batch == m, sums, 0.0)


def stage_piece(pieces, place, step):
    for k, piece in enumerate(pieces):

        @pl.when(step == k)
        def _(piece=piece):
            if len(piece) == 1:
                place[...] = piece[0][...]
            else:
                half = piece[0].shape[1]
                place[:, :half] = piece[0][...]
                place[:, half:] = piece[1][...]


def split_refs(layout, refs):
    pieces, at = [], 0
    for many in layout:
        pieces.append(refs[at : at + many])
        at += many
    return pieces, refs[at:]


def expand_body(sz, layout, offset, meta, *refs):
    pieces, rest = split_refs(layout, refs)
    stat, params, weight, act, pre, stat_out, place = rest
    step = pl.program_id(0)
    stage_piece(pieces, place, step)
    k = meta[sz.arrive + offset + step]
    batch = meta[sz.batch + k]
    average, inv = moments(pick(sz, stat[...], batch), pick_count(sz, meta, batch))
    z = params[2:3] * ((place[...].astype(F32) - average) * inv) + params[3:4]
    acted = (z * sigmoid(z)).astype(BF16)
    act[0] = acted
    value = jnp.dot(acted, weight[...], preferred_element_type=F32)
    pre[0] = value

    @pl.when(step == 0)
    def _():
        stat_out[...] = jnp.zeros_like(stat_out)

    rows = lax.broadcasted_iota(jnp.int32, value.shape, 0)
    kept = jnp.where(rows < PIXELS * meta[sz.live + k], value, 0.0)
    add_sums(sz, stat_out, batch, kept, kept * kept)


def out_body(sz, meta, pre, stat, params, x, cot, out, grad, stat_out):
    step = pl.program_id(0)
    batch = meta[sz.batch + step]
    average, inv = moments(pick(sz, stat[...], batch), pick_count(sz, meta, batch))
    normed = (pre[0] - average) * inv
    summed = params[0:1] * normed + params[1:2] + x[0].astype(F32)
    sigma = sigmoid(summed)
    rows = lax.broadcasted_iota(jnp.int32, summed.shape, 0)
    live = rows < PIXELS * meta[sz.live + step]
    out[0] = jnp.where(live, summed * sigma, 0.0)
    upstream = jnp.where(
        live, cot[0].astype(F32) * (sigma * (1.0 + summed * (1.0 - sigma))), 0.0
    )
    grad[0] = upstream

    @pl.when(step == 0)
    def _():
        stat_out[...] = jnp.zeros_like(stat_out)

    add_sums(sz, stat_out, batch, upstream, upstream * normed)


def shrink_body(sz, lead, meta, pre, stat, params, grad, sums, weight, back, *parts):
    if lead:
        k = sz.half
    else:
        step = pl.program_id(0)
        k = jnp.where(step < sz.half, step, step + 1)
    batch = meta[sz.batch + k]
    count = pick_count(sz, meta, batch)
    average, inv = moments(pick(sz, stat[...], batch), count)
    both = pick(sz, sums[...], batch)
    normed = (pre[0] - average) * inv
    rows = lax.broadcasted_iota(jnp.int32, normed.shape, 0)
    live = rows < PIXELS * meta[sz.live + k]
    value = params[0:1] * inv * (grad[0] - (both[0:1] + normed * both[1:2]) / count)
    value = jnp.where(live, value, 0.0).astype(BF16)
    back[0] = value
    part = lax.dot_general(
        value, weight[...], (((1,), (1,)), ((), ())), preferred_element_type=F32
    ).astype(BF16)
    if lead:
        half = part.shape[1] // 2
        parts[0][...] = part[:, :half]
        parts[1][...] = part[:, half:]
    else:
        parts[0][0] = part


def middle_up_body(sz, meta, f, b, own, pre, stat, params, up, stat_out, native, padded):
    split_lanes(f[...].astype(F32) + b[...].astype(F32) + own[0].astype(F32), native)
    to_padded(sz, native, padded)
    average, inv = moments(stat[...], sz.own_count(meta))
    normed = (pre[...] - average) * inv
    z = params[2:3] * normed + params[3:4]
    value = jnp.where(
        row_mask(sz, pre.shape[1], meta[sz.live]), padded[...] * silu_slope(z), 0.0
    )
    up[...] = value
    put_sums(stat_out, value, value * normed)


def conv_back_body(
    sz,
    meta,
    up,
    sums,
    pre_two,
    stat_two,
    pre_one,
    stat_one,
    params,
    weight,
    stay,
    send,
    up_one,
    stat_out,
    strip,
    taps,
    total,
):
    step = pl.program_id(0)
    n = sz.images
    width = up.shape[1]

    @pl.when(step == 0)
    def _():
        count = sz.own_count(meta)
        average, inv = moments(stat_two[...], count)
        normed = (pre_two[...] - average) * inv
        value = params[2:3] * inv * (up[...] - (sums[0:1] + normed * sums[1:2]) / count)
        value = jnp.where(row_mask(sz, width, meta[sz.live]), value, 0.0)
        half, _, lanes = stay.shape
        for p in range(2 * half):
            for plane in range(2 * half):

                @pl.when(meta[sz.planes + p] == plane)
                def _(p=p, plane=plane):
                    out = stay if p < half else send
                    out[p % half] = value[:, plane * lanes : (plane + 1) * lanes].astype(BF16)

        lay_taps(sz, value, strip, taps)
        total[...] = jnp.zeros_like(total)

    at = pl.multiple_of((2 - step) * 8 * n, 8 * n)
    for b in range(3):
        total[...] += lax.dot_general(
            taps[2 - b, pl.ds(at, sz.padded), :],
            weight[0, b],
            (((1,), (1,)), ((), ())),
            preferred_element_type=F32,
        )

    @pl.when(step == 2)
    def _():
        average, inv = moments(stat_one[...], sz.own_count(meta))
        normed = (pre_one[...] - average) * inv
        z = params[0:1] * normed + params[1:2]
        value = jnp.where(
            row_mask(sz, width, meta[sz.live]), total[...] * silu_slope(z), 0.0
        )
        up_one[...] = value
        put_sums(stat_out, value, value * normed)


def first_back_body(sz, meta, up, sums, pre, stat, params, back, padded, native):
    count = sz.own_count(meta)
    average, inv = moments(stat[...], count)
    normed = (pre[...] - average) * inv
    value = params[0:1] * inv * (up[...] - (sums[0:1] + normed * sums[1:2]) / count)
    padded[...] = jnp.where(row_mask(sz, pre.shape[1], meta[sz.live]), value, 0.0)
    to_native(sz, padded, native, back)


def input_body(sz, layout, more, meta, *refs):
    pieces, rest = split_refs(layout, refs)
    if more:
        grad, x, weight, had, out, grad_weight, place, total = rest
    else:
        grad, x, weight, out, grad_weight, place, total = rest
    step = pl.program_id(0)
    stage_piece(pieces, place, step)
    value = place[...]
    out[0] = grad[0] + lax.dot_general(
        value, weight[...], (((1,), (1,)), ((), ())), preferred_element_type=F32
    )

    @pl.when(step == 0)
    def _():
        total[...] = had[...] if more else jnp.zeros_like(total)

    total[...] += lax.dot_general(
        x[0], value, (((0,), (0,)), ((), ())), preferred_element_type=F32
    )

    @pl.when(step == len(layout) - 1)
    def _():
        grad_weight[...] = total[...].astype(grad_weight.dtype)


def middle_grad_body(sz, dp, meta, acts, backs, out, strip, taps, total):
    source = pl.program_id(0)
    n = sz.images
    lay_taps(sz, backs[0, 0].astype(F32), strip, taps)
    shifted = [
        taps[2 - b, (2 - a) * 8 * n : (2 - a) * 8 * n + sz.padded, :]
        for a in range(3)
        for b in range(3)
    ]

    @pl.when(source == 0)
    def _():
        total[...] = jnp.zeros_like(total)

    total[...] += lax.dot_general(
        acts[0],
        jnp.concatenate(shifted, axis=1),
        (((0,), (0,)), ((), ())),
        preferred_element_type=F32,
    )

    @pl.when(source == dp - 1)
    def _():
        depth, lanes = out.shape[1] // TAPS, out.shape[2]
        for k in range(sz.chunks):
            at = pl.multiple_of(meta[k] * depth, depth)
            for tap in range(TAPS):
                out[k, tap * depth : (tap + 1) * depth, :] = total[
                    pl.ds(at, depth), tap * lanes : (tap + 1) * lanes
                ].astype(BF16)


def assemble_body(sz, half, depth, meta, *refs):
    stacks, out = refs[:-1], refs[-1]
    early = sz.chunks - 3

    def fill(plane):
        for q, k in enumerate(sz.arrival):
            pieces = stacks[plane if q < early else half + plane]
            at = pl.multiple_of(meta[k] * depth, depth)
            for tap in range(TAPS):
                value = pieces[0, q if q < early else q - early, tap * depth : (tap + 1) * depth, :]
                if len(out.shape) == 3:
                    out[tap, pl.ds(at, depth), :] = value
                else:
                    out[0, tap, pl.ds(at, depth), :] = value

    for p in range(2 * half):

        @pl.when(pl.program_id(0) == p)
        def _(p=p):
            fill(p if p < half else half + p)


def prepare_body(weights, last, params, _, out):
    many, lanes = weights.shape
    out[:many, :] = weights[...].astype(BF16)
    depth = last.shape[0]
    for b in range(last.shape[1] // lanes):
        out[many + b * depth : many + (b + 1) * depth, :] = last[
            :, b * lanes : (b + 1) * lanes
        ].astype(BF16)
    value = params[...]
    count, width = value.shape
    one = value.astype(BF16)
    left = value - one.astype(F32)
    two = left.astype(BF16)
    three = (left - two.astype(F32)).astype(BF16)
    rest = jnp.zeros((16 - 3 * count, width), F32)
    rows = jnp.concatenate([part.astype(F32) for part in (one, two, three)] + [rest], axis=0)
    if width < lanes:
        rows = jnp.concatenate([rows, jnp.zeros((16, lanes - width), F32)], axis=1)
    out[out.shape[0] - 16 :, :] = rows.astype(BF16)


def last_assemble_body(meta, blocks, out):
    lanes = blocks.shape[3]
    for b in range(blocks.shape[1]):
        out[:, b * lanes : (b + 1) * lanes] = blocks[0, b]


def last_grad_body(sz, meta, act, back, out, total):
    step = pl.program_id(0)

    @pl.when(step == 0)
    def _():
        total[...] = jnp.zeros_like(total)

    total[...] += lax.dot_general(
        act[0], back[0], (((0,), (0,)), ((), ())), preferred_element_type=F32
    )

    @pl.when(step == sz.chunks - 1)
    def _():
        depth = out.shape[1]
        for k in range(sz.chunks):
            at = pl.multiple_of(meta[k] * depth, depth)
            out[k] = total[pl.ds(at, depth), :].astype(BF16)


def pieces_in(sz, pieces):
    ins, layout = [], []
    for piece in pieces:
        parts = piece if isinstance(piece, tuple) else (piece,)
        layout.append(len(parts))
        ins += [whole(p) for p in parts]
    return ins, layout


def local(
    dp,
    chan,
    inputs,
    cotangent,
    w_first,
    first_m,
    first_v,
    w_middle,
    middle_m,
    middle_v,
    w_last,
    last_m,
    last_v,
    mid_params,
    mid_m,
    mid_v,
    out_params,
    out_m,
    out_v,
    image_counts,
):
    ring = Ring(chan)
    d = lax.axis_index("dp")
    c = lax.axis_index("chan")
    micro, pixels, deep = inputs.shape
    images = micro * pixels // PIXELS // chan
    sz = Sizes(chan, micro, images)
    rows, padded = sz.rows, sz.padded
    per_batch = chan // micro
    depth, lanes = w_middle.shape[2], w_middle.shape[3]
    mid = depth * chan
    half = dp // 2
    last_blocks = w_last.shape[1] // lanes
    own_blocks = deep // lanes
    ratio = last_blocks // own_blocks


    dp_bits = bits_below(dp)
    wide_bits = dp_bits[1:]
    first = w_first.astype(BF16)
    first_stages = []
    for bit in dp_bits:
        other = swap(first, "dp", bit, dp)
        first_stages.append(other)
        first = jnp.where(
            (d & bit) == 0,
            jnp.concatenate([first, other], axis=1),
            jnp.concatenate([other, first], axis=1),
        )
    many = TAPS * depth
    tail_at = many + last_blocks * depth
    (payload,) = pl.pallas_call(
        prepare_body,
        in_specs=[pl.BlockSpec(memory_space=pltpu.VMEM)] * 3
        + [pl.BlockSpec(memory_space=pl.ANY)],
        out_specs=[pl.BlockSpec(memory_space=pltpu.VMEM)],
        out_shape=[jax.ShapeDtypeStruct((tail_at + 16, lanes), BF16)],
    )(w_middle.reshape(many, lanes), w_last, mid_params, first_stages[0])
    meta = make_meta(sz, ring, dp, ratio, image_counts, payload)
    at = meta[:chan]
    mids = Gather(ring, payload, 0)
    while mids.count < chan // 2:
        mids.step()

    x = inputs.reshape(chan, rows, deep)
    cot = cotangent.reshape(chan, rows, deep)

    def at_place(k, meta):
        return (meta[k], 0, 0)

    def in_order(k, meta):
        return (k, 0, 0)

    opposite = chan // 2

    def skipping(k, meta):
        return (jnp.where(k < opposite, k, k + 1), 0, 0)

    def skipping_at(k, meta):
        return (meta[jnp.where(k < opposite, k, k + 1)], 0, 0)

    low, high = run(
        first_lead_body,
        meta,
        (1,),
        [(x, (1, rows, deep), lambda k, meta: (meta[opposite], 0, 0)), whole(first)],
        [whole_out((rows, mid // 2), BF16), whole_out((rows, mid // 2), BF16)],
    )
    (parts,) = run(
        first_part_body,
        meta,
        (chan - 1,),
        [(x, (1, rows, deep), skipping_at), whole(first)],
        [((chan, rows, mid), BF16, (1, rows, mid), skipping)],
        cost=(2 * chan * rows * deep * mid, 2 * chan * rows * (deep + mid)),
    )
    sums = Scatter(ring, low, high, lambda k: parts[k], 1)
    while sums.count < opposite:
        sums.step()
    f, b = sums.f, sums.b

    came = [jnp.concatenate(p, axis=0) if isinstance(p, tuple) else p for p in mids.pieces]
    tails = jnp.stack([p[many:] for p in came])
    near, far = [], []
    for group in (sz.arrival[: chan - 3], sz.arrival[chan - 3 :]):
        stack = jnp.stack([came[k][:many] for k in group])[None]
        planes = [stack]
        for bit in wide_bits:
            planes += [swap(p, "dp", bit, dp) for p in planes]
        near.append(planes)
        far.append([swap(p, "dp", 1, dp) for p in planes])
    near = [near[g][q] for g in range(2) for q in range(half)]
    far = [far[g][q] for g in range(2) for q in range(half)]
    if lanes % 128 == 0:
        placed = ((TAPS, mid, mid), BF16, (TAPS, mid, lanes), lambda p, meta: (0, 0, meta[sz.planes + p]))
    else:
        placed = (
            (dp, TAPS, mid, lanes),
            BF16,
            (1, TAPS, mid, lanes),
            lambda p, meta: (meta[sz.planes + p], 0, 0, 0),
        )
    (middle,) = run(
        functools.partial(assemble_body, sz, half, depth),
        meta,
        (dp,),
        [whole(p) for p in near + far],
        [placed],
    )
    here = (at[None, :] == jnp.arange(chan)[:, None])[:, :, None, None]
    tail = tails[:, last_blocks * depth :, :depth].astype(F32)
    tail = (tail[:, 8:12] + tail[:, 4:8]) + tail[:, 0:4]
    params = jnp.sum(jnp.where(here, tail[None], 0.0), axis=1)
    params = params.transpose(1, 0, 2).reshape(4, mid)
    if lanes % 128 != 0:
        middle = middle.transpose(1, 2, 0, 3)
    middle = middle.reshape(3, 3, mid, mid)
    lasts = tails[:, : last_blocks * depth].reshape(chan, ratio, own_blocks, depth, lanes)
    own_last = lax.dynamic_index_in_dim(lasts, c % ratio, axis=1, keepdims=False)
    found = jnp.where(d == c // ratio, own_last, jnp.zeros_like(own_last))
    for shift in range(1, dp):
        moves = [
            ((k // ratio) * chan + k, ((k // ratio) ^ shift) * chan + k) for k in range(chan)
        ]
        found = found + lax.ppermute(own_last, ("dp", "chan"), moves)
    (last,) = run(
        last_assemble_body,
        meta,
        (chan,),
        [(found, (1, own_blocks, depth, lanes), lambda k, meta: (k, 0, 0, 0))],
        [((mid, deep), BF16, (depth, deep), lambda k, meta: (meta[k], 0))],
    )

    def head(stack):
        return (stack, (1,) + stack.shape[1:], lambda *_: (0, 0, 0))

    stat_bits = [k for k in bits_below(chan) if k < per_batch]

    def total_rows(stat):
        return sum_over(sum_over(stat, "dp", dp_bits, dp), "chan", stat_bits, chan)

    def all_batches(stat):
        for bit in bits_below(chan):
            if bit >= per_batch:
                other = swap(stat, "chan", bit, chan)
                stat = jnp.where(
                    (c & bit) == 0,
                    jnp.concatenate([stat, other], axis=0),
                    jnp.concatenate([other, stat], axis=0),
                )
        return stat

    pre_one, stat_one = run(
        functools.partial(first_body, sz),
        meta,
        (1,),
        [whole(f), whole(b), head(parts)],
        [whole_out((padded, mid), F32), whole_out((2, mid), F32)],
        [pltpu.VMEM((mid // 128, rows, 128), F32)],
        vmem=VMEM,
        cost=(10 * padded * mid, 10 * padded * mid),
    )
    stat_one = total_rows(stat_one)

    tap_block = (1, 3, mid, mid)
    conv_flops = 2 * TAPS * padded * mid * mid
    conv_bytes = 2 * TAPS * mid * mid + 16 * padded * mid
    pre_two, raw, stat_two, acted = run(
        functools.partial(conv_body, sz),
        meta,
        (3,),
        [
            whole(pre_one),
            whole(stat_one),
            whole(params),
            (middle, tap_block, lambda s, meta: (s, 0, 0, 0)),
        ],
        [
            whole_out((padded, mid), F32),
            whole_out((rows, mid), BF16),
            whole_out((2, mid), F32),
            whole_out((padded, mid), BF16),
        ],
        [
            pltpu.VMEM((74 * images, mid), F32),
            pltpu.VMEM((3, 72 * images, mid), BF16),
            pltpu.VMEM((padded, mid), F32),
            pltpu.VMEM((mid // 128, rows, 128), F32),
        ],
        vmem=VMEM,
        cost=(conv_flops, conv_bytes),
    )
    gather = Gather(ring, raw, 1)
    gather.step()
    stat_two = sum_over(stat_two, "chan", stat_bits[:1], chan)
    gather.step(stat_two)
    stat_two = sum_over(stat_two, "dp", dp_bits, dp)
    if gather.count < opposite - 1:
        gather.step(stat_two)
    stat_two = sum_over(stat_two, "chan", stat_bits[1:], chan)
    stats_two = all_batches(stat_two)
    while gather.count < opposite - 1:
        gather.step()
    gather.step(stats_two)
    pieces = gather.pieces
    order = [1] + wide_bits[::-1]
    acts = acted[None]
    for bit in order:
        acts = jnp.concatenate([acts, swap(acts, "dp", bit, dp)], axis=0)

    def expand(start, steps, into):
        ins, layout = pieces_in(sz, [pieces[k] for k in sz.arrival[start : start + steps]])

        def arrived(k, meta):
            return (meta[sz.arrive + start + k], 0, 0)

        return run(
            functools.partial(expand_body, sz, layout, start),
            meta,
            (steps,),
            ins + [whole(stats_two), whole(params), whole(last)],
            [
                ((chan, rows, mid), BF16, (1, rows, mid), arrived),
                ((chan, rows, deep), F32, (1, rows, deep), arrived),
                whole_out((2 * micro, deep), F32),
            ],
            [pltpu.VMEM((rows, mid), BF16)],
            vmem=VMEM,
            cost=(2 * steps * rows * deep * mid, steps * rows * (4 * mid + 4 * deep)),
            into=into,
        )

    early = chan - 3
    act, pre_three, stat_early = expand(0, early, [])
    act, pre_three, stat_late = expand(early, 3, [act, pre_three])
    stat_three = stat_early + stat_late
    stat_three = sum_over(stat_three, "dp", bits_below(dp), dp)
    block_out, grad_summed, sums_three = run(
        functools.partial(out_body, sz),
        meta,
        (chan,),
        [
            (pre_three, (1, rows, deep), in_order),
            whole(stat_three),
            whole(out_params),
            (x, (1, rows, deep), at_place),
            (cot, (1, rows, deep), at_place),
        ],
        [
            ((chan, rows, deep), F32, (1, rows, deep), at_place),
            ((chan, rows, deep), F32, (1, rows, deep), in_order),
            whole_out((2 * micro, deep), F32),
        ],
        vmem=VMEM,
        cost=(20 * chan * rows * deep, 16 * chan * rows * deep),
    )
    sums_three = sum_over(sums_three, "dp", bits_below(dp), dp)

    def shrink(steps, place, into, lead):
        if lead:
            made = [whole_out((rows, mid // 2), BF16), whole_out((rows, mid // 2), BF16)]
        else:
            made = [((chan, rows, mid), BF16, (1, rows, mid), place)]
        return run(
            functools.partial(shrink_body, sz, lead),
            meta,
            (steps,),
            [
                (pre_three, (1, rows, deep), place),
                whole(stat_three),
                whole(out_params),
                (grad_summed, (1, rows, deep), place),
                whole(sums_three),
                whole(last),
            ],
            [((chan, rows, deep), BF16, (1, rows, deep), place)] + made,
            vmem=VMEM,
            cost=(2 * steps * rows * deep * mid, steps * rows * (2 * mid + 10 * deep)),
            into=into,
        )

    back_last, low, high = shrink(1, lambda k, meta: (opposite, 0, 0), [], True)
    back_last, back_parts = shrink(chan - 1, skipping, [back_last], False)
    sums = Scatter(ring, low, high, lambda k: back_parts[k], 1)
    while sums.count < opposite:
        sums.step()
    f, b = sums.f, sums.b
    (grad_last,) = run(
        functools.partial(last_grad_body, sz),
        meta,
        (chan,),
        [(act, (1, rows, mid), in_order), (back_last, (1, rows, deep), in_order)],
        [whole_out((chan, depth, deep), BF16)],
        [pltpu.VMEM((mid, deep), F32)],
        cost=(2 * chan * rows * deep * mid, 2 * chan * rows * (mid + deep)),
    )
    for bit in dp_bits:
        grad_last = add16(grad_last, swap(grad_last, "dp", bit, dp))
    held = [
        jnp.where(c % ratio == r, grad_last, jnp.zeros_like(grad_last)) for r in range(ratio)
    ]
    held = jnp.concatenate(held, axis=2)
    held = jnp.where(d == c // ratio, held, jnp.zeros_like(held))
    cut = held.shape[2] // 2
    last_sums = Scatter(
        ring, held[opposite, :, :cut], held[opposite, :, cut:], lambda k: held[k], 1
    )
    while last_sums.count < opposite:
        last_sums.step()
    owned_last = held[0].astype(F32) + last_sums.f.astype(F32) + last_sums.b.astype(F32)

    up_two, sums_two = run(
        functools.partial(middle_up_body, sz),
        meta,
        (1,),
        [
            whole(f),
            whole(b),
            head(back_parts),
            whole(pre_two),
            whole(stat_two),
            whole(params),
        ],
        [whole_out((padded, mid), F32), whole_out((2, mid), F32)],
        [pltpu.VMEM((mid // 128, rows, 128), F32), pltpu.VMEM((padded, mid), F32)],
        vmem=VMEM,
        cost=(20 * padded * mid, 14 * padded * mid),
    )
    sums_two = total_rows(sums_two)
    stay, send, up_one, sums_one = run(
        functools.partial(conv_back_body, sz),
        meta,
        (3,),
        [
            whole(up_two),
            whole(sums_two),
            whole(pre_two),
            whole(stat_two),
            whole(pre_one),
            whole(stat_one),
            whole(params),
            (middle, tap_block, lambda s, meta: (s, 0, 0, 0)),
        ],
        [
            whole_out((half, padded, lanes), BF16),
            whole_out((half, padded, lanes), BF16),
            whole_out((padded, mid), F32),
            whole_out((2, mid), F32),
        ],
        [
            pltpu.VMEM((74 * images, mid), F32),
            pltpu.VMEM((3, 72 * images, mid), BF16),
            pltpu.VMEM((padded, mid), F32),
        ],
        vmem=VMEM,
        cost=(conv_flops, conv_bytes),
    )

    sums_one = total_rows(sums_one)
    (back_one,) = run(
        functools.partial(first_back_body, sz),
        meta,
        (1,),
        [whole(up_one), whole(sums_one), whole(pre_one), whole(stat_one), whole(params)],
        [whole_out((rows, mid), BF16)],
        [pltpu.VMEM((padded, mid), F32), pltpu.VMEM((mid // 128, rows, 128), F32)],
        cost=(10 * padded * mid, 10 * padded * mid),
    )
    gather = Gather(ring, back_one, 1)
    while gather.count < opposite:
        gather.step()
    pieces = gather.pieces

    backs = jnp.stack([stay, swap(send, "dp", 1, dp)])
    for bit in wide_bits[::-1]:
        cut = backs.shape[1] // 2
        backs = jnp.concatenate(
            [backs[:, :cut], swap(backs[:, cut:], "dp", bit, dp)], axis=0
        )
    (grad_middle,) = run(
        functools.partial(middle_grad_body, sz, dp),
        meta,
        (dp,),
        [
            (acts, (1, padded, mid), lambda r, meta: (r, 0, 0)),
            (backs, (1, 1, padded, lanes), lambda r, meta: (r, 0, 0, 0)),
        ],
        [whole_out((chan, TAPS * depth, lanes), BF16)],
        [
            pltpu.VMEM((74 * images, lanes), F32),
            pltpu.VMEM((3, 72 * images, lanes), BF16),
            pltpu.VMEM((mid, TAPS * lanes), F32),
        ],
        cost=(conv_flops, conv_bytes),
        after=[back_one],
    )
    cut = TAPS * depth // 2
    middle_sums = Scatter(
        ring,
        grad_middle[opposite, :cut],
        grad_middle[opposite, cut:],
        lambda k: grad_middle[k],
        0,
    )
    middle_steps = [middle_sums.f]
    while middle_sums.count < opposite:
        middle_sums.step()
        middle_steps.append(middle_sums.f)
    owned_middle = (
        grad_middle[0].astype(F32) + middle_sums.f.astype(F32) + middle_sums.b.astype(F32)
    ).reshape(3, 3, depth, lanes)

    def input_back(start, steps, had, into, after):
        ins, layout = pieces_in(sz, [pieces[k] for k in sz.arrival[start : start + steps]])
        done = start + steps == chan

        def arrived(k, meta):
            return (meta[sz.arrive + start + k], 0, 0)

        def arrived_at(k, meta):
            return (meta[meta[sz.arrive + start + k]], 0, 0)

        return run(
            functools.partial(input_body, sz, layout, bool(had)),
            meta,
            (steps,),
            ins
            + [
                (grad_summed, (1, rows, deep), arrived),
                (x, (1, rows, deep), arrived_at),
                whole(first),
            ]
            + [whole(h) for h in had],
            [
                ((chan, rows, deep), F32, (1, rows, deep), arrived_at),
                whole_out((deep, mid), BF16 if done else F32),
            ],
            [pltpu.VMEM((rows, mid), BF16), pltpu.VMEM((deep, mid), F32)],
            vmem=VMEM,
            cost=(4 * steps * rows * deep * mid, steps * rows * (2 * mid + 10 * deep)),
            into=into,
            after=after,
        )

    input_grad, grad_early = input_back(0, early, [], [], middle_steps[1:2])
    input_grad, grad_first = input_back(early, 3, [grad_early], [input_grad], middle_steps[2:3])
    owned_first = scatter_columns(grad_first, d, dp)

    sums_first, sums_middle = all_batches(sums_one), all_batches(sums_two)

    def over_batches(stat, row):
        total = stat[row]
        for m in range(1, micro):
            total = total + stat[2 * m + row]
        return total

    grad_mid = jnp.stack(
        [
            over_batches(sums_first, 1),
            over_batches(sums_first, 0),
            over_batches(sums_middle, 1),
            over_batches(sums_middle, 0),
        ]
    )
    grad_mid = lax.dynamic_slice_in_dim(grad_mid, c * depth, depth, axis=1)
    grad_out = jnp.stack([over_batches(sums_three, 1), over_batches(sums_three, 0)])

    return (
        block_out.reshape(inputs.shape),
        input_grad.reshape(inputs.shape),
        *adamw(w_first, owned_first, first_m, first_v, rate_first),
        *adamw(w_middle, owned_middle, middle_m, middle_v, rate_middle),
        *adamw(w_last, owned_last, last_m, last_v, rate_last),
        *adamw(mid_params, grad_mid, mid_m, mid_v, rate_norm),
        *adamw(out_params, grad_out, out_m, out_v, rate_norm),
    )


def scatter_columns(grad, d, dp):
    blocks = grad.reshape(grad.shape[0], dp, grad.shape[1] // dp)
    kept = [blocks[:, p] for p in range(dp)]
    for bit in bits_below(dp):
        kept = [
            jnp.where((d & bit) == 0, kept[q], kept[q ^ bit]) for q in range(len(kept))
        ]
    todo = {q: kept[q] for q in range(dp)}
    for bit in [1] + bits_below(dp)[:0:-1]:
        send = sorted(q for q in todo if q & bit)
        stay = sorted(q for q in todo if not q & bit)
        got = swap(jnp.stack([todo[q] for q in send]), "dp", bit, dp)
        todo = {
            q: todo[q].astype(F32) + got[send.index(q | bit)].astype(F32) for q in stay
        }
        if len(todo) > 1:
            todo = {q: v.astype(BF16) for q, v in todo.items()}
    return todo[0]


def solution(mesh):
    rows = P(None, "dp", "chan")
    flat = P("chan", "dp")
    square = P(None, None, "chan", "dp")
    vector = P(None, "chan")
    state = (flat,) * 3 + (square,) * 3 + (flat,) * 3 + (vector,) * 6
    return jax.shard_map(
        functools.partial(local, mesh.shape["dp"], mesh.shape["chan"]),
        mesh=mesh,
        in_specs=(rows, rows) + state + (P(),),
        out_specs=(rows, rows) + state,
        check_vma=False,
    )
```

```python
import functools

import jax
import jax.numpy as jnp
import numpy as np
from jax import lax
from jax.experimental import pallas as pl
from jax.experimental.pallas import tpu as pltpu
from jax.sharding import PartitionSpec as P

STEPS = 5
SIDE = 7
PIXELS = SIDE * SIDE
TAPS = 9
VMEM = 24
F32 = jnp.float32
BF16 = jnp.bfloat16

norm_eps = 1e-05
adam_eps = 1e-08
adam_beta = 0.5
decay_rate = 0.05
rate_first = 0.02
rate_middle = 0.015
rate_last = 0.04
rate_norm = 0.25


def sigmoid(value):
    return 0.5 * jnp.tanh(0.5 * value) + 0.5


def silu_slope(value):
    sigma = sigmoid(value)
    return sigma * (1.0 + value * (1.0 - sigma))


def moments(stat, count):
    average = stat[0:1] / count
    variance = stat[1:2] / count - average * average
    return average, lax.rsqrt(variance + norm_eps)


def adamw(weight, gradient, moment_one, moment_two, step_rate):
    one_new = adam_beta * moment_one + (1.0 - adam_beta) * gradient
    two_new = adam_beta * moment_two + (1.0 - adam_beta) * gradient * gradient
    correct = 1.0 - adam_beta**STEPS
    weight_new = weight - step_rate * (
        one_new / correct / (jnp.sqrt(two_new / correct) + adam_eps) + decay_rate * weight
    )
    return (weight_new, one_new, two_new)


def ring_of(size):
    across = max(size // 4, 1)
    along = size // across
    order = [(z, 0) for z in range(along)]
    outward = True
    for z in reversed(range(along)):
        steps = list(range(1, across))
        order += [(z, x) for x in (steps if outward else steps[::-1])]
        outward = not outward
    return [z * across + x for z, x in order]


class Ring:
    def __init__(self, size):
        self.size = size
        self.order = ring_of(size)
        ahead = [(self.order[i], self.order[(i + 1) % size]) for i in range(size)]
        self.ahead = ahead
        self.back = [(b, a) for a, b in ahead]
        place = np.argsort(np.array(self.order))
        self.table = np.array(
            [[self.order[(place[c] + k) % size] for k in range(size)] for c in range(size)],
            np.int32,
        )

    def fw(self, x):
        return lax.ppermute(x, "chan", self.ahead)

    def bw(self, x):
        return lax.ppermute(x, "chan", self.back)


def tie(x, other):
    first = lax.slice(other, (0,) * other.ndim, (1,) * other.ndim).reshape(())
    return jnp.where(first > -3e38, x, jnp.zeros_like(x))


def beside(x, other):
    return jnp.where(other > -3e38, x, jnp.zeros_like(x))


class Gather:
    def __init__(self, ring, x, axis):
        self.ring, self.axis, self.half = ring, axis, x.shape[axis] // 2
        self.pieces = [x] + [None] * (ring.size - 1)
        self.count = 0

    def step(self, other=None):
        ring, size = self.ring, self.ring.size
        a, b = self.pieces[(size - self.count) % size], self.pieces[self.count]
        if other is not None:
            a, b = tie(a, other), tie(b, other)
        self.count += 1
        if self.count < size // 2:
            got = [ring.fw(a), ring.bw(b)]
            self.pieces[size - self.count], self.pieces[self.count] = got
        else:
            got = [
                ring.fw(lax.slice_in_dim(a, 0, self.half, axis=self.axis)),
                ring.bw(lax.slice_in_dim(b, self.half, b.shape[self.axis], axis=self.axis)),
            ]
            self.pieces[size // 2] = tuple(got)
        return got


class Scatter:
    def __init__(self, ring, low, high, part, axis):
        self.ring, self.part, self.axis = ring, part, axis
        self.f, self.b = ring.fw(low), ring.bw(high)
        self.count = 1

    def step(self):
        size, axis = self.ring.size, self.axis
        k = size // 2 - self.count
        left, right = self.part(k), self.part(size - k)
        if self.count == 1:
            width = left.shape[axis]
            half = width // 2
            f = jnp.concatenate(
                [
                    beside(add16(lax.slice_in_dim(left, 0, half, axis=axis), self.f), self.b),
                    lax.slice_in_dim(left, half, width, axis=axis),
                ],
                axis,
            )
            b = jnp.concatenate(
                [
                    lax.slice_in_dim(right, 0, half, axis=axis),
                    beside(add16(lax.slice_in_dim(right, half, width, axis=axis), self.b), self.f),
                ],
                axis,
            )
        else:
            f = beside(add16(left, self.f), self.b)
            b = beside(add16(right, self.b), self.f)
        self.count += 1
        self.f, self.b = self.ring.fw(f), self.ring.bw(b)


def add16(one, two):
    return (one.astype(F32) + two.astype(F32)).astype(BF16)


def swap(x, axis, bit, size):
    return lax.ppermute(x, axis, [(i, i ^ bit) for i in range(size)])


def bits_below(size):
    return [1 << k for k in range(size.bit_length() - 1)]


def sum_over(x, axis, bits, size):
    for bit in bits:
        x = x + swap(x, axis, bit, size)
    return x


def run(body, meta, grid, ins, outs, scratch=(), vmem=VMEM, cost=None, after=(), into=()):
    extra = list(into) + list(after)
    first, last = len(ins), len(ins) + len(extra)

    def kernel(meta, *refs):
        body(meta, *refs[:first], *refs[last:])

    return pl.pallas_call(
        kernel if extra else body,
        grid_spec=pltpu.PrefetchScalarGridSpec(
            num_scalar_prefetch=1,
            grid=grid,
            in_specs=[pl.BlockSpec(b, m) for _, b, m in ins]
            + [pl.BlockSpec(memory_space=pl.ANY)] * len(extra),
            out_specs=[pl.BlockSpec(b, m) for _, _, b, m in outs],
            scratch_shapes=list(scratch),
        ),
        out_shape=[jax.ShapeDtypeStruct(s, d) for s, d, _, _ in outs],
        compiler_params=pltpu.CompilerParams(vmem_limit_bytes=vmem << 20),
        cost_estimate=pl.CostEstimate(
            flops=cost[0], bytes_accessed=cost[1], transcendentals=0
        )
        if cost
        else None,
        input_output_aliases={1 + first + q: q for q in range(len(into))},
    )(meta, *[a for a, _, _ in ins], *extra)


def whole(x):
    zeros = (0,) * x.ndim
    return (x, x.shape, lambda *_: zeros)


def whole_out(shape, dtype):
    zeros = (0,) * len(shape)
    return (shape, dtype, shape, lambda *_: zeros)


class Sizes:
    def __init__(self, chunks, micro, images):
        self.chunks = chunks
        self.half = chunks // 2
        self.micro = micro
        self.images = images
        self.rows = PIXELS * images
        self.padded = SIDE * 8 * images
        self.live = chunks
        self.batch = 2 * chunks
        self.count = 3 * chunks
        self.arrive = 3 * chunks + micro
        self.planes = 4 * chunks + micro
        self.arrival = [0]
        for step in range(1, chunks // 2):
            self.arrival += [chunks - step, step]
        self.arrival.append(chunks // 2)

    def own_count(self, meta):
        batch = meta[self.batch]
        count = meta[self.count]
        for m in range(1, self.micro):
            count = jnp.where(batch == m, meta[self.count + m], count)
        return count.astype(F32)


def split_lanes(value, native):
    for q in range(native.shape[0]):
        native[q] = value[:, q * 128 : (q + 1) * 128]


def meta_body(sz, dp, ratio, counts, table, _, out):
    d, c = lax.axis_index("dp"), lax.axis_index("chan")
    per_batch = sz.chunks // sz.micro
    for k in range(sz.chunks):
        chunk = table[c, k]
        batch = lax.div(chunk, per_batch)
        have = counts[batch, d] - sz.images * lax.rem(chunk, per_batch)
        out[k] = chunk
        out[sz.live + k] = jnp.minimum(jnp.maximum(have, 0), sz.images)
        out[sz.batch + k] = batch
        out[sz.arrive + k] = jnp.int32(sz.arrival[k])
    for m in range(sz.micro):
        total = counts[m, 0]
        for g in range(1, dp):
            total += counts[m, g]
        out[sz.count + m] = PIXELS * total
    for p in range(dp):
        out[sz.planes + p] = d ^ ((p % (dp // 2)) * 2 + p // (dp // 2))
    out[sz.planes + dp] = lax.div(c, ratio)
    out[sz.planes + dp + 1] = lax.rem(c, ratio)


def make_meta(sz, ring, dp, ratio, counts, other):
    smem = pl.BlockSpec(memory_space=pltpu.SMEM)
    return pl.pallas_call(
        functools.partial(meta_body, sz, dp, ratio),
        in_specs=[smem, smem, pl.BlockSpec(memory_space=pl.ANY)],
        out_specs=smem,
        out_shape=jax.ShapeDtypeStruct((sz.planes + dp + 2,), jnp.int32),
    )(counts, jnp.asarray(ring.table), other)


def to_padded(sz, native, padded):
    n = sz.images
    for q in range(native.shape[0]):
        for i in range(SIDE):
            for j in range(SIDE):
                at = (i * 8 + j) * n
                padded[at : at + n, q * 128 : (q + 1) * 128] = native[
                    q, pl.ds(i * SIDE + j, n, stride=PIXELS), :
                ]
    for i in range(SIDE):
        at = (i * 8 + 7) * n
        padded[at : at + n, :] = jnp.zeros((n, padded.shape[1]), F32)


def to_native(sz, padded, native, out):
    n = sz.images
    for q in range(native.shape[0]):
        for i in range(SIDE):
            for j in range(SIDE):
                at = (i * 8 + j) * n
                native[q, pl.ds(i * SIDE + j, n, stride=PIXELS), :] = padded[
                    at : at + n, q * 128 : (q + 1) * 128
                ]
        out[:, q * 128 : (q + 1) * 128] = native[q].astype(out.dtype)


def row_mask(sz, width, live):
    rows = lax.broadcasted_iota(jnp.int32, (sz.padded, width), 0)
    n = sz.images
    inside = lax.rem(lax.div(rows, n), 8) < SIDE
    if live is None:
        return inside
    return jnp.logical_and(inside, lax.rem(rows, n) < live)


def put_sums(stat, one, two):
    stat[0:1, :] = jnp.sum(one, axis=0, keepdims=True)
    stat[1:2, :] = jnp.sum(two, axis=0, keepdims=True)


def lay_taps(sz, value, strip, taps):
    n = sz.images
    width = strip.shape[1]
    strip[0 : 9 * n, :] = jnp.zeros((9 * n, width), F32)
    strip[65 * n : 74 * n, :] = jnp.zeros((9 * n, width), F32)
    strip[9 * n : 65 * n, :] = value
    for b in range(3):
        taps[b] = strip[b * n : b * n + 72 * n, :].astype(BF16)


def first_lead_body(meta, x, weight, low, high):
    value = jnp.dot(x[0], weight[...], preferred_element_type=F32).astype(BF16)
    half = low.shape[1]
    low[...] = value[:, :half]
    high[...] = value[:, half:]


def first_part_body(meta, x, weight, out):
    out[0] = jnp.dot(x[0], weight[...], preferred_element_type=F32).astype(BF16)


def first_body(sz, meta, f, b, own, pre, stat, native):
    split_lanes(f[...].astype(F32) + b[...].astype(F32) + own[0].astype(F32), native)
    to_padded(sz, native, pre)
    value = pre[...]
    kept = jnp.where(row_mask(sz, value.shape[1], meta[sz.live]), value, 0.0)
    put_sums(stat, kept, kept * kept)


def conv_body(
    sz, meta, pre, stat, params, weight, out, raw, stat_out, acted, strip, taps, total, native
):
    step = pl.program_id(0)
    n = sz.images
    width = pre.shape[1]

    @pl.when(step == 0)
    def _():
        average, inv = moments(stat[...], sz.own_count(meta))
        z = params[0:1] * ((pre[...] - average) * inv) + params[1:2]
        act = jnp.where(row_mask(sz, width, None), z * sigmoid(z), 0.0)
        acted[...] = act.astype(BF16)
        lay_taps(sz, act, strip, taps)
        total[...] = jnp.zeros_like(total)

    at = pl.multiple_of(step * 8 * n, 8 * n)
    for b in range(3):
        total[...] += jnp.dot(
            taps[b, pl.ds(at, sz.padded), :], weight[0, b], preferred_element_type=F32
        )

    @pl.when(step == 2)
    def _():
        value = jnp.where(row_mask(sz, width, None), total[...], 0.0)
        out[...] = value
        to_native(sz, total, native, raw)
        kept = jnp.where(row_mask(sz, width, meta[sz.live]), value, 0.0)
        put_sums(stat_out, kept, kept * kept)


def pick(sz, stat, batch):
    found = stat[0:2]
    for m in range(1, sz.micro):
        found = jnp.where(batch == m, stat[2 * m : 2 * m + 2], found)
    return found


def pick_count(sz, meta, batch):
    count = meta[sz.count]
    for m in range(1, sz.micro):
        count = jnp.where(batch == m, meta[sz.count + m], count)
    return count.astype(F32)


def add_sums(sz, stat, batch, one, two):
    sums = jnp.concatenate(
        [jnp.sum(one, axis=0, keepdims=True), jnp.sum(two, axis=0, keepdims=True)], axis=0
    )
    for m in range(sz.micro):
        stat[2 * m : 2 * m + 2, :] += jnp.where(batch == m, sums, 0.0)


def stage_piece(pieces, place, step):
    for k, piece in enumerate(pieces):

        @pl.when(step == k)
        def _(piece=piece):
            if len(piece) == 1:
                place[...] = piece[0][...]
            else:
                half = piece[0].shape[1]
                place[:, :half] = piece[0][...]
                place[:, half:] = piece[1][...]


def split_refs(layout, refs):
    pieces, at = [], 0
    for many in layout:
        pieces.append(refs[at : at + many])
        at += many
    return pieces, refs[at:]


def expand_body(sz, layout, offset, meta, *refs):
    pieces, rest = split_refs(layout, refs)
    stat, params, weight, act, pre, stat_out, place = rest
    step = pl.program_id(0)
    stage_piece(pieces, place, step)
    k = meta[sz.arrive + offset + step]
    batch = meta[sz.batch + k]
    average, inv = moments(pick(sz, stat[...], batch), pick_count(sz, meta, batch))
    z = params[2:3] * ((place[...].astype(F32) - average) * inv) + params[3:4]
    acted = (z * sigmoid(z)).astype(BF16)
    act[0] = acted
    value = jnp.dot(acted, weight[...], preferred_element_type=F32)
    pre[0] = value

    @pl.when(step == 0)
    def _():
        stat_out[...] = jnp.zeros_like(stat_out)

    rows = lax.broadcasted_iota(jnp.int32, value.shape, 0)
    kept = jnp.where(rows < PIXELS * meta[sz.live + k], value, 0.0)
    add_sums(sz, stat_out, batch, kept, kept * kept)


def out_body(sz, meta, pre, stat, params, x, cot, out, grad, stat_out):
    step = pl.program_id(0)
    batch = meta[sz.batch + step]
    average, inv = moments(pick(sz, stat[...], batch), pick_count(sz, meta, batch))
    normed = (pre[0] - average) * inv
    summed = params[0:1] * normed + params[1:2] + x[0].astype(F32)
    sigma = sigmoid(summed)
    rows = lax.broadcasted_iota(jnp.int32, summed.shape, 0)
    live = rows < PIXELS * meta[sz.live + step]
    out[0] = jnp.where(live, summed * sigma, 0.0)
    upstream = jnp.where(
        live, cot[0].astype(F32) * (sigma * (1.0 + summed * (1.0 - sigma))), 0.0
    )
    grad[0] = upstream

    @pl.when(step == 0)
    def _():
        stat_out[...] = jnp.zeros_like(stat_out)

    add_sums(sz, stat_out, batch, upstream, upstream * normed)


def shrink_body(sz, lead, meta, pre, stat, params, grad, sums, weight, back, *parts):
    if lead:
        k = sz.half
    else:
        step = pl.program_id(0)
        k = jnp.where(step < sz.half, step, step + 1)
    batch = meta[sz.batch + k]
    count = pick_count(sz, meta, batch)
    average, inv = moments(pick(sz, stat[...], batch), count)
    both = pick(sz, sums[...], batch)
    normed = (pre[0] - average) * inv
    rows = lax.broadcasted_iota(jnp.int32, normed.shape, 0)
    live = rows < PIXELS * meta[sz.live + k]
    value = params[0:1] * inv * (grad[0] - (both[0:1] + normed * both[1:2]) / count)
    value = jnp.where(live, value, 0.0).astype(BF16)
    back[0] = value
    part = lax.dot_general(
        value, weight[...], (((1,), (1,)), ((), ())), preferred_element_type=F32
    ).astype(BF16)
    if lead:
        half = part.shape[1] // 2
        parts[0][...] = part[:, :half]
        parts[1][...] = part[:, half:]
    else:
        parts[0][0] = part


def middle_up_body(sz, meta, f, b, own, pre, stat, params, up, stat_out, native, padded):
    split_lanes(f[...].astype(F32) + b[...].astype(F32) + own[0].astype(F32), native)
    to_padded(sz, native, padded)
    average, inv = moments(stat[...], sz.own_count(meta))
    normed = (pre[...] - average) * inv
    z = params[2:3] * normed + params[3:4]
    value = jnp.where(
        row_mask(sz, pre.shape[1], meta[sz.live]), padded[...] * silu_slope(z), 0.0
    )
    up[...] = value
    put_sums(stat_out, value, value * normed)


def conv_back_body(
    sz,
    meta,
    up,
    sums,
    pre_two,
    stat_two,
    pre_one,
    stat_one,
    params,
    weight,
    stay,
    send,
    up_one,
    stat_out,
    strip,
    taps,
    total,
):
    step = pl.program_id(0)
    n = sz.images
    width = up.shape[1]

    @pl.when(step == 0)
    def _():
        count = sz.own_count(meta)
        average, inv = moments(stat_two[...], count)
        normed = (pre_two[...] - average) * inv
        value = params[2:3] * inv * (up[...] - (sums[0:1] + normed * sums[1:2]) / count)
        value = jnp.where(row_mask(sz, width, meta[sz.live]), value, 0.0)
        half, _, lanes = stay.shape
        for p in range(2 * half):
            for plane in range(2 * half):

                @pl.when(meta[sz.planes + p] == plane)
                def _(p=p, plane=plane):
                    out = stay if p < half else send
                    out[p % half] = value[:, plane * lanes : (plane + 1) * lanes].astype(BF16)

        lay_taps(sz, value, strip, taps)
        total[...] = jnp.zeros_like(total)

    at = pl.multiple_of((2 - step) * 8 * n, 8 * n)
    for b in range(3):
        total[...] += lax.dot_general(
            taps[2 - b, pl.ds(at, sz.padded), :],
            weight[0, b],
            (((1,), (1,)), ((), ())),
            preferred_element_type=F32,
        )

    @pl.when(step == 2)
    def _():
        average, inv = moments(stat_one[...], sz.own_count(meta))
        normed = (pre_one[...] - average) * inv
        z = params[0:1] * normed + params[1:2]
        value = jnp.where(
            row_mask(sz, width, meta[sz.live]), total[...] * silu_slope(z), 0.0
        )
        up_one[...] = value
        put_sums(stat_out, value, value * normed)


def first_back_body(sz, meta, up, sums, pre, stat, params, back, padded, native):
    count = sz.own_count(meta)
    average, inv = moments(stat[...], count)
    normed = (pre[...] - average) * inv
    value = params[0:1] * inv * (up[...] - (sums[0:1] + normed * sums[1:2]) / count)
    padded[...] = jnp.where(row_mask(sz, pre.shape[1], meta[sz.live]), value, 0.0)
    to_native(sz, padded, native, back)


def input_body(sz, layout, more, meta, *refs):
    pieces, rest = split_refs(layout, refs)
    if more:
        grad, x, weight, had, out, grad_weight, place, total = rest
    else:
        grad, x, weight, out, grad_weight, place, total = rest
    step = pl.program_id(0)
    stage_piece(pieces, place, step)
    value = place[...]
    out[0] = grad[0] + lax.dot_general(
        value, weight[...], (((1,), (1,)), ((), ())), preferred_element_type=F32
    )

    @pl.when(step == 0)
    def _():
        total[...] = had[...] if more else jnp.zeros_like(total)

    total[...] += lax.dot_general(
        x[0], value, (((0,), (0,)), ((), ())), preferred_element_type=F32
    )

    @pl.when(step == len(layout) - 1)
    def _():
        grad_weight[...] = total[...].astype(grad_weight.dtype)


def middle_grad_body(sz, dp, meta, acts, backs, out, strip, taps, total):
    source = pl.program_id(0)
    n = sz.images
    lay_taps(sz, backs[0, 0].astype(F32), strip, taps)
    shifted = [
        taps[2 - b, (2 - a) * 8 * n : (2 - a) * 8 * n + sz.padded, :]
        for a in range(3)
        for b in range(3)
    ]

    @pl.when(source == 0)
    def _():
        total[...] = jnp.zeros_like(total)

    total[...] += lax.dot_general(
        acts[0],
        jnp.concatenate(shifted, axis=1),
        (((0,), (0,)), ((), ())),
        preferred_element_type=F32,
    )

    @pl.when(source == dp - 1)
    def _():
        depth, lanes = out.shape[1] // TAPS, out.shape[2]
        for k in range(sz.chunks):
            at = pl.multiple_of(meta[k] * depth, depth)
            for tap in range(TAPS):
                out[k, tap * depth : (tap + 1) * depth, :] = total[
                    pl.ds(at, depth), tap * lanes : (tap + 1) * lanes
                ].astype(BF16)


def assemble_body(sz, half, depth, meta, *refs):
    stacks, out = refs[:-1], refs[-1]
    early = sz.chunks - 3

    def fill(plane):
        for q, k in enumerate(sz.arrival):
            pieces = stacks[plane if q < early else half + plane]
            at = pl.multiple_of(meta[k] * depth, depth)
            for tap in range(TAPS):
                value = pieces[0, q if q < early else q - early, tap * depth : (tap + 1) * depth, :]
                if len(out.shape) == 3:
                    out[tap, pl.ds(at, depth), :] = value
                else:
                    out[0, tap, pl.ds(at, depth), :] = value

    for p in range(2 * half):

        @pl.when(pl.program_id(0) == p)
        def _(p=p):
            fill(p if p < half else half + p)


def prepare_body(weights, last, params, _, out):
    many, lanes = weights.shape
    out[:many, :] = weights[...].astype(BF16)
    depth = last.shape[0]
    for b in range(last.shape[1] // lanes):
        out[many + b * depth : many + (b + 1) * depth, :] = last[
            :, b * lanes : (b + 1) * lanes
        ].astype(BF16)
    value = params[...]
    count, width = value.shape
    one = value.astype(BF16)
    left = value - one.astype(F32)
    two = left.astype(BF16)
    three = (left - two.astype(F32)).astype(BF16)
    rest = jnp.zeros((16 - 3 * count, width), F32)
    rows = jnp.concatenate([part.astype(F32) for part in (one, two, three)] + [rest], axis=0)
    if width < lanes:
        rows = jnp.concatenate([rows, jnp.zeros((16, lanes - width), F32)], axis=1)
    out[out.shape[0] - 16 :, :] = rows.astype(BF16)


def last_assemble_body(meta, blocks, out):
    lanes = blocks.shape[3]
    for b in range(blocks.shape[1]):
        out[:, b * lanes : (b + 1) * lanes] = blocks[0, b]


def last_grad_body(sz, meta, act, back, out, total):
    step = pl.program_id(0)

    @pl.when(step == 0)
    def _():
        total[...] = jnp.zeros_like(total)

    total[...] += lax.dot_general(
        act[0], back[0], (((0,), (0,)), ((), ())), preferred_element_type=F32
    )

    @pl.when(step == sz.chunks - 1)
    def _():
        depth = out.shape[1]
        for k in range(sz.chunks):
            at = pl.multiple_of(meta[k] * depth, depth)
            out[k] = total[pl.ds(at, depth), :].astype(BF16)


def pieces_in(sz, pieces):
    ins, layout = [], []
    for piece in pieces:
        parts = piece if isinstance(piece, tuple) else (piece,)
        layout.append(len(parts))
        ins += [whole(p) for p in parts]
    return ins, layout


def local(
    dp,
    chan,
    inputs,
    cotangent,
    w_first,
    first_m,
    first_v,
    w_middle,
    middle_m,
    middle_v,
    w_last,
    last_m,
    last_v,
    mid_params,
    mid_m,
    mid_v,
    out_params,
    out_m,
    out_v,
    image_counts,
):
    ring = Ring(chan)
    d = lax.axis_index("dp")
    c = lax.axis_index("chan")
    micro, pixels, deep = inputs.shape
    images = micro * pixels // PIXELS // chan
    sz = Sizes(chan, micro, images)
    rows, padded = sz.rows, sz.padded
    per_batch = chan // micro
    depth, lanes = w_middle.shape[2], w_middle.shape[3]
    mid = depth * chan
    half = dp // 2
    last_blocks = w_last.shape[1] // lanes
    own_blocks = deep // lanes
    ratio = last_blocks // own_blocks


    dp_bits = bits_below(dp)
    wide_bits = dp_bits[1:]
    first = w_first.astype(BF16)
    first_stages = []
    for bit in dp_bits:
        other = swap(first, "dp", bit, dp)
        first_stages.append(other)
        first = jnp.where(
            (d & bit) == 0,
            jnp.concatenate([first, other], axis=1),
            jnp.concatenate([other, first], axis=1),
        )
    many = TAPS * depth
    tail_at = many + last_blocks * depth
    (payload,) = pl.pallas_call(
        prepare_body,
        in_specs=[pl.BlockSpec(memory_space=pltpu.VMEM)] * 3
        + [pl.BlockSpec(memory_space=pl.ANY)],
        out_specs=[pl.BlockSpec(memory_space=pltpu.VMEM)],
        out_shape=[jax.ShapeDtypeStruct((tail_at + 16, lanes), BF16)],
    )(w_middle.reshape(many, lanes), w_last, mid_params, first_stages[0])
    meta = make_meta(sz, ring, dp, ratio, image_counts, payload)
    at = meta[:chan]
    mids = Gather(ring, payload, 0)
    while mids.count < chan // 2:
        mids.step()

    x = inputs.reshape(chan, rows, deep)
    cot = cotangent.reshape(chan, rows, deep)

    def at_place(k, meta):
        return (meta[k], 0, 0)

    def in_order(k, meta):
        return (k, 0, 0)

    opposite = chan // 2

    def skipping(k, meta):
        return (jnp.where(k < opposite, k, k + 1), 0, 0)

    def skipping_at(k, meta):
        return (meta[jnp.where(k < opposite, k, k + 1)], 0, 0)

    low, high = run(
        first_lead_body,
        meta,
        (1,),
        [(x, (1, rows, deep), lambda k, meta: (meta[opposite], 0, 0)), whole(first)],
        [whole_out((rows, mid // 2), BF16), whole_out((rows, mid // 2), BF16)],
    )
    (parts,) = run(
        first_part_body,
        meta,
        (chan - 1,),
        [(x, (1, rows, deep), skipping_at), whole(first)],
        [((chan, rows, mid), BF16, (1, rows, mid), skipping)],
        cost=(2 * chan * rows * deep * mid, 2 * chan * rows * (deep + mid)),
    )
    sums = Scatter(ring, low, high, lambda k: parts[k], 1)
    while sums.count < opposite:
        sums.step()
    f, b = sums.f, sums.b

    came = [jnp.concatenate(p, axis=0) if isinstance(p, tuple) else p for p in mids.pieces]
    tails = jnp.stack([p[many:] for p in came])
    near, far = [], []
    for group in (sz.arrival[: chan - 3], sz.arrival[chan - 3 :]):
        stack = jnp.stack([came[k][:many] for k in group])[None]
        planes = [stack]
        for bit in wide_bits:
            planes += [swap(p, "dp", bit, dp) for p in planes]
        near.append(planes)
        far.append([swap(p, "dp", 1, dp) for p in planes])
    near = [near[g][q] for g in range(2) for q in range(half)]
    far = [far[g][q] for g in range(2) for q in range(half)]
    if lanes % 128 == 0:
        placed = ((TAPS, mid, mid), BF16, (TAPS, mid, lanes), lambda p, meta: (0, 0, meta[sz.planes + p]))
    else:
        placed = (
            (dp, TAPS, mid, lanes),
            BF16,
            (1, TAPS, mid, lanes),
            lambda p, meta: (meta[sz.planes + p], 0, 0, 0),
        )
    (middle,) = run(
        functools.partial(assemble_body, sz, half, depth),
        meta,
        (dp,),
        [whole(p) for p in near + far],
        [placed],
    )
    here = (at[None, :] == jnp.arange(chan)[:, None])[:, :, None, None]
    tail = tails[:, last_blocks * depth :, :depth].astype(F32)
    tail = (tail[:, 8:12] + tail[:, 4:8]) + tail[:, 0:4]
    params = jnp.sum(jnp.where(here, tail[None], 0.0), axis=1)
    params = params.transpose(1, 0, 2).reshape(4, mid)
    if lanes % 128 != 0:
        middle = middle.transpose(1, 2, 0, 3)
    middle = middle.reshape(3, 3, mid, mid)
    lasts = tails[:, : last_blocks * depth].reshape(chan, ratio, own_blocks, depth, lanes)
    own_last = lax.dynamic_index_in_dim(lasts, c % ratio, axis=1, keepdims=False)
    found = jnp.where(d == c // ratio, own_last, jnp.zeros_like(own_last))
    for shift in range(1, dp):
        moves = [
            ((k // ratio) * chan + k, ((k // ratio) ^ shift) * chan + k) for k in range(chan)
        ]
        found = found + lax.ppermute(own_last, ("dp", "chan"), moves)
    (last,) = run(
        last_assemble_body,
        meta,
        (chan,),
        [(found, (1, own_blocks, depth, lanes), lambda k, meta: (k, 0, 0, 0))],
        [((mid, deep), BF16, (depth, deep), lambda k, meta: (meta[k], 0))],
    )

    def head(stack):
        return (stack, (1,) + stack.shape[1:], lambda *_: (0, 0, 0))

    stat_bits = [k for k in bits_below(chan) if k < per_batch]

    def total_rows(stat):
        return sum_over(sum_over(stat, "dp", dp_bits, dp), "chan", stat_bits, chan)

    def all_batches(stat):
        for bit in bits_below(chan):
            if bit >= per_batch:
                other = swap(stat, "chan", bit, chan)
                stat = jnp.where(
                    (c & bit) == 0,
                    jnp.concatenate([stat, other], axis=0),
                    jnp.concatenate([other, stat], axis=0),
                )
        return stat

    pre_one, stat_one = run(
        functools.partial(first_body, sz),
        meta,
        (1,),
        [whole(f), whole(b), head(parts)],
        [whole_out((padded, mid), F32), whole_out((2, mid), F32)],
        [pltpu.VMEM((mid // 128, rows, 128), F32)],
        vmem=VMEM,
        cost=(10 * padded * mid, 10 * padded * mid),
    )
    stat_one = total_rows(stat_one)

    tap_block = (1, 3, mid, mid)
    conv_flops = 2 * TAPS * padded * mid * mid
    conv_bytes = 2 * TAPS * mid * mid + 16 * padded * mid
    pre_two, raw, stat_two, acted = run(
        functools.partial(conv_body, sz),
        meta,
        (3,),
        [
            whole(pre_one),
            whole(stat_one),
            whole(params),
            (middle, tap_block, lambda s, meta: (s, 0, 0, 0)),
        ],
        [
            whole_out((padded, mid), F32),
            whole_out((rows, mid), BF16),
            whole_out((2, mid), F32),
            whole_out((padded, mid), BF16),
        ],
        [
            pltpu.VMEM((74 * images, mid), F32),
            pltpu.VMEM((3, 72 * images, mid), BF16),
            pltpu.VMEM((padded, mid), F32),
            pltpu.VMEM((mid // 128, rows, 128), F32),
        ],
        vmem=VMEM,
        cost=(conv_flops, conv_bytes),
    )
    gather = Gather(ring, raw, 1)
    gather.step()
    stat_two = sum_over(stat_two, "chan", stat_bits[:1], chan)
    gather.step(stat_two)
    stat_two = sum_over(stat_two, "dp", dp_bits, dp)
    if gather.count < opposite - 1:
        gather.step(stat_two)
    stat_two = sum_over(stat_two, "chan", stat_bits[1:], chan)
    stats_two = all_batches(stat_two)
    while gather.count < opposite - 1:
        gather.step()
    gather.step(stats_two)
    pieces = gather.pieces
    order = [1] + wide_bits[::-1]
    acts = acted[None]
    for bit in order:
        acts = jnp.concatenate([acts, swap(acts, "dp", bit, dp)], axis=0)

    def expand(start, steps, into):
        ins, layout = pieces_in(sz, [pieces[k] for k in sz.arrival[start : start + steps]])

        def arrived(k, meta):
            return (meta[sz.arrive + start + k], 0, 0)

        return run(
            functools.partial(expand_body, sz, layout, start),
            meta,
            (steps,),
            ins + [whole(stats_two), whole(params), whole(last)],
            [
                ((chan, rows, mid), BF16, (1, rows, mid), arrived),
                ((chan, rows, deep), F32, (1, rows, deep), arrived),
                whole_out((2 * micro, deep), F32),
            ],
            [pltpu.VMEM((rows, mid), BF16)],
            vmem=VMEM,
            cost=(2 * steps * rows * deep * mid, steps * rows * (4 * mid + 4 * deep)),
            into=into,
        )

    early = chan - 3
    act, pre_three, stat_early = expand(0, chan - 1, [])
    act, pre_three, stat_late = expand(chan - 1, 1, [act, pre_three])
    stat_three = stat_early + stat_late
    stat_three = sum_over(stat_three, "dp", bits_below(dp), dp)
    block_out, grad_summed, sums_three = run(
        functools.partial(out_body, sz),
        meta,
        (chan,),
        [
            (pre_three, (1, rows, deep), in_order),
            whole(stat_three),
            whole(out_params),
            (x, (1, rows, deep), at_place),
            (cot, (1, rows, deep), at_place),
        ],
        [
            ((chan, rows, deep), F32, (1, rows, deep), at_place),
            ((chan, rows, deep), F32, (1, rows, deep), in_order),
            whole_out((2 * micro, deep), F32),
        ],
        vmem=VMEM,
        cost=(20 * chan * rows * deep, 16 * chan * rows * deep),
    )
    sums_three = sum_over(sums_three, "dp", bits_below(dp), dp)

    def shrink(steps, place, into, lead):
        if lead:
            made = [whole_out((rows, mid // 2), BF16), whole_out((rows, mid // 2), BF16)]
        else:
            made = [((chan, rows, mid), BF16, (1, rows, mid), place)]
        return run(
            functools.partial(shrink_body, sz, lead),
            meta,
            (steps,),
            [
                (pre_three, (1, rows, deep), place),
                whole(stat_three),
                whole(out_params),
                (grad_summed, (1, rows, deep), place),
                whole(sums_three),
                whole(last),
            ],
            [((chan, rows, deep), BF16, (1, rows, deep), place)] + made,
            vmem=VMEM,
            cost=(2 * steps * rows * deep * mid, steps * rows * (2 * mid + 10 * deep)),
            into=into,
        )

    back_last, low, high = shrink(1, lambda k, meta: (opposite, 0, 0), [], True)
    back_last, back_parts = shrink(chan - 1, skipping, [back_last], False)
    sums = Scatter(ring, low, high, lambda k: back_parts[k], 1)
    while sums.count < opposite:
        sums.step()
    f, b = sums.f, sums.b
    (grad_last,) = run(
        functools.partial(last_grad_body, sz),
        meta,
        (chan,),
        [(act, (1, rows, mid), in_order), (back_last, (1, rows, deep), in_order)],
        [whole_out((chan, depth, deep), BF16)],
        [pltpu.VMEM((mid, deep), F32)],
        cost=(2 * chan * rows * deep * mid, 2 * chan * rows * (mid + deep)),
    )
    for bit in dp_bits:
        grad_last = add16(grad_last, swap(grad_last, "dp", bit, dp))
    held = [
        jnp.where(c % ratio == r, grad_last, jnp.zeros_like(grad_last)) for r in range(ratio)
    ]
    held = jnp.concatenate(held, axis=2)
    held = jnp.where(d == c // ratio, held, jnp.zeros_like(held))
    cut = held.shape[2] // 2
    last_sums = Scatter(
        ring, held[opposite, :, :cut], held[opposite, :, cut:], lambda k: held[k], 1
    )
    while last_sums.count < opposite:
        last_sums.step()
    owned_last = held[0].astype(F32) + last_sums.f.astype(F32) + last_sums.b.astype(F32)

    up_two, sums_two = run(
        functools.partial(middle_up_body, sz),
        meta,
        (1,),
        [
            whole(f),
            whole(b),
            head(back_parts),
            whole(pre_two),
            whole(stat_two),
            whole(params),
        ],
        [whole_out((padded, mid), F32), whole_out((2, mid), F32)],
        [pltpu.VMEM((mid // 128, rows, 128), F32), pltpu.VMEM((padded, mid), F32)],
        vmem=VMEM,
        cost=(20 * padded * mid, 14 * padded * mid),
    )
    sums_two = total_rows(sums_two)
    stay, send, up_one, sums_one = run(
        functools.partial(conv_back_body, sz),
        meta,
        (3,),
        [
            whole(up_two),
            whole(sums_two),
            whole(pre_two),
            whole(stat_two),
            whole(pre_one),
            whole(stat_one),
            whole(params),
            (middle, tap_block, lambda s, meta: (s, 0, 0, 0)),
        ],
        [
            whole_out((half, padded, lanes), BF16),
            whole_out((half, padded, lanes), BF16),
            whole_out((padded, mid), F32),
            whole_out((2, mid), F32),
        ],
        [
            pltpu.VMEM((74 * images, mid), F32),
            pltpu.VMEM((3, 72 * images, mid), BF16),
            pltpu.VMEM((padded, mid), F32),
        ],
        vmem=VMEM,
        cost=(conv_flops, conv_bytes),
    )

    sums_one = total_rows(sums_one)
    (back_one,) = run(
        functools.partial(first_back_body, sz),
        meta,
        (1,),
        [whole(up_one), whole(sums_one), whole(pre_one), whole(stat_one), whole(params)],
        [whole_out((rows, mid), BF16)],
        [pltpu.VMEM((padded, mid), F32), pltpu.VMEM((mid // 128, rows, 128), F32)],
        cost=(10 * padded * mid, 10 * padded * mid),
    )
    gather = Gather(ring, back_one, 1)
    while gather.count < opposite:
        gather.step()
    pieces = gather.pieces

    backs = jnp.stack([stay, swap(send, "dp", 1, dp)])
    for bit in wide_bits[::-1]:
        cut = backs.shape[1] // 2
        backs = jnp.concatenate(
            [backs[:, :cut], swap(backs[:, cut:], "dp", bit, dp)], axis=0
        )
    (grad_middle,) = run(
        functools.partial(middle_grad_body, sz, dp),
        meta,
        (dp,),
        [
            (acts, (1, padded, mid), lambda r, meta: (r, 0, 0)),
            (backs, (1, 1, padded, lanes), lambda r, meta: (r, 0, 0, 0)),
        ],
        [whole_out((chan, TAPS * depth, lanes), BF16)],
        [
            pltpu.VMEM((74 * images, lanes), F32),
            pltpu.VMEM((3, 72 * images, lanes), BF16),
            pltpu.VMEM((mid, TAPS * lanes), F32),
        ],
        cost=(conv_flops, conv_bytes),
        after=[back_one],
    )
    cut = TAPS * depth // 2
    middle_sums = Scatter(
        ring,
        grad_middle[opposite, :cut],
        grad_middle[opposite, cut:],
        lambda k: grad_middle[k],
        0,
    )
    middle_steps = [middle_sums.f]
    while middle_sums.count < opposite:
        middle_sums.step()
        middle_steps.append(middle_sums.f)
    owned_middle = (
        grad_middle[0].astype(F32) + middle_sums.f.astype(F32) + middle_sums.b.astype(F32)
    ).reshape(3, 3, depth, lanes)

    def input_back(start, steps, had, into, after):
        ins, layout = pieces_in(sz, [pieces[k] for k in sz.arrival[start : start + steps]])
        done = start + steps == chan

        def arrived(k, meta):
            return (meta[sz.arrive + start + k], 0, 0)

        def arrived_at(k, meta):
            return (meta[meta[sz.arrive + start + k]], 0, 0)

        return run(
            functools.partial(input_body, sz, layout, bool(had)),
            meta,
            (steps,),
            ins
            + [
                (grad_summed, (1, rows, deep), arrived),
                (x, (1, rows, deep), arrived_at),
                whole(first),
            ]
            + [whole(h) for h in had],
            [
                ((chan, rows, deep), F32, (1, rows, deep), arrived_at),
                whole_out((deep, mid), BF16 if done else F32),
            ],
            [pltpu.VMEM((rows, mid), BF16), pltpu.VMEM((deep, mid), F32)],
            vmem=VMEM,
            cost=(4 * steps * rows * deep * mid, steps * rows * (2 * mid + 10 * deep)),
            into=into,
            after=after,
        )

    input_grad, grad_early = input_back(0, early, [], [], middle_steps[1:2])
    input_grad, grad_first = input_back(early, 3, [grad_early], [input_grad], middle_steps[2:3])
    owned_first = scatter_columns(grad_first, d, dp)

    sums_first, sums_middle = all_batches(sums_one), all_batches(sums_two)

    def over_batches(stat, row):
        total = stat[row]
        for m in range(1, micro):
            total = total + stat[2 * m + row]
        return total

    grad_mid = jnp.stack(
        [
            over_batches(sums_first, 1),
            over_batches(sums_first, 0),
            over_batches(sums_middle, 1),
            over_batches(sums_middle, 0),
        ]
    )
    grad_mid = lax.dynamic_slice_in_dim(grad_mid, c * depth, depth, axis=1)
    grad_out = jnp.stack([over_batches(sums_three, 1), over_batches(sums_three, 0)])

    return (
        block_out.reshape(inputs.shape),
        input_grad.reshape(inputs.shape),
        *adamw(w_first, owned_first, first_m, first_v, rate_first),
        *adamw(w_middle, owned_middle, middle_m, middle_v, rate_middle),
        *adamw(w_last, owned_last, last_m, last_v, rate_last),
        *adamw(mid_params, grad_mid, mid_m, mid_v, rate_norm),
        *adamw(out_params, grad_out, out_m, out_v, rate_norm),
    )


def scatter_columns(grad, d, dp):
    blocks = grad.reshape(grad.shape[0], dp, grad.shape[1] // dp)
    kept = [blocks[:, p] for p in range(dp)]
    for bit in bits_below(dp):
        kept = [
            jnp.where((d & bit) == 0, kept[q], kept[q ^ bit]) for q in range(len(kept))
        ]
    todo = {q: kept[q] for q in range(dp)}
    for bit in [1] + bits_below(dp)[:0:-1]:
        send = sorted(q for q in todo if q & bit)
        stay = sorted(q for q in todo if not q & bit)
        got = swap(jnp.stack([todo[q] for q in send]), "dp", bit, dp)
        todo = {
            q: todo[q].astype(F32) + got[send.index(q | bit)].astype(F32) for q in stay
        }
        if len(todo) > 1:
            todo = {q: v.astype(BF16) for q, v in todo.items()}
    return todo[0]


def solution(mesh):
    rows = P(None, "dp", "chan")
    flat = P("chan", "dp")
    square = P(None, None, "chan", "dp")
    vector = P(None, "chan")
    state = (flat,) * 3 + (square,) * 3 + (flat,) * 3 + (vector,) * 6
    return jax.shard_map(
        functools.partial(local, mesh.shape["dp"], mesh.shape["chan"]),
        mesh=mesh,
        in_specs=(rows, rows) + state + (P(),),
        out_specs=(rows, rows) + state,
        check_vma=False,
    )
```
